256 devices in a mesh: gx: 4 (over y), gy: 8 (over x, core), gz: 8 (over z).
Axes of the slice: x: 4, y: 4, z: 8, core: 2. Of those that a mesh axis runs over, the one named last changes fastest.
Arguments:
- populations: float32 [19, 128, 128, 512], P(None, 'gz', 'gy', 'gx'), may hold values from 0.25 to 21, as said below
- solute_state: float32 [7, 2048, 4096], P(None, ('gx', 'gy', 'gz')), may hold values from 0.05 to 3.9, as said below
- pore_mask: int32 [128, 128, 512], P('gz', 'gy', 'gx'), may hold values from 0 to 1, as said below
- block_slot: int32 [8, 8, 32], P('gz', 'gy', 'gx'), may hold values from -1 to 63, as said below
- slot_block: int32 [2048], P(('gx', 'gy', 'gz')), may hold values from -1 to 63, as said below
Outputs:
- new_populations: float32 [19, 128, 128, 512], P(None, 'gz', 'gy', 'gx')
- new_solute: float32 [7, 2048, 4096], P(None, ('gx', 'gy', 'gz'))
The draws below stay inside these ranges and needn't reach their ends.
Inputs may be any that keep to these rules, and one draw needn't show every extreme that they name: pore_mask is 1 only inside blocks listed in block_slot. `block_slot`: in each column of fixed gx and gy, the listed blocks are numbered k = 0, 1, ... in order of the gz index and then of the x block within the device; block k sits in owner k % 8 (index along gz within the same column), slot k // 8. Every device lists 1 to 8 blocks and in every column some device lists all 8, so one device hands 1 block to some owner. `slot_block`: the inverse of block_slot: an owner's filled slots come first, in increasing k. `populations`: Positive. `solute_state`: Positive.
All inputs are finite; a program needn't handle non-finite values.
Results may differ from the reference program's by a relative error of at most 0.0001.
Values sent between devices are 32-bit elements; how exact they have to be, the bound alone decides.
No kernel may reach another device: no remote copies, remote signals or barrier semaphores. Data moves between devices by JAX's collectives and lax.ppermute only.
A program may use at most 192 MiB of HBM per device.

```python
import jax
import jax.numpy as jnp

BLOCK = 16
STEPS = 4
NBD = 8
OWN = 8
CELLS = 4096
NX = 512
NY = 128
NZ = 128
SLOTS = 2048
N_GX = 4
N_GY = 8
N_GZ = 8


FLOW_WEIGHTS = [1.0 / 3.0] + [1.0 / 18.0] * 6 + [1.0 / 36.0] * 12


SOLUTE_WEIGHTS = [0.25] + [0.125] * 6


def layout(key):
    count_key, pick_key, full_key, voxel_key = jax.random.split(key, 4)
    counts = jax.random.randint(count_key, (N_GX, N_GY, N_GZ), 1, NBD + 1)
    fullest = jax.random.randint(full_key, (N_GX, N_GY), 0, N_GZ)
    counts = jnp.where(jnp.arange(N_GZ)[None, None, :] == fullest[:, :, None], NBD, counts)
    scores = jax.random.randint(pick_key, (N_GX, N_GY, N_GZ, NBD), 0, 1 << 20) * NBD + jnp.arange(NBD)[None, None, None, :]
    ranks = jnp.argsort(jnp.argsort(scores, axis=-1, stable=True), axis=-1, stable=True)
    flags = (ranks < counts[..., None]).astype(jnp.int32)
    flat_flags = flags.reshape(N_GX, N_GY, N_GZ * NBD)
    number = jnp.cumsum(flat_flags, axis=-1) - flat_flags
    owner_gz = number % N_GZ
    within = number // N_GZ
    slot_value = jnp.where(flat_flags > 0, owner_gz * OWN + within, -1)
    block_slot = slot_value.reshape(N_GX, N_GY, N_GZ, NBD).transpose(2, 1, 0, 3).reshape(N_GZ, N_GY, N_GX * NBD)
    position = jnp.broadcast_to(jnp.arange(N_GZ * NBD)[None, None, :], (N_GX, N_GY, N_GZ * NBD))
    target = jnp.where(flat_flags > 0, slot_value, N_GZ * OWN)
    column_x = jnp.broadcast_to(jnp.arange(N_GX)[:, None, None], target.shape)
    column_y = jnp.broadcast_to(jnp.arange(N_GY)[None, :, None], target.shape)
    slot_block = jnp.full((N_GX, N_GY, N_GZ * OWN), -1, jnp.int32)
    slot_block = slot_block.at[column_x, column_y, target].set(position.astype(jnp.int32), mode='drop')
    slot_block = slot_block.reshape(N_GX * N_GY * N_GZ * OWN)
    block_open = (block_slot >= 0).astype(jnp.int32)
    block_open = jnp.repeat(jnp.repeat(jnp.repeat(block_open, BLOCK, axis=0), BLOCK, axis=1), BLOCK, axis=2)
    voxels = (jax.random.randint(voxel_key, (NZ, NY, NX), 0, 100) < 27).astype(jnp.int32)
    return (block_open * voxels, block_slot.astype(jnp.int32), slot_block)


def draw_pore_mask(key, part):
    return layout(key)[0]


def draw_block_slot(key, part):
    return layout(key)[1]


def draw_slot_block(key, part):
    return layout(key)[2]


def draw_populations(key, part):
    key = jax.random.fold_in(key, 11)
    weights = jnp.array(FLOW_WEIGHTS, jnp.float32)[:, None, None, None]
    factor = jax.random.uniform(key, (19, NZ, NY, NX), jnp.float32, 0.5, 1.5)
    return weights * 36.0 * factor


def draw_solute_state(key, part):
    key = jax.random.fold_in(key, 23)
    weights = jnp.array(SOLUTE_WEIGHTS, jnp.float32)[:, None, None]
    factor = jax.random.uniform(key, (7, SLOTS, CELLS), jnp.float32, 0.2, 1.8)
    return weights * 8.0 * factor


def setup_inputs(seed: int = 0) -> dict:
    splits = jax.random.split(jax.random.key(seed), 6)
    populations = draw_populations(jax.random.fold_in(splits[5], 71), 0)
    solute_state = draw_solute_state(jax.random.fold_in(splits[5], 71), 0)
    pore_mask = draw_pore_mask(jax.random.fold_in(splits[5], 71), 0)
    block_slot = draw_block_slot(jax.random.fold_in(splits[5], 71), 0)
    slot_block = draw_slot_block(jax.random.fold_in(splits[5], 71), 0)
    return {"populations": populations, "solute_state": solute_state, "pore_mask": pore_mask, "block_slot": block_slot, "slot_block": slot_block}


FLOW_DIRS = [(0, 0, 0), (1, 0, 0), (-1, 0, 0), (0, 1, 0), (0, -1, 0), (0, 0, 1), (0, 0, -1),
             (1, 1, 0), (-1, -1, 0), (1, -1, 0), (-1, 1, 0), (1, 0, 1), (-1, 0, -1), (1, 0, -1),
             (-1, 0, 1), (0, 1, 1), (0, -1, -1), (0, 1, -1), (0, -1, 1)]
FLOW_WEIGHTS = [1.0 / 3.0] + [1.0 / 18.0] * 6 + [1.0 / 36.0] * 12
SOLUTE_DIRS = FLOW_DIRS[:7]
SOLUTE_WEIGHTS = [0.25] + [0.125] * 6
OMEGA_FLOW = 1.2
OMEGA_SOLUTE = 1.5
FORCE_GAIN = 0.02
REST_CONC = 8.0


def opposite(directions):
    return [directions.index((-a, -b, -c)) for (a, b, c) in directions]


def moments(populations, porous):
    density = jnp.sum(populations, axis=0)
    parts = []
    for coord in range(3):
        summed = jnp.zeros_like(density)
        for which, vector in enumerate(FLOW_DIRS):
            if vector[coord] != 0:
                summed = summed + vector[coord] * populations[which]
        parts.append(porous * summed / density)
    return density, jnp.stack(parts)


def solute_collide(solute, velocity):
    concentration = jnp.sum(solute, axis=0)
    results = []
    for which, vector in enumerate(SOLUTE_DIRS):
        along = vector[0] * velocity[0] + vector[1] * velocity[1] + vector[2] * velocity[2]
        balance = SOLUTE_WEIGHTS[which] * concentration * (1.0 + 4.0 * along)
        results.append(solute[which] + OMEGA_SOLUTE * (balance - solute[which]))
    return jnp.stack(results)


def flow_collide(populations, density, velocity, concentration, porous):
    uplift = porous * FORCE_GAIN * (concentration - REST_CONC)
    shift_x, shift_y, shift_z = velocity[0], velocity[1], velocity[2] + uplift
    square = shift_x * shift_x + shift_y * shift_y + shift_z * shift_z
    results = []
    for which, vector in enumerate(FLOW_DIRS):
        along = vector[0] * shift_x + vector[1] * shift_y + vector[2] * shift_z
        balance = FLOW_WEIGHTS[which] * density * (1.0 + 3.0 * along + 4.5 * along * along - 1.5 * square)
        relaxed = populations[which] + OMEGA_FLOW * (balance - populations[which])
        results.append(jnp.where(porous > 0, relaxed, populations[which]))
    return jnp.stack(results)


def stream(post, padded, porous, padded_pore, directions):
    reverse = opposite(directions)
    size_z, size_y, size_x = porous.shape
    results = []
    for which, (step_x, step_y, step_z) in enumerate(directions):
        source = padded[which, 1 - step_z:1 - step_z + size_z, 1 - step_y:1 - step_y + size_y,
                        1 - step_x:1 - step_x + size_x]
        source_open = padded_pore[1 - step_z:1 - step_z + size_z, 1 - step_y:1 - step_y + size_y,
                                  1 - step_x:1 - step_x + size_x]
        moved = jnp.where(source_open > 0, source, post[reverse[which]])
        results.append(jnp.where(porous > 0, moved, post[which]))
    return jnp.stack(results)


def reference(populations, solute_state, pore_mask, block_slot, slot_block):
    porous = pore_mask.astype(jnp.float32)
    blocks_z, blocks_y, blocks_x = block_slot.shape
    listed = block_slot >= 0
    owner_gz = block_slot // OWN
    within = block_slot % OWN
    column_x = (jnp.arange(blocks_x, dtype=jnp.int32) // NBD)[None, None, :]
    column_y = jnp.arange(blocks_y, dtype=jnp.int32)[None, :, None]
    global_slot = ((column_x * N_GY + column_y) * N_GZ + owner_gz) * OWN + within
    slot_index = jnp.where(listed, global_slot, 0).reshape(-1).astype(jnp.int32)
    tile_data = solute_state[:, slot_index, :] * listed.reshape(1, -1, 1).astype(jnp.float32)
    tile_data = tile_data.reshape(7, blocks_z, blocks_y, blocks_x, BLOCK, BLOCK, BLOCK)
    solute_dense = tile_data.transpose(0, 1, 4, 2, 5, 3, 6).reshape(
        7, blocks_z * BLOCK, blocks_y * BLOCK, blocks_x * BLOCK)
    padded_pore = jnp.pad(porous, 1)
    wide = ((0, 0), (1, 1), (1, 1), (1, 1))
    for repeat in range(STEPS):
        density, velocity = moments(populations, porous)
        post_solute = solute_collide(solute_dense, velocity)
        solute_dense = stream(post_solute, jnp.pad(post_solute, wide), porous, padded_pore, SOLUTE_DIRS)
        concentration = jnp.sum(solute_dense, axis=0)
        post_flow = flow_collide(populations, density, velocity, concentration, porous)
        populations = stream(post_flow, jnp.pad(post_flow, wide), porous, padded_pore, FLOW_DIRS)
    back_tiles = solute_dense.reshape(7, blocks_z, BLOCK, blocks_y, BLOCK, blocks_x, BLOCK)
    back_tiles = back_tiles.transpose(0, 1, 3, 5, 2, 4, 6).reshape(7, blocks_z * blocks_y * blocks_x, CELLS)
    slot_count = solute_state.shape[1]
    slot_ids = jnp.arange(slot_count, dtype=jnp.int32)
    column = slot_ids // (N_GZ * OWN)
    slot_cx = column // N_GY
    slot_cy = column % N_GY
    held = slot_block >= 0
    safe_block = jnp.where(held, slot_block, 0).astype(jnp.int32)
    block_z = safe_block // NBD
    block_x = slot_cx * NBD + safe_block % NBD
    flat_index = ((block_z * blocks_y + slot_cy) * blocks_x + block_x).astype(jnp.int32)
    picked = back_tiles[:, flat_index, :]
    new_solute = jnp.where(held[None, :, None], picked, jnp.float32(0.0))
    return populations, new_solute
```

```python
import functools

import jax
import jax.numpy as jnp
from jax import lax
from jax.experimental import pallas as pl
from jax.experimental.pallas import tpu as pltpu
from jax.sharding import PartitionSpec as P

STEPS = 4
DIRS = [
    (0, 0, 0),
    (1, 0, 0),
    (-1, 0, 0),
    (0, 1, 0),
    (0, -1, 0),
    (0, 0, 1),
    (0, 0, -1),
    (1, 1, 0),
    (-1, -1, 0),
    (1, -1, 0),
    (-1, 1, 0),
    (1, 0, 1),
    (-1, 0, -1),
    (1, 0, -1),
    (-1, 0, 1),
    (0, 1, 1),
    (0, -1, -1),
    (0, 1, -1),
    (0, -1, 1),
]
OPP = [DIRS.index((-a, -b, -c)) for a, b, c in DIRS]
PAIRS = [(i, OPP[i]) for i in range(1, 19, 2)]
WEIGHTS = [1.0 / 3.0] + [1.0 / 18.0] * 6 + [1.0 / 36.0] * 12
OMEGA_FLOW = 1.2
FORCE_GAIN = 0.02
REST_CONC = 8.0
Y_UP = [i for i in range(19) if DIRS[i][1] == 1]
Y_DN = [i for i in range(19) if DIRS[i][1] == -1]
Z_UP = [i for i in range(19) if DIRS[i][2] == 1]
Z_DN = [i for i in range(19) if DIRS[i][2] == -1]
RHO, VEL, PART, NORM, TRANS, FIELDS = 5, 6, 9, 10, 11, 12
SLABS = FIELDS + 2
B = 16
L = 128
W = 8
PLANE = 2 * B
ROWS = B * PLANE
PADDED = 64
PADROWS = (B + 2) * PADDED
BLOCKROWS = 7 * 32 * 8
F32 = jnp.float32
VMEM = pl.BlockSpec(memory_space=pltpu.VMEM)
SMEM = pl.BlockSpec(memory_space=pltpu.SMEM)


def call(kernel, out_shape, in_specs, scratch, flops, nbytes, limit=48):
    return pl.pallas_call(
        kernel,
        out_shape=out_shape,
        in_specs=in_specs,
        out_specs=jax.tree.map(lambda _: VMEM, out_shape),
        scratch_shapes=scratch,
        compiler_params=pltpu.CompilerParams(vmem_limit_bytes=limit * 1024 * 1024),
        cost_estimate=pl.CostEstimate(flops=flops, bytes_accessed=nbytes, transcendentals=0),
    )


def shape(*dims):
    return jax.ShapeDtypeStruct(dims, F32)


def lanes(rows):
    return lax.broadcasted_iota(jnp.int32, (rows, L), 1)


def row_ids(rows):
    return lax.broadcasted_iota(jnp.int32, (rows, L), 0)


def ring(v, step):
    rolled = pltpu.roll(v, step % L, axis=1)
    other = jnp.concatenate([rolled[B:], rolled[:B]], axis=0)
    return jnp.where(lanes(PLANE) == (0 if step > 0 else L - 1), other, rolled)


def halves(main, side):
    return jnp.concatenate([main, side], axis=0)


def spread(main, side):
    return halves(jnp.broadcast_to(main, (B, L)), jnp.broadcast_to(side, (B, L)))


def shift_rows(v, step, fill):
    rolled = pltpu.roll(v, step % PLANE, axis=0)
    return jnp.where(row_ids(PLANE) % B == (0 if step > 0 else B - 1), fill, rolled)


def is_open(bits, which):
    return (bits & (1 << which)) != 0


def along(which, vx, vy, vz):
    total = None
    for sign, part in zip(DIRS[which], (vx, vy, vz)):
        if sign != 0:
            if total is None:
                total = part if sign > 0 else -part
            else:
                total = total + part if sign > 0 else total - part
    return total


def moments(pops, porous):
    rho = pops[0]
    for which in range(1, 19):
        rho = rho + pops[which]
    scale = porous / rho
    parts = []
    for coord in range(3):
        plus = sum(pops[i] for i in range(19) if DIRS[i][coord] == 1)
        minus = sum(pops[i] for i in range(19) if DIRS[i][coord] == -1)
        parts.append((plus - minus) * scale)
    return rho, parts


def solute_collide(solute, velocity):
    conc = sum(solute)
    out = [-0.5 * solute[0] + 0.375 * conc]
    base = 0.1875 * conc
    for coord in range(3):
        turn = 0.75 * conc * velocity[coord]
        out.append((base - 0.5 * solute[1 + 2 * coord]) + turn)
        out.append((base - 0.5 * solute[2 + 2 * coord]) - turn)
    return out


def chosen(bits, moved, post, which):
    return jnp.where(
        is_open(bits, which),
        moved,
        jnp.where(is_open(bits, 0), post[OPP[which]], post[which]),
    )


def turn_blocks(x):
    row = row_ids(8)
    group = lanes(8) // B
    for bit in (1, 2, 4):
        up = pltpu.roll(pltpu.roll(x, 8 - bit, axis=0), B * bit, axis=1)
        down = up
        if bit != 4:
            down = pltpu.roll(pltpu.roll(x, bit, axis=0), L - B * bit, axis=1)
        low = (row & bit) == 0
        same = low == ((group & bit) == 0)
        x = jnp.where(same, x, jnp.where(low, up, down))
    return x


def gather_kernel(slot_ref, state_ref, send_ref):
    for dest in range(8):
        slot = jnp.int32(0)
        for s in range(8):
            home = slot_ref[s]
            slot = jnp.where((home >= 0) & (home // 8 == dest), s, slot)
        send_ref[dest] = state_ref[pl.ds(slot, BLOCKROWS // 8, stride=8), :]


def spread_kernel(slot_ref, recv_ref, dense_ref, low_ref, high_ref, turn_ref):
    for tile in range(8):
        owner = jnp.maximum(slot_ref[0, 0, tile], 0) // 8
        turn_ref[pl.ds(tile, BLOCKROWS // 8, stride=8), :] = recv_ref[owner]

    def body(group, carry):
        pack_columns(
            group,
            lambda at: turn_blocks(turn_ref[pl.ds(at, 8), :]),
            dense_ref,
            low_ref,
            high_ref,
        )
        return carry

    lax.fori_loop(0, BLOCKROWS // 128, body, 0)


def pack_columns(group, load, dense_ref, low_ref, high_ref):
    lane = lanes(8) // W
    low = jnp.zeros((8, L), F32)
    high = jnp.zeros((8, L), F32)
    for i in range(16):
        at = pl.multiple_of(group * 128 + i * 8, 8)
        x = load(at)
        if dense_ref is not None:
            dense_ref[pl.ds(at, 8), :] = x
        low = jnp.where(lane == i, x if i == 0 else pltpu.roll(x, W * i, axis=1), low)
        turn = (W + W * i) % L
        high = jnp.where(lane == i, x if turn == 0 else pltpu.roll(x, turn, axis=1), high)
    at = pl.multiple_of(group * 8, 8)
    low_ref[pl.ds(at, 8), :] = low
    high_ref[pl.ds(at, 8), :] = high


def unpack_columns(right, left, i):
    a = right if i == 0 else pltpu.roll(right, L - W * i, axis=1)
    b = left if i == 15 else pltpu.roll(left, L - W - W * i, axis=1)
    return jnp.where(lanes(8) < L // 2, a, b)


def columns_kernel(pops_ref, low_ref, high_ref):
    def body(group, carry):
        pack_columns(group, lambda at: pops_ref[pl.ds(at, 8), :], None, low_ref, high_ref)
        return carry

    lax.fori_loop(0, 19 * 2, body, 0)


def fill_ring(main_ref, right_ref, left_ref, out_ref, count):
    def body(group, carry):
        at = pl.multiple_of(group * 8, 8)
        right = right_ref[pl.ds(at, 8), :]
        left = left_ref[pl.ds(at, 8), :]
        comp = group // 2
        for i in range(16):
            z = (group % 2) * 8 + i // 2
            row = z * PLANE + (i % 2) * 8
            src = pl.multiple_of(group * 128 + i * 8, 8)
            out_ref[comp, pl.ds(pl.multiple_of(row, 8), 8), :] = main_ref[pl.ds(src, 8), :]
            out_ref[comp, pl.ds(pl.multiple_of(row + B, 8), 8), :] = unpack_columns(right, left, i)
        return carry

    lax.fori_loop(0, count * 2, body, 0)


def plane(ref, z, *lead):
    return ref[(*lead, pl.ds(pl.multiple_of(z * PLANE, PLANE), PLANE), slice(None))]


def padded_plane(ref, zz, shift, *lead):
    at = zz * PADDED + 8
    return halves(
        ref[(*lead, pl.ds(at - shift, B), slice(None))],
        ref[(*lead, pl.ds(at + 32 - shift, B), slice(None))],
    )


def put_padded(ref, comp, zz, v):
    at = zz * PADDED + 8
    if not isinstance(zz, int):
        at = pl.multiple_of(at, 8)
    ref[comp, pl.ds(at, B), :] = v[:B]
    ref[comp, pl.ds(at + 32, B), :] = v[B:]


def face_rows(ref, row, *lead):
    return halves(
        ref[(*lead, pl.ds(row, B, stride=PLANE), slice(None))],
        ref[(*lead, pl.ds(B + row, B, stride=PLANE), slice(None))],
    )


def start_kernel(pops_ref, right_ref, left_ref, mask_ref, out_ref, aux_ref, bits_ref, open_ref):
    fill_ring(pops_ref, right_ref, left_ref, out_ref, 19)

    def body(z, carry):
        here = padded_plane(mask_ref, z + 1, 0)
        bits = jnp.where(here > 0, 1, 0)
        for which in range(1, 19):
            cx, cy, cz = DIRS[which]
            source = padded_plane(mask_ref, z + 1 - cz, cy)
            if cx:
                source = ring(source, cx)
            bits = bits + jnp.where(source * here > 0, 1 << which, 0)
        bits_ref[pl.ds(pl.multiple_of(z * PLANE, PLANE), PLANE), :] = bits
        rho, velocity = moments([plane(out_ref, z, i) for i in range(19)], here)
        for k, v in enumerate([rho] + velocity):
            aux_ref[k, pl.ds(pl.multiple_of(z * PLANE, PLANE), PLANE), :] = v
        return carry

    lax.fori_loop(0, B, body, 0)
    row = row_ids(B)
    for tile in range(2):
        for side in range(2):
            edge = tile * 32 + (7, 24)[side]
            inner = tile * 32 + (8, 23)[side]
            halo = mask_ref[pl.ds(PADDED + edge, B, stride=PADDED), :]
            own = mask_ref[pl.ds(PADDED + inner, B, stride=PADDED), :]
            first = mask_ref[pl.ds(edge, 1), :]
            last = mask_ref[pl.ds(PADROWS - PADDED + edge, 1), :]
            trans = jnp.where(row == 0, halo * first, jnp.where(row == B - 1, halo * last, 0.0))
            put_open(open_ref, 0, side, tile, halo * own)
            put_open(open_ref, 1, side, tile, trans)
            zz = (0, B + 1)[side]
            near = (1, B)[side]
            at = zz * PADDED + tile * 32
            halo = mask_ref[pl.ds(at + 8, B), :]
            own = mask_ref[pl.ds(near * PADDED + tile * 32 + 8, B), :]
            first = mask_ref[pl.ds(at + 7, 1), :]
            last = mask_ref[pl.ds(at + 24, 1), :]
            trans = jnp.where(row == 0, halo * first, jnp.where(row == B - 1, halo * last, 0.0))
            put_open(open_ref, 2, side, tile, halo * own)
            put_open(open_ref, 3, side, tile, trans)


def open_at(kind, side, tile):
    return ((kind * 2 + side) * 2 + tile) * B


def put_open(ref, kind, side, tile, v):
    ref[pl.ds(open_at(kind, side, tile), B), :] = v


def get_open(ref, kind, side):
    return ref[pl.ds(open_at(kind, side, 0), PLANE), :] > 0


def write_message(out_ref, fields):
    lane = lanes(B) // 16
    for slab in range(2):
        packed = jnp.zeros((B, L), F32)
        for k in range(8):
            f = slab * 8 + k
            if f < FIELDS:
                turn = (W + 16 * k) % L
                packed = jnp.where(lane == k, pltpu.roll(fields[f][B:], turn, axis=1), packed)
        out_ref[pl.ds((FIELDS + slab) * B, B), :] = packed
    for f in range(FIELDS):
        out_ref[pl.ds(f * B, B), :] = fields[f][:B]


def read_field(ref, f):
    side = ref[pl.ds((FIELDS + f // 8) * B, B), :]
    return halves(ref[pl.ds(f * B, B), :], pltpu.roll(side, L - W - 16 * (f % 8), axis=1))


def read_row(ref, f, row):
    side = ref[pl.ds((FIELDS + f // 8) * B + row, 1), :]
    side = jnp.broadcast_to(side, (8, L))
    main = jnp.broadcast_to(ref[pl.ds(f * B + row, 1), :], (8, L))
    return main, pltpu.roll(side, L - W - 16 * (f % 8), axis=1)


def read_diag(ref, side, f):
    base = SLABS * B + side * SLABS
    main = jnp.broadcast_to(ref[pl.ds(base + f, 1), :], (8, L))
    packed = jnp.broadcast_to(ref[pl.ds(base + FIELDS + f // 8, 1), :], (8, L))
    return main, pltpu.roll(packed, L - W - 16 * (f % 8), axis=1)


def spread8(pair):
    return halves(
        jnp.concatenate([pair[0], pair[0]], axis=0), jnp.concatenate([pair[1], pair[1]], axis=0)
    )


def partial_sum(f, inner, bits, normal_up, in_rows):
    row = row_ids(PLANE) % B
    total = f[0]
    total = total + jnp.where(is_open(bits, 1), ring(f[1], 1), f[2])
    total = total + jnp.where(is_open(bits, 2), ring(f[2], -1), f[1])
    up, down = in_rows
    moved = jnp.where(row == 0, 0.0, pltpu.roll(f[up], 1, axis=0))
    total = total + jnp.where(is_open(bits, up), moved, f[down])
    moved = jnp.where(row == B - 1, 0.0, pltpu.roll(f[down], PLANE - 1, axis=0))
    total = total + jnp.where(is_open(bits, down), moved, f[up])
    outward, inward = normal_up
    total = total + jnp.where(is_open(bits, outward), inner, f[inward])
    total = total + jnp.where(is_open(bits, inward), 0.0, f[outward])
    return total


def write_messages(pops_ref, post_ref, aux_ref, bits_ref, y_refs, z_refs):
    row = row_ids(PLANE) % B
    for side in range(2):
        names = (Y_DN, Y_UP)[side]
        edge, inner = ((0, 1), (B - 1, B - 2))[side]
        normal = ((4, 3), (3, 4))[side]
        bits = face_rows(bits_ref, edge)
        f = [face_rows(post_ref, edge, i) for i in range(7)]
        part = partial_sum(f, face_rows(post_ref, inner, normal[0]), bits, normal, (5, 6))
        fields = [face_rows(pops_ref, edge, c) for c in names]
        fields += [face_rows(aux_ref, edge, k) for k in range(4)]
        fields += [part, f[normal[0]], jnp.where(row == 0, f[6], f[5])]
        write_message(y_refs[side], fields)
    for side in range(2):
        names = (Z_DN, Z_UP)[side]
        edge, inner = ((0, 1), (B - 1, B - 2))[side]
        normal = ((6, 5), (5, 6))[side]
        bits = plane(bits_ref, edge)
        f = [plane(post_ref, edge, i) for i in range(7)]
        part = partial_sum(f, plane(post_ref, inner, normal[0]), bits, normal, (3, 4))
        fields = [plane(pops_ref, edge, c) for c in names]
        fields += [plane(aux_ref, edge, k) for k in range(4)]
        fields += [part, f[normal[0]], jnp.where(row == 0, f[4], f[3])]
        write_message(z_refs[side], fields)


def relax(f, which, rho, vx, vy, vz, base):
    a = along(which, vx, vy, vz)
    scale = (OMEGA_FLOW * WEIGHTS[which]) * rho
    return (1.0 - OMEGA_FLOW) * f + scale * (base + a * (3.0 + 4.5 * a))


def lifted(conc, vx, vy, vz):
    vz = vz + FORCE_GAIN * (conc - REST_CONC)
    return vz, 1.0 - 1.5 * (vx * vx + vy * vy + vz * vz)


def stream_solute(z, post_ref, bits, ghost_ref, zghost):
    def fill(side):
        return spread(
            ghost_ref[pl.ds(side * PLANE + z, 1), :], ghost_ref[pl.ds(side * PLANE + B + z, 1), :]
        )

    post = [plane(post_ref, z, i) for i in range(7)]
    moved = [
        None,
        ring(post[1], 1),
        ring(post[2], -1),
        shift_rows(post[3], 1, fill(0)),
        shift_rows(post[4], -1, fill(1)),
        jnp.where(z == 0, zghost[0], plane(post_ref, jnp.maximum(z - 1, 0), 5)),
        jnp.where(z == B - 1, zghost[1], plane(post_ref, jnp.minimum(z + 1, B - 1), 6)),
    ]
    return [post[0]] + [chosen(bits, moved[i], post, i) for i in range(1, 7)]


def set_ghosts(ghost_ref, y_refs, z_refs):
    for side in range(2):
        ghost_ref[pl.ds(side * PLANE, PLANE), :] = read_field(y_refs[side], NORM)
        ghost_ref[pl.ds((2 + side) * PLANE, PLANE), :] = read_field(z_refs[side], NORM)


def collide_halos(post_ref, open_ref, y_refs, z_refs, flow_ref):
    row = row_ids(PLANE) % B
    for side in range(2):
        msg = y_refs[side]
        own = face_rows(post_ref, (0, B - 1)[side], (4, 3)[side])
        ends = jnp.where(
            row == 0,
            spread8(read_diag(z_refs[0], side, TRANS)),
            spread8(read_diag(z_refs[1], side, TRANS)),
        )
        conc = read_field(msg, PART)
        conc = conc + jnp.where(get_open(open_ref, 0, side), own, 0.0)
        conc = conc + jnp.where(get_open(open_ref, 1, side), ends, 0.0)
        rho, vx, vy, vz = (read_field(msg, k) for k in range(RHO, RHO + 4))
        vz, base = lifted(conc, vx, vy, vz)
        at = PADDED + (7, 24)[side]
        for k, which in enumerate((Y_UP, Y_DN)[side]):
            v = relax(read_field(msg, k), which, rho, vx, vy, vz, base)
            flow_ref[which, pl.ds(at, B, stride=PADDED), :] = v[:B]
            flow_ref[which, pl.ds(at + 32, B, stride=PADDED), :] = v[B:]
    for side in range(2):
        msg = z_refs[side]
        own = plane(post_ref, (0, B - 1)[side], (6, 5)[side])
        ends = jnp.where(
            row == 0, spread8(read_diag(msg, 0, NORM)), spread8(read_diag(msg, 1, NORM))
        )
        conc = read_field(msg, PART)
        conc = conc + jnp.where(get_open(open_ref, 2, side), own, 0.0)
        conc = conc + jnp.where(get_open(open_ref, 3, side), ends, 0.0)
        rho, vx, vy, vz = (read_field(msg, k) for k in range(RHO, RHO + 4))
        vz, base = lifted(conc, vx, vy, vz)
        for k, which in enumerate((Z_UP, Z_DN)[side]):
            v = relax(read_field(msg, k), which, rho, vx, vy, vz, base)
            put_padded(flow_ref, which, (0, B + 1)[side], v)
    for y_side in range(2):
        for z_side in range(2):
            which = DIRS.index((0, 1 - 2 * y_side, 1 - 2 * z_side))
            names = (Y_UP, Y_DN)[y_side]
            msg = z_refs[z_side]
            z_row = (0, B - 1)[z_side]
            y_row = (0, B - 1)[y_side]
            from_y = read_row(y_refs[y_side], TRANS, z_row)
            from_z = read_row(msg, TRANS, y_row)
            get = [read_diag(msg, y_side, f) for f in range(FIELDS)]
            for tile in range(2):
                open_y = open_ref[pl.ds(open_at(1, y_side, tile) + z_row, 1), :]
                open_z = open_ref[pl.ds(open_at(3, z_side, tile) + y_row, 1), :]
                conc = get[PART][tile]
                conc = conc + jnp.where(open_y > 0, from_y[tile], 0.0)
                conc = conc + jnp.where(open_z > 0, from_z[tile], 0.0)
                rho, vx, vy, vz = (get[k][tile] for k in range(RHO, RHO + 4))
                vz, base = lifted(conc, vx, vy, vz)
                v = relax(get[names.index(which)][tile], which, rho, vx, vy, vz, base)
                at = (0, B + 1)[z_side] * PADDED + tile * 32 + (7, 24)[y_side]
                flow_ref[which, pl.ds(at, 1), :] = v[:1]


def collide_flow(z, pops_ref, aux_ref, bits, conc, flow_ref):
    porous = jnp.where(is_open(bits, 0), 1.0, 0.0)
    rho, vx, vy, vz = (plane(aux_ref, z, k) for k in range(4))
    vz = vz + porous * (FORCE_GAIN * (conc - REST_CONC))
    base = 1.0 - 1.5 * (vx * vx + vy * vy + vz * vz)
    omega = OMEGA_FLOW * porous
    keep = 1.0 - omega
    scaled = omega * rho
    v = keep * plane(pops_ref, z, 0) + (WEIGHTS[0] * scaled) * base
    put_padded(flow_ref, 0, z + 1, v)
    for i, j in PAIRS:
        a = along(i, vx, vy, vz)
        scale = WEIGHTS[i] * scaled
        even = scale * (base + 4.5 * (a * a))
        odd = scale * (3.0 * a)
        put_padded(flow_ref, i, z + 1, keep * plane(pops_ref, z, i) + (even + odd))
        put_padded(flow_ref, j, z + 1, keep * plane(pops_ref, z, j) + (even - odd))


def stream_flow(z, bits, flow_ref):
    post = [padded_plane(flow_ref, z + 1, 0, i) for i in range(19)]
    out = [post[0]]
    for which in range(1, 19):
        cx, cy, cz = DIRS[which]
        moved = post[which]
        if cy or cz:
            moved = padded_plane(flow_ref, z + 1 - cz, cy, which)
        if cx:
            moved = ring(moved, cx)
        out.append(chosen(bits, moved, post, which))
    return out


def first_kernel(
    dense_ref, right_ref, left_ref, pops_ref, aux_ref, bits_ref,
    post_ref, ydn_ref, yup_ref, zdn_ref, zup_ref, solute_ref,
):
    fill_ring(dense_ref, right_ref, left_ref, solute_ref, 7)

    def body(z, carry):
        solute = [plane(solute_ref, z, i) for i in range(7)]
        post = solute_collide(solute, [plane(aux_ref, z, k) for k in range(1, 4)])
        for i in range(7):
            post_ref[i, pl.ds(pl.multiple_of(z * PLANE, PLANE), PLANE), :] = post[i]
        return carry

    lax.fori_loop(0, B, body, 0)
    write_messages(pops_ref, post_ref, aux_ref, bits_ref, (ydn_ref, yup_ref), (zdn_ref, zup_ref))


def step_kernel(
    pops_ref, post_ref, aux_ref, bits_ref, open_ref, ylo_ref, yhi_ref, zlo_ref, zhi_ref,
    pops_out, post_out, aux_out, ydn_ref, yup_ref, zdn_ref, zup_ref,
    flow_ref, solute_ref, ghost_ref,
):
    y_refs, z_refs = (ylo_ref, yhi_ref), (zlo_ref, zhi_ref)
    set_ghosts(ghost_ref, y_refs, z_refs)
    collide_halos(post_ref, open_ref, y_refs, z_refs, flow_ref)

    def first(z, carry):
        at = pl.ds(pl.multiple_of(z * PLANE, PLANE), PLANE)
        bits = bits_ref[at, :]
        zghost = [ghost_ref[pl.ds((2 + s) * PLANE, PLANE), :] for s in range(2)]
        solute = stream_solute(z, post_ref, bits, ghost_ref, zghost)
        for i in range(7):
            solute_ref[i, at, :] = solute[i]
        collide_flow(z, pops_ref, aux_ref, bits, sum(solute), flow_ref)
        return carry

    lax.fori_loop(0, B, first, 0)

    def second(z, carry):
        at = pl.ds(pl.multiple_of(z * PLANE, PLANE), PLANE)
        bits = bits_ref[at, :]
        pops = stream_flow(z, bits, flow_ref)
        for i in range(19):
            pops_out[i, at, :] = pops[i]
        rho, velocity = moments(pops, jnp.where(is_open(bits, 0), 1.0, 0.0))
        for k, v in enumerate([rho] + velocity):
            aux_out[k, at, :] = v
        post = solute_collide([solute_ref[i, at, :] for i in range(7)], velocity)
        for i in range(7):
            post_out[i, at, :] = post[i]
        return carry

    lax.fori_loop(0, B, second, 0)
    write_messages(pops_out, post_out, aux_out, bits_ref, (ydn_ref, yup_ref), (zdn_ref, zup_ref))


def last_solute_kernel(
    slot_ref, post_ref, bits_ref, ylo_ref, yhi_ref, zlo_ref, zhi_ref,
    send_ref, turn_ref, ghost_ref,
):
    set_ghosts(ghost_ref, (ylo_ref, yhi_ref), (zlo_ref, zhi_ref))

    def body(z, carry):
        bits = plane(bits_ref, z)
        zghost = [ghost_ref[pl.ds((2 + s) * PLANE, PLANE), :] for s in range(2)]
        solute = stream_solute(z, post_ref, bits, ghost_ref, zghost)
        for i in range(7):
            for half in range(2):
                at = pl.multiple_of(i * 256 + z * B + half * 8, 8)
                turn_ref[pl.ds(at, 8), :] = turn_blocks(solute[i][half * 8 : half * 8 + 8])
        return carry

    lax.fori_loop(0, B, body, 0)
    for owner in range(8):
        tile = jnp.int32(0)
        for j in range(8):
            slot = slot_ref[0, 0, j]
            tile = jnp.where((slot >= 0) & (slot // 8 == owner), j, tile)
        send_ref[owner] = turn_ref[pl.ds(tile, BLOCKROWS // 8, stride=8), :]


def last_flow_kernel(
    pops_ref, post_ref, aux_ref, bits_ref, open_ref, ylo_ref, yhi_ref, zlo_ref, zhi_ref,
    pops_out, flow_ref, ghost_ref,
):
    y_refs, z_refs = (ylo_ref, yhi_ref), (zlo_ref, zhi_ref)
    set_ghosts(ghost_ref, y_refs, z_refs)
    collide_halos(post_ref, open_ref, y_refs, z_refs, flow_ref)

    def first(z, carry):
        bits = plane(bits_ref, z)
        zghost = [ghost_ref[pl.ds((2 + s) * PLANE, PLANE), :] for s in range(2)]
        solute = stream_solute(z, post_ref, bits, ghost_ref, zghost)
        collide_flow(z, pops_ref, aux_ref, bits, sum(solute), flow_ref)
        return carry

    lax.fori_loop(0, B, first, 0)

    def second(z, carry):
        pops = stream_flow(z, plane(bits_ref, z), flow_ref)
        for i in range(19):
            pops_out[i, pl.ds(pl.multiple_of(z * B, B), B), :] = pops[i][:B]
        return carry

    lax.fori_loop(0, B, second, 0)


def scatter_kernel(slot_ref, recv_ref, out_ref):
    for s in range(8):
        home = slot_ref[s]
        block = recv_ref[jnp.maximum(home, 0) // 8]
        out_ref[pl.ds(s, BLOCKROWS // 8, stride=8), :] = jnp.where(home >= 0, block, 0.0)


def neighbours(low, high, axis):
    count = lax.axis_size(axis)
    up = [(i, (i + 1) % count) for i in range(count)]
    down = [(i, (i - 1) % count) for i in range(count)]
    return lax.ppermute(high, axis, up), lax.ppermute(low, axis, down)


def inside(axis):
    at = lax.axis_index(axis)
    return (at > 0).astype(F32), (at < lax.axis_size(axis) - 1).astype(F32)


def padded_mask(pore_mask):
    mask = pore_mask.astype(F32)
    left, right = neighbours(mask[:, :, :W], mask[:, :, L - W :], "gx")
    has_left, has_right = inside("gx")
    gap = jnp.zeros((B, B, L - 2 * W), F32)
    side = jnp.concatenate([right * has_right, gap, left * has_left], axis=2)
    cells = jnp.stack([mask, side], axis=1)
    low, high = neighbours(cells[:, :, :1], cells[:, :, B - 1 :], "gy")
    has_low, has_high = inside("gy")
    gap = jnp.zeros((B, 2, 7, L), F32)
    cells = jnp.concatenate([gap, low * has_low, cells, high * has_high, gap], axis=2)
    low, high = neighbours(cells[:1], cells[B - 1 :], "gz")
    has_low, has_high = inside("gz")
    cells = jnp.concatenate([low * has_low, cells, high * has_high], axis=0)
    return cells.reshape(PADROWS, L)


def exchange(ydn, yup, zdn, zup):
    ylo, yhi = neighbours(ydn, yup, "gy")

    def with_edges(face, row):
        lo = ylo.reshape(SLABS, B, L)[:, row]
        hi = yhi.reshape(SLABS, B, L)[:, row]
        return jnp.concatenate([face, lo, hi, jnp.zeros((4, L), F32)], axis=0)

    zlo, zhi = neighbours(with_edges(zdn, 0), with_edges(zup, B - 1), "gz")
    return ylo, yhi, zlo, zhi


def shards(populations, solute_state, pore_mask, block_slot, slot_block):
    message = shape(SLABS * B, L)
    state = solute_state.reshape(7, 8, 32, L).transpose(0, 2, 1, 3).reshape(BLOCKROWS, L)
    send = call(gather_kernel, shape(8, 224, L), [SMEM, VMEM], [], 1, 2 * 10**6)(slot_block, state)
    recv = lax.all_to_all(send, "gz", split_axis=0, concat_axis=0, tiled=True)
    flat = populations.reshape(19 * 256, L)
    low, high = call(columns_kernel, (shape(304, L),) * 2, [VMEM], [], 10**7, 3 * 10**6)(flat)
    left, right = neighbours(low, high, "gx")
    mask = padded_mask(pore_mask)
    pops, aux, bits, opens = call(
        start_kernel,
        (
            shape(19, ROWS, L),
            shape(4, ROWS, L),
            jax.ShapeDtypeStruct((ROWS, L), jnp.int32),
            shape(PLANE * 8, L),
        ),
        [VMEM] * 4,
        [],
        10**7,
        10**7,
    )(flat, right, left, mask)
    dense, low, high = call(
        spread_kernel,
        (shape(BLOCKROWS, L), shape(112, L), shape(112, L)),
        [SMEM, VMEM],
        [pltpu.VMEM((BLOCKROWS, L), F32)],
        10**7,
        2 * 10**6,
    )(block_slot, recv)
    left, right = neighbours(low, high, "gx")
    post, *faces = call(
        first_kernel,
        (shape(7, ROWS, L),) + (message,) * 4,
        [VMEM] * 6,
        [pltpu.VMEM((7, ROWS, L), F32)],
        10**7,
        10**7,
    )(dense, right, left, pops, aux, bits)
    scratch = [
        pltpu.VMEM((19, PADROWS, L), F32),
        pltpu.VMEM((7, ROWS, L), F32),
        pltpu.VMEM((4 * PLANE, L), F32),
    ]
    for step in range(STEPS - 1):
        halos = exchange(*faces)
        pops, post, aux, *faces = call(
            step_kernel,
            (shape(19, ROWS, L), shape(7, ROWS, L), shape(4, ROWS, L)) + (message,) * 4,
            [VMEM] * 9,
            scratch,
            10**8,
            2 * 10**7,
        )(pops, post, aux, bits, opens, *halos)
    halos = exchange(*faces)
    send = call(
        last_solute_kernel,
        shape(8, 224, L),
        [SMEM] + [VMEM] * 6,
        [pltpu.VMEM((BLOCKROWS, L), F32), scratch[2]],
        10**7,
        5 * 10**6,
    )(block_slot, post, bits, *halos)
    recv = lax.all_to_all(send, "gz", split_axis=0, concat_axis=0, tiled=True)
    pops = call(
        last_flow_kernel, shape(19, 256, L), [VMEM] * 9, [scratch[0], scratch[2]], 10**8, 2 * 10**7
    )(pops, post, aux, bits, opens, *halos)
    out = call(scatter_kernel, shape(BLOCKROWS, L), [SMEM, VMEM], [], 1, 2 * 10**6)(slot_block, recv)
    new_solute = out.reshape(7, 32, 8, L).transpose(0, 2, 1, 3).reshape(7, 8, 4096)
    return pops.reshape(19, B, B, L), new_solute


def solution(mesh):
    in_specs = (
        P(None, "gz", "gy", "gx"),
        P(None, ("gx", "gy", "gz"), None),
        P("gz", "gy", "gx"),
        P("gz", "gy", "gx"),
        P(("gx", "gy", "gz")),
    )
    out_specs = (P(None, "gz", "gy", "gx"), P(None, ("gx", "gy", "gz"), None))
    return jax.shard_map(shards, mesh=mesh, in_specs=in_specs, out_specs=out_specs, check_vma=False)
```

```python
import functools

import jax
import jax.numpy as jnp
from jax import lax
from jax.experimental import pallas as pl
from jax.experimental.pallas import tpu as pltpu
from jax.sharding import PartitionSpec as P

STEPS = 4
DIRS = [
    (0, 0, 0),
    (1, 0, 0),
    (-1, 0, 0),
    (0, 1, 0),
    (0, -1, 0),
    (0, 0, 1),
    (0, 0, -1),
    (1, 1, 0),
    (-1, -1, 0),
    (1, -1, 0),
    (-1, 1, 0),
    (1, 0, 1),
    (-1, 0, -1),
    (1, 0, -1),
    (-1, 0, 1),
    (0, 1, 1),
    (0, -1, -1),
    (0, 1, -1),
    (0, -1, 1),
]
OPP = [DIRS.index((-a, -b, -c)) for a, b, c in DIRS]
PAIRS = [(i, OPP[i]) for i in range(1, 19, 2)]
WEIGHTS = [1.0 / 3.0] + [1.0 / 18.0] * 6 + [1.0 / 36.0] * 12
OMEGA_FLOW = 1.2
FORCE_GAIN = 0.02
REST_CONC = 8.0
Y_UP = [i for i in range(19) if DIRS[i][1] == 1]
Y_DN = [i for i in range(19) if DIRS[i][1] == -1]
Z_UP = [i for i in range(19) if DIRS[i][2] == 1]
Z_DN = [i for i in range(19) if DIRS[i][2] == -1]
RHO, VEL, PART, NORM, TRANS, MASK = 5, 6, 9, 10, 11, 12
SIDES = 2
B = 16
L = 128
W = 8
PLANE = 2 * B
ROWS = B * PLANE
PADDED = 64
PADROWS = (B + 2) * PADDED
BLOCKROWS = 7 * 32 * 8
F32 = jnp.float32
VMEM = pl.BlockSpec(memory_space=pltpu.VMEM)
SMEM = pl.BlockSpec(memory_space=pltpu.SMEM)


def call(kernel, out_shape, in_specs, scratch, flops, nbytes, aliases={}, keep=False):
    run = pl.pallas_call(
        kernel,
        out_shape=out_shape,
        in_specs=in_specs,
        out_specs=jax.tree.map(lambda _: VMEM, out_shape),
        scratch_shapes=scratch,
        input_output_aliases=aliases,
        compiler_params=pltpu.CompilerParams(vmem_limit_bytes=20 * 1024 * 1024),
        cost_estimate=pl.CostEstimate(flops=flops, bytes_accessed=nbytes, transcendentals=0),
    )

    if not keep:
        return run

    def placed(*args):
        return run(
            *(
                pltpu.with_memory_space_constraint(x, pltpu.VMEM) if spec is VMEM else x
                for x, spec in zip(args, in_specs)
            )
        )

    return placed


def shape(*dims):
    return jax.ShapeDtypeStruct(dims, F32)


def held(*dims, dtype=F32):
    return pltpu.VMEM(dims, dtype)


def lanes(rows):
    return lax.broadcasted_iota(jnp.int32, (rows, L), 1)


def row_ids(rows):
    return lax.broadcasted_iota(jnp.int32, (rows, L), 0)


def ring(v, step):
    rolled = pltpu.roll(v, step % L, axis=1)
    other = jnp.concatenate([rolled[B:], rolled[:B]], axis=0)
    return jnp.where(lanes(PLANE) == (0 if step > 0 else L - 1), other, rolled)


def halves(main, side):
    return jnp.concatenate([main, side], axis=0)


def spread(main, side):
    return halves(jnp.broadcast_to(main, (B, L)), jnp.broadcast_to(side, (B, L)))


def shift_rows(v, step, fill):
    rolled = pltpu.roll(v, step % PLANE, axis=0)
    return jnp.where(row_ids(PLANE) % B == (0 if step > 0 else B - 1), fill, rolled)


def is_open(bits, which):
    return (bits & (1 << which)) != 0


def along(which, vx, vy, vz):
    total = None
    for sign, part in zip(DIRS[which], (vx, vy, vz)):
        if sign != 0:
            if total is None:
                total = part if sign > 0 else -part
            else:
                total = total + part if sign > 0 else total - part
    return total


def moments(pops, porous):
    rho = pops[0]
    for which in range(1, 19):
        rho = rho + pops[which]
    scale = porous / rho
    parts = []
    for coord in range(3):
        plus = sum(pops[i] for i in range(19) if DIRS[i][coord] == 1)
        minus = sum(pops[i] for i in range(19) if DIRS[i][coord] == -1)
        parts.append((plus - minus) * scale)
    return rho, parts


def solute_collide(solute, velocity):
    conc = sum(solute)
    out = [-0.5 * solute[0] + 0.375 * conc]
    base = 0.1875 * conc
    for coord in range(3):
        turn = 0.75 * conc * velocity[coord]
        out.append((base - 0.5 * solute[1 + 2 * coord]) + turn)
        out.append((base - 0.5 * solute[2 + 2 * coord]) - turn)
    return out


def chosen(bits, moved, post, which):
    return jnp.where(
        is_open(bits, which),
        moved,
        jnp.where(is_open(bits, 0), post[OPP[which]], post[which]),
    )


def turn_blocks(x):
    row, lane = row_ids(8), lanes(8)
    x = take(x, (lane - B * row) & (L - 1), 1)
    x = take(x, (lane // B - row) & 7, 0)
    return take(x, (lane + B * row) & (L - 1), 1)


def take(x, index, axis):
    return jnp.take_along_axis(x, index, axis=axis, mode="promise_in_bounds")


def gather_kernel(slot_ref, state_ref, send_ref):
    for dest in range(8):
        slot = jnp.int32(0)
        for s in range(8):
            home = slot_ref[s]
            slot = jnp.where((home >= 0) & (home // 8 == dest), s, slot)
        send_ref[dest] = state_ref[pl.ds(slot, BLOCKROWS // 8, stride=8), :]


def spread_kernel(slot_ref, recv_ref, dense_ref, turn_ref):
    for tile in range(8):
        owner = jnp.maximum(slot_ref[0, 0, tile], 0) // 8
        turn_ref[pl.ds(tile, BLOCKROWS // 8, stride=8), :] = recv_ref[owner]

    def body(group, carry):
        for i in range(16):
            at = pl.multiple_of(group * 128 + i * 8, 8)
            dense_ref[pl.ds(at, 8), :] = turn_blocks(turn_ref[pl.ds(at, 8), :])
        return carry

    lax.fori_loop(0, BLOCKROWS // 128, body, 0)


def pack_columns(load, low_ref, high_ref, at):
    lane = lanes(8) // W
    low = jnp.zeros((8, L), F32)
    high = jnp.zeros((8, L), F32)
    for i in range(16):
        x = load(i)
        low = jnp.where(lane == i, x if i == 0 else pltpu.roll(x, W * i, axis=1), low)
        turn = (W + W * i) % L
        high = jnp.where(lane == i, x if turn == 0 else pltpu.roll(x, turn, axis=1), high)
    at = pl.multiple_of(at, 8)
    low_ref[pl.ds(at, 8), :] = low
    high_ref[pl.ds(at, 8), :] = high


def columns_kernel(pops_ref, mask_ref, low_ref, high_ref):
    def rows(start, i):
        return pl.ds(pl.multiple_of(start + i * 8, 8), 8)

    def body(group, carry):
        at = (group % 2) * 128
        pack_columns(
            lambda i: pops_ref[group // 2, rows(at, i), :], low_ref, high_ref, group * 8
        )
        return carry

    lax.fori_loop(0, 38, body, 0)
    for group in range(2):
        pack_columns(
            lambda i: mask_ref[rows(group * 128, i), :].astype(F32),
            low_ref,
            high_ref,
            (38 + group) * 8,
        )


def unpack_columns(right, left, i):
    a = right if i == 0 else pltpu.roll(right, L - W * i, axis=1)
    b = left if i == 15 else pltpu.roll(left, L - W - W * i, axis=1)
    return jnp.where(lanes(8) < L // 2, a, b)


def ring_kernel(
    flag_ref, pops_ref, mask_ref, right_ref, left_ref,
    side_ref, ring_ref, aux_ref,
):
    def body(group, carry):
        at = pl.ds(pl.multiple_of(group * 8, 8), 8)
        right, left = right_ref[at, :], left_ref[at, :]
        for i in range(16):
            row = pl.multiple_of((group % 2) * 128 + i * 8, 8)
            side_ref[group // 2, pl.ds(row, 8), :] = unpack_columns(right, left, i)
        return carry

    lax.fori_loop(0, 38, body, 0)
    lane = lanes(8)
    inside = jnp.where(lane < W, flag_ref[1], jnp.where(lane >= L - W, flag_ref[0], 0.0))
    for group in range(2):
        right, left = right_ref[pl.ds(304 + group * 8, 8), :], left_ref[pl.ds(304 + group * 8, 8), :]
        for i in range(16):
            z = group * 8 + i // 2
            row = z * PLANE + (i % 2) * 8
            ring_ref[pl.ds(row, 8), :] = mask_ref[pl.ds(group * 128 + i * 8, 8), :].astype(F32)
            ring_ref[pl.ds(row + B, 8), :] = unpack_columns(right, left, i) * inside
    def flow(z, carry):
        pops = [flow_plane((pops_ref, side_ref), z, i) for i in range(19)]
        rho, velocity = moments(pops, plane(ring_ref, z))
        for k, v in enumerate([rho] + velocity):
            aux_ref[k, pl.ds(pl.multiple_of(z * PLANE, PLANE), PLANE), :] = v
        return carry

    lax.fori_loop(0, B, flow, 0)


def plane(ref, z, *lead):
    return ref[(*lead, pl.ds(pl.multiple_of(z * PLANE, PLANE), PLANE), slice(None))]


def flow_plane(refs, z, which):
    at = pl.ds(pl.multiple_of(z * B, B), B)
    return halves(refs[0][which, at, :], refs[1][which, at, :])


def flow_rows(refs, row, which):
    at = pl.ds(row, B, stride=B)
    return halves(refs[0][which, at, :], refs[1][which, at, :])


def padded_plane(ref, zz, shift, *lead):
    at = zz * PADDED + 8
    return halves(
        ref[(*lead, pl.ds(at - shift, B), slice(None))],
        ref[(*lead, pl.ds(at + 32 - shift, B), slice(None))],
    )


def put_rows(ref, zz, v):
    ref[pl.ds(zz * PADDED + 8, B), :] = v[:B]
    ref[pl.ds(zz * PADDED + 40, B), :] = v[B:]


def put_padded(ref, comp, zz, v):
    at = zz * PADDED + 8
    if not isinstance(zz, int):
        at = pl.multiple_of(at, 8)
    ref[comp, pl.ds(at, B), :] = v[:B]
    ref[comp, pl.ds(at + 32, B), :] = v[B:]


def face_rows(ref, row, *lead):
    return halves(
        ref[(*lead, pl.ds(row, B, stride=PLANE), slice(None))],
        ref[(*lead, pl.ds(B + row, B, stride=PLANE), slice(None))],
    )


def set_bits(mask_ref, bits_ref, z):
    here = padded_plane(mask_ref, z + 1, 0)
    bits = jnp.where(here > 0, 1, 0)
    for which in range(1, 19):
        cx, cy, cz = DIRS[which]
        source = padded_plane(mask_ref, z + 1 - cz, cy)
        if cx:
            source = ring(source, cx)
        bits = bits + jnp.where(source * here > 0, 1 << which, 0)
    bits_ref[pl.ds(pl.multiple_of(z * PLANE, PLANE), PLANE), :] = bits


def inner_open_kernel(flag_ref, ring_ref, ylo_ref, yhi_ref, mask_ref, bits_ref, open_ref):
    mask_ref[...] = jnp.zeros_like(mask_ref)
    for z in range(B):
        put_rows(mask_ref, z + 1, ring_ref[pl.ds(z * PLANE, PLANE), :])
    for side in range(2):
        halo = read_field((ylo_ref, yhi_ref)[side], MASK) * flag_ref[2 + side]
        for tile in range(2):
            part = halo[tile * B : (tile + 1) * B]
            edge = PADDED + tile * 32 + (7, 24)[side]
            inner = PADDED + tile * 32 + (8, 23)[side]
            mask_ref[pl.ds(edge, B, stride=PADDED), :] = part
            own = mask_ref[pl.ds(inner, B, stride=PADDED), :]
            put_open(open_ref, 0, side, tile, part * own)

    def body(z, carry):
        set_bits(mask_ref, bits_ref, z)
        return carry

    lax.fori_loop(1, B - 1, body, 0)


def edge_open_kernel(
    flag_ref, zlo_ref, zhi_ref, mask_in, bits_in, open_in, mask_ref, bits_ref, open_ref
):
    row = row_ids(B)
    for side in range(2):
        z_ref, zz = (zlo_ref, zhi_ref)[side], (0, B + 1)[side]
        put_rows(mask_ref, zz, read_field(z_ref, MASK) * flag_ref[4 + side])
        for y_side in range(2):
            pair = read_diag(z_ref, y_side, MASK)
            for tile in range(2):
                at = zz * PADDED + tile * 32 + (7, 24)[y_side]
                scale = flag_ref[4 + side] * flag_ref[2 + y_side]
                mask_ref[pl.ds(at, 1), :] = pair[tile][:1] * scale

    def body(k, carry):
        set_bits(mask_ref, bits_ref, k * (B - 1))
        return carry

    lax.fori_loop(0, 2, body, 0)
    for tile in range(2):
        for side in range(2):
            edge = tile * 32 + (7, 24)[side]
            halo = mask_ref[pl.ds(PADDED + edge, B, stride=PADDED), :]
            first = mask_ref[pl.ds(edge, 1), :]
            last = mask_ref[pl.ds(PADROWS - PADDED + edge, 1), :]
            ends = jnp.where(row == 0, halo * first, jnp.where(row == B - 1, halo * last, 0.0))
            put_open(open_ref, 1, side, tile, ends)
            at = (0, B + 1)[side] * PADDED + tile * 32
            near = (1, B)[side]
            halo = mask_ref[pl.ds(at + 8, B), :]
            own = mask_ref[pl.ds(near * PADDED + tile * 32 + 8, B), :]
            first = mask_ref[pl.ds(at + 7, 1), :]
            last = mask_ref[pl.ds(at + 24, 1), :]
            ends = jnp.where(row == 0, halo * first, jnp.where(row == B - 1, halo * last, 0.0))
            put_open(open_ref, 2, side, tile, halo * own)
            put_open(open_ref, 3, side, tile, ends)


def open_at(kind, side, tile):
    return ((kind * 2 + side) * 2 + tile) * B


def put_open(ref, kind, side, tile, v):
    ref[pl.ds(open_at(kind, side, tile), B), :] = v


def get_open(ref, kind, side):
    return ref[pl.ds(open_at(kind, side, 0), PLANE), :] > 0


def write_message(out_ref, fields):
    lane = lanes(B) // 16
    for slab in range(SIDES):
        packed = jnp.zeros((B, L), F32)
        for k, field in enumerate(fields[slab * 8 : slab * 8 + 8]):
            turn = (W + 16 * k) % L
            packed = jnp.where(lane == k, pltpu.roll(field[B:], turn, axis=1), packed)
        out_ref[pl.ds(slab * B, B), :] = packed
    for f, field in enumerate(fields):
        out_ref[pl.ds((SIDES + f) * B, B), :] = field[:B]


def unpack_side(packed, f):
    return pltpu.roll(packed, L - W - 16 * (f % 8), axis=1)


def read_field(ref, f):
    side = ref[pl.ds(f // 8 * B, B), :]
    return halves(ref[pl.ds((SIDES + f) * B, B), :], unpack_side(side, f))


def read_row(ref, f, row):
    main = jnp.broadcast_to(ref[pl.ds((SIDES + f) * B + row, 1), :], (8, L))
    side = jnp.broadcast_to(ref[pl.ds(f // 8 * B + row, 1), :], (8, L))
    return main, unpack_side(side, f)


def read_diag(ref, side, f):
    slabs = ref.shape[0] // (B + 2)
    base = slabs * B + side * slabs
    main = jnp.broadcast_to(ref[pl.ds(base + SIDES + f, 1), :], (8, L))
    packed = jnp.broadcast_to(ref[pl.ds(base + f // 8, 1), :], (8, L))
    return main, unpack_side(packed, f)


def spread8(pair):
    return halves(
        jnp.concatenate([pair[0], pair[0]], axis=0), jnp.concatenate([pair[1], pair[1]], axis=0)
    )


def partial_sum(f, inner, is_open, outward, in_rows):
    row = row_ids(PLANE) % B
    total = f[0]
    total = total + jnp.where(is_open(1), ring(f[1], 1), f[2])
    total = total + jnp.where(is_open(2), ring(f[2], -1), f[1])
    up, down = in_rows
    moved = jnp.where(is_open(up), pltpu.roll(f[up], 1, axis=0), f[down])
    total = total + jnp.where(row == 0, 0.0, moved)
    moved = jnp.where(is_open(down), pltpu.roll(f[down], PLANE - 1, axis=0), f[up])
    total = total + jnp.where(row == B - 1, 0.0, moved)
    return total + jnp.where(is_open(outward), inner, f[OPP[outward]])


def open_bits(bits):
    return lambda which: is_open(bits, which)


def open_mask(own, inner, in_rows):
    shifted = {
        1: ring(own, 1),
        2: ring(own, -1),
        in_rows[0]: pltpu.roll(own, 1, axis=0),
        in_rows[1]: pltpu.roll(own, PLANE - 1, axis=0),
    }
    return lambda which: shifted.get(which, inner) > 0


def write_y_messages(pops_refs, post_ref, aux_ref, y_refs, bits_ref=None, ring_ref=None):
    row = row_ids(PLANE) % B
    for side in range(2):
        names = (Y_DN, Y_UP)[side]
        edge, inner = ((0, 1), (B - 1, B - 2))[side]
        normal = (4, 3)[side]
        if ring_ref is None:
            opened = open_bits(face_rows(bits_ref, edge))
        else:
            opened = open_mask(face_rows(ring_ref, edge), face_rows(ring_ref, inner), (5, 6))
        f = [face_rows(post_ref, edge, i) for i in range(7)]
        part = partial_sum(f, face_rows(post_ref, inner, normal), opened, normal, (5, 6))
        fields = [flow_rows(pops_refs, edge, c) for c in names]
        fields += [face_rows(aux_ref, edge, k) for k in range(4)]
        fields += [part, f[normal], jnp.where(row == 0, f[6], f[5])]
        if ring_ref is not None:
            fields.append(face_rows(ring_ref, edge))
        write_message(y_refs[side], fields)


def write_z_messages(pops_refs, post_ref, aux_ref, z_refs, bits_ref=None, ring_ref=None):
    row = row_ids(PLANE) % B
    for side in range(2):
        names = (Z_DN, Z_UP)[side]
        edge, inner = ((0, 1), (B - 1, B - 2))[side]
        normal = (6, 5)[side]
        if ring_ref is None:
            opened = open_bits(plane(bits_ref, edge))
        else:
            opened = open_mask(plane(ring_ref, edge), plane(ring_ref, inner), (3, 4))
        f = [plane(post_ref, edge, i) for i in range(7)]
        part = partial_sum(f, plane(post_ref, inner, normal), opened, normal, (3, 4))
        fields = [flow_plane(pops_refs, edge, c) for c in names]
        fields += [plane(aux_ref, edge, k) for k in range(4)]
        fields += [part, f[normal], jnp.where(row == 0, f[4], f[3])]
        if ring_ref is not None:
            fields.append(plane(ring_ref, edge))
        write_message(z_refs[side], fields)


def relax(f, which, rho, vx, vy, vz, base):
    a = along(which, vx, vy, vz)
    scale = (OMEGA_FLOW * WEIGHTS[which]) * rho
    return (1.0 - OMEGA_FLOW) * f + scale * (base + a * (3.0 + 4.5 * a))


def lifted(conc, vx, vy, vz):
    vz = vz + FORCE_GAIN * (conc - REST_CONC)
    return vz, 1.0 - 1.5 * (vx * vx + vy * vy + vz * vz)


def stream_solute(z, post_ref, bits, ghost_ref, below, above):
    def fill(side):
        return spread(
            ghost_ref[pl.ds(side * PLANE + z, 1), :], ghost_ref[pl.ds(side * PLANE + B + z, 1), :]
        )

    post = [plane(post_ref, z, i) for i in range(7)]
    moved = [
        None,
        ring(post[1], 1),
        ring(post[2], -1),
        shift_rows(post[3], 1, fill(0)),
        shift_rows(post[4], -1, fill(1)),
        below,
        above,
    ]
    return [post[0]] + [chosen(bits, moved[i], post, i) for i in range(1, 7)]


def set_ghosts(ghost_ref, y_refs):
    for side in range(2):
        ghost_ref[pl.ds(side * PLANE, PLANE), :] = read_field(y_refs[side], NORM)


def collide_face(msg, names, conc, put):
    rho, vx, vy, vz = (read_field(msg, k) for k in range(RHO, RHO + 4))
    vz, base = lifted(conc, vx, vy, vz)
    for k, which in enumerate(names):
        put(which, relax(read_field(msg, k), which, rho, vx, vy, vz, base))


def collide_y_halos(post_ref, open_ref, y_refs, z_refs, flow_ref):
    row = row_ids(PLANE) % B
    for side in range(2):
        msg = y_refs[side]
        own = face_rows(post_ref, (0, B - 1)[side], (4, 3)[side])
        conc = read_field(msg, PART)
        conc = conc + jnp.where(get_open(open_ref, 0, side), own, read_field(msg, NORM))
        if z_refs is not None:
            ends = jnp.where(
                row == 0,
                spread8(read_diag(z_refs[0], side, TRANS)),
                spread8(read_diag(z_refs[1], side, TRANS)),
            )
            ends = jnp.where(get_open(open_ref, 1, side), ends, read_field(msg, TRANS))
            conc = conc + ends
        at = PADDED + (7, 24)[side]

        def put(which, v):
            for tile in range(2):
                part = v[tile * B : (tile + 1) * B]
                if z_refs is None:
                    flow_ref[which, pl.ds(at + tile * 32, B, stride=PADDED), :] = part
                else:
                    for z in (0, B - 1):
                        flow_ref[which, pl.ds(at + tile * 32 + z * PADDED, 1), :] = part[z : z + 1]

        collide_face(msg, (Y_UP, Y_DN)[side], conc, put)


def collide_z_halos(post_ref, open_ref, y_refs, z_refs, flow_ref):
    row = row_ids(PLANE) % B
    for side in range(2):
        msg = z_refs[side]
        own = plane(post_ref, (0, B - 1)[side], (6, 5)[side])
        ends = jnp.where(
            row == 0, spread8(read_diag(msg, 0, NORM)), spread8(read_diag(msg, 1, NORM))
        )
        ends = jnp.where(get_open(open_ref, 3, side), ends, read_field(msg, TRANS))
        conc = read_field(msg, PART)
        conc = conc + jnp.where(get_open(open_ref, 2, side), own, read_field(msg, NORM))
        conc = conc + jnp.where((row == 0) | (row == B - 1), ends, 0.0)
        zz = (0, B + 1)[side]
        collide_face(
            msg, (Z_UP, Z_DN)[side], conc, lambda which, v: put_padded(flow_ref, which, zz, v)
        )
    for y_side in range(2):
        for z_side in range(2):
            which = DIRS.index((0, 1 - 2 * y_side, 1 - 2 * z_side))
            names = (Y_UP, Y_DN)[y_side]
            msg = z_refs[z_side]
            z_row = (0, B - 1)[z_side]
            y_row = (0, B - 1)[y_side]
            from_y = read_row(y_refs[y_side], TRANS, z_row)
            from_z = read_row(msg, TRANS, y_row)
            get = [read_diag(msg, y_side, f) for f in range(TRANS + 1)]
            for tile in range(2):
                open_y = open_ref[pl.ds(open_at(1, y_side, tile) + z_row, 1), :]
                open_z = open_ref[pl.ds(open_at(3, z_side, tile) + y_row, 1), :]
                conc = get[PART][tile]
                conc = conc + jnp.where(open_y > 0, from_y[tile], get[TRANS][tile])
                conc = conc + jnp.where(open_z > 0, from_z[tile], get[NORM][tile])
                rho, vx, vy, vz = (get[k][tile] for k in range(RHO, RHO + 4))
                vz, base = lifted(conc, vx, vy, vz)
                v = relax(get[names.index(which)][tile], which, rho, vx, vy, vz, base)
                at = (0, B + 1)[z_side] * PADDED + tile * 32 + (7, 24)[y_side]
                flow_ref[which, pl.ds(at, 1), :] = v[:1]


def collide_flow(z, pops_refs, aux_ref, bits, conc, flow_ref):
    porous = jnp.where(is_open(bits, 0), 1.0, 0.0)
    rho, vx, vy, vz = (plane(aux_ref, z, k) for k in range(4))
    vz = vz + porous * (FORCE_GAIN * (conc - REST_CONC))
    base = 1.0 - 1.5 * (vx * vx + vy * vy + vz * vz)
    omega = OMEGA_FLOW * porous
    keep = 1.0 - omega
    scaled = omega * rho
    v = keep * flow_plane(pops_refs, z, 0) + (WEIGHTS[0] * scaled) * base
    put_padded(flow_ref, 0, z + 1, v)
    for i, j in PAIRS:
        a = along(i, vx, vy, vz)
        scale = WEIGHTS[i] * scaled
        even = scale * (base + 4.5 * (a * a))
        odd = scale * (3.0 * a)
        put_padded(flow_ref, i, z + 1, keep * flow_plane(pops_refs, z, i) + (even + odd))
        put_padded(flow_ref, j, z + 1, keep * flow_plane(pops_refs, z, j) + (even - odd))


def stream_flow(z, bits, flow_ref):
    post = [padded_plane(flow_ref, z + 1, 0, i) for i in range(19)]
    out = [post[0]]
    for which in range(1, 19):
        cx, cy, cz = DIRS[which]
        moved = post[which]
        if cy or cz:
            moved = padded_plane(flow_ref, z + 1 - cz, cy, which)
        if cx:
            moved = ring(moved, cx)
        out.append(chosen(bits, moved, post, which))
    return out


def first_kernel(
    dense_ref, right_ref, left_ref, pops_ref, side_ref, aux_ref, ring_ref,
    post_ref, ydn_ref, yup_ref, zdn_ref, zup_ref, turn_ref,
):
    turn_ref[pl.ds(0, BLOCKROWS // 8, stride=8), :] = right_ref[...]
    turn_ref[pl.ds(7, BLOCKROWS // 8, stride=8), :] = left_ref[...]
    lane = lanes(8)
    near = (lane < W) | (lane >= L - W)

    def body(z, carry):
        solute = []
        for i in range(7):
            at = pl.multiple_of(i * 256 + z * B, B)
            side = [
                jnp.where(near, turn_blocks(turn_ref[pl.ds(at + 8 * k, 8), :]), 0.0)
                for k in range(2)
            ]
            solute.append(jnp.concatenate([dense_ref[pl.ds(at, B), :]] + side, axis=0))
        post = solute_collide(solute, [plane(aux_ref, z, k) for k in range(1, 4)])
        for i in range(7):
            post_ref[i, pl.ds(pl.multiple_of(z * PLANE, PLANE), PLANE), :] = post[i]
        return carry

    lax.fori_loop(0, B, body, 0)
    pops_refs = pops_ref, side_ref
    write_y_messages(pops_refs, post_ref, aux_ref, (ydn_ref, yup_ref), ring_ref=ring_ref)
    write_z_messages(pops_refs, post_ref, aux_ref, (zdn_ref, zup_ref), ring_ref=ring_ref)


def pull(z, refs, bits_ref, flow_ref, solute_ref):
    pops_ref, side_ref, post_ref, aux_ref = refs
    at = pl.ds(pl.multiple_of(z * PLANE, PLANE), PLANE)
    main = pl.ds(pl.multiple_of(z * B, B), B)
    bits = bits_ref[at, :]
    pops = stream_flow(z, bits, flow_ref)
    for i in range(19):
        pops_ref[i, main, :] = pops[i][:B]
        if side_ref is not None:
            side_ref[i, main, :] = pops[i][B:]
    if side_ref is None:
        return
    rho, velocity = moments(pops, jnp.where(is_open(bits, 0), 1.0, 0.0))
    for k, v in enumerate([rho] + velocity):
        aux_ref[k, at, :] = v
    post = solute_collide([solute_ref[i, at, :] for i in range(7)], velocity)
    for i in range(7):
        post_ref[i, at, :] = post[i]


def push(z, refs, bits, solute, flow_ref, solute_ref, turn_ref):
    pops_ref, side_ref, post_ref, aux_ref = refs
    for i in range(7):
        if turn_ref is None:
            solute_ref[i, pl.ds(pl.multiple_of(z * PLANE, PLANE), PLANE), :] = solute[i]
        else:
            for half in range(2):
                at = pl.multiple_of(i * 256 + z * B + half * 8, 8)
                turn_ref[pl.ds(at, 8), :] = turn_blocks(solute[i][half * 8 : half * 8 + 8])
    collide_flow(z, (pops_ref, side_ref), aux_ref, bits, sum(solute), flow_ref)


def inner_kernel(last, *refs):
    pops_in, side_in, post_in, aux_in, bits_ref, open_ref, ylo_ref, yhi_ref = refs[:8]
    if last:
        pops_ref, flow_ref, turn_ref, ghost_ref = refs[8:]
        state, out = (pops_ref, side_in, post_in, aux_in), (pops_ref, None, None, None)
        solute_ref = None
    else:
        pops_ref, side_ref, post_ref, aux_ref, flow_ref, solute_ref, ghost_ref = refs[8:]
        state = out = (pops_ref, side_ref, post_ref, aux_ref)
        turn_ref = None
    set_ghosts(ghost_ref, (ylo_ref, yhi_ref))
    collide_y_halos(state[2], open_ref, (ylo_ref, yhi_ref), None, flow_ref)

    def first(z, carry):
        bits = plane(bits_ref, z)
        post_ref = state[2]
        solute = stream_solute(
            z, post_ref, bits, ghost_ref, plane(post_ref, z - 1, 5), plane(post_ref, z + 1, 6)
        )
        push(z, state, bits, solute, flow_ref, solute_ref, turn_ref)
        return carry

    def second(z, carry):
        pull(z, out, bits_ref, flow_ref, solute_ref)
        return carry

    lax.fori_loop(1, B - 1, first, 0)
    lax.fori_loop(2, B - 2, second, 0)


def edge_kernel(last, *refs):
    if last:
        slot_ref, refs = refs[0], refs[1:]
    pops_in, side_in, post_in, aux_in, flow_in, solute_ref, bits_ref, open_ref = refs[:8]
    y_refs, z_refs = refs[8:10], refs[10:12]
    if last:
        pops_ref, flow_ref, turn_ref, send_ref, ghost_ref = refs[12:]
        state, out = (pops_ref, side_in, post_in, aux_in), (pops_ref, None, None, None)
    else:
        pops_ref, side_ref, post_ref, aux_ref, flow_ref, ydn_ref, yup_ref, ghost_ref = refs[12:]
        state = out = (pops_ref, side_ref, post_ref, aux_ref)
        turn_ref = None
    set_ghosts(ghost_ref, y_refs)
    post_ref = state[2]
    collide_y_halos(post_ref, open_ref, y_refs, z_refs, flow_ref)
    collide_z_halos(post_ref, open_ref, y_refs, z_refs, flow_ref)
    for z in (0, B - 1):
        bits = plane(bits_ref, z)
        below = read_field(z_refs[0], NORM) if z == 0 else plane(post_ref, z - 1, 5)
        above = read_field(z_refs[1], NORM) if z == B - 1 else plane(post_ref, z + 1, 6)
        solute = stream_solute(z, post_ref, bits, ghost_ref, below, above)
        push(z, state, bits, solute, flow_ref, solute_ref, turn_ref)

    def second(k, carry):
        pull(k + 12 * (k // 2), out, bits_ref, flow_ref, solute_ref)
        return carry

    lax.fori_loop(0, 4, second, 0)
    if not last:
        write_y_messages(
            (pops_ref, side_ref), post_ref, aux_ref, (ydn_ref, yup_ref), bits_ref=bits_ref
        )
        return
    for owner in range(8):
        tile = jnp.int32(0)
        for j in range(8):
            slot = slot_ref[0, 0, j]
            tile = jnp.where((slot >= 0) & (slot // 8 == owner), j, tile)
        send_ref[owner] = turn_ref[pl.ds(tile, BLOCKROWS // 8, stride=8), :]


def z_kernel(pops_ref, side_ref, post_ref, aux_ref, bits_ref, zdn_ref, zup_ref):
    write_z_messages(
        (pops_ref, side_ref), post_ref, aux_ref, (zdn_ref, zup_ref), bits_ref=bits_ref
    )


def scatter_kernel(slot_ref, recv_ref, out_ref):
    for s in range(8):
        home = slot_ref[s]
        block = recv_ref[jnp.maximum(home, 0) // 8]
        out_ref[pl.ds(s, BLOCKROWS // 8, stride=8), :] = jnp.where(home >= 0, block, 0.0)


def neighbours(low, high, axis):
    count = lax.axis_size(axis)
    up = [(i, (i + 1) % count) for i in range(count)]
    down = [(i, (i - 1) % count) for i in range(count)]
    return lax.ppermute(high, axis, up), lax.ppermute(low, axis, down)


def inside():
    flags = []
    for axis in ("gx", "gy", "gz"):
        at = lax.axis_index(axis)
        flags += [at > 0, at < lax.axis_size(axis) - 1]
    return jnp.stack(flags).astype(F32)


def with_edges(face, halos, row):
    slabs = face.shape[0] // B
    rows = [face] + [halo.reshape(slabs, B, L)[:, row] for halo in halos]
    pad = -slabs * (B + 2) % 8
    return jnp.concatenate(rows + [jnp.zeros((pad, L), F32)], axis=0)


def exchange_z(halos, zdn, zup):
    return neighbours(with_edges(zdn, halos, 0), with_edges(zup, halos, B - 1), "gz")


def shards(populations, solute_state, pore_mask, block_slot, slot_block):
    flags = inside()
    state = solute_state.reshape(7, 8, 32, L).transpose(0, 2, 1, 3).reshape(BLOCKROWS, L)
    send = call(gather_kernel, shape(8, 224, L), [SMEM, VMEM], [], 1, 2 * 10**6)(slot_block, state)
    recv = lax.all_to_all(send, "gz", split_axis=0, concat_axis=0, tiled=True)

    pops = populations.reshape(19, 256, L)
    mask = pore_mask.reshape(256, L)
    low, high = call(columns_kernel, (shape(320, L),) * 2, [VMEM] * 2, [], 10**7, 3 * 10**6)(
        pops, mask
    )
    left, right = neighbours(low, high, "gx")
    side, ring_mask, aux = call(
        ring_kernel,
        (shape(19, 256, L), shape(ROWS, L), shape(4, ROWS, L)),
        [SMEM] + [VMEM] * 4,
        [],
        10**7,
        10**7,
    )(flags, pops, mask, right, left)

    def block_of(tile):
        owner = jnp.maximum(block_slot[0, 0, tile], 0) // 8
        return lax.dynamic_index_in_dim(recv, owner, 0, keepdims=False)

    left, right = neighbours(block_of(0), block_of(7), "gx")
    turn = pltpu.VMEM((BLOCKROWS, L), F32)
    dense = call(spread_kernel, shape(BLOCKROWS, L), [SMEM, VMEM], [turn], 10**7, 2 * 10**6)(
        block_slot, recv
    )
    message = shape((SIDES + MASK + 1) * B, L)
    post, ydn, yup, zdn, zup = call(
        first_kernel, (shape(7, ROWS, L),) + (message,) * 4, [VMEM] * 7, [turn], 10**7, 10**7
    )(dense, right, left, pops, side, aux, ring_mask)

    ghost = pltpu.VMEM((2 * PLANE, L), F32)
    states = (held(19, 256, L), held(19, 256, L), held(7, ROWS, L), held(4, ROWS, L))
    flow_out, solute_out = held(19, PADROWS, L), held(7, ROWS, L)
    bits_out, open_out = held(ROWS, L, dtype=jnp.int32), held(PLANE * 8, L)
    message = held((SIDES + MASK) * B, L)
    state = (pops, side, post, aux)
    for step in range(STEPS):
        last = step == STEPS - 1
        y_halos = neighbours(ydn, yup, "gy")
        z_halos = exchange_z(y_halos, zdn, zup)
        if step == 0:
            mask, bits, opens = call(
                inner_open_kernel,
                (held(PADROWS, L), bits_out, open_out),
                [SMEM] + [VMEM] * 3,
                [],
                10**7,
                10**6,
                keep=True,
            )(flags, ring_mask, *y_halos)
        if last:
            outs = (states[0], flow_out, held(BLOCKROWS, L))
            aliases = {0: 0}
        else:
            outs = states + (flow_out, solute_out)
            aliases = {0: 0, 1: 1, 2: 2, 3: 3}
        moved = call(
            functools.partial(inner_kernel, last),
            outs,
            [VMEM] * 8,
            [ghost],
            10**8,
            2 * 10**7,
            aliases=aliases,
            keep=True,
        )(*state, bits, opens, *y_halos)
        if step == 0:
            mask, bits, opens = call(
                edge_open_kernel,
                (held(PADROWS, L), bits_out, open_out),
                [SMEM] + [VMEM] * 5,
                [],
                10**6,
                10**6,
                aliases={3: 0, 4: 1, 5: 2},
                keep=True,
            )(flags, *z_halos, mask, bits, opens)
        if last:
            pops, flow, turned = moved
            pops, flow, turned, send = call(
                functools.partial(edge_kernel, True),
                (states[0], flow_out, held(BLOCKROWS, L), shape(8, 224, L)),
                [SMEM] + [VMEM] * 12,
                [ghost],
                10**7,
                10**7,
                aliases={1: 0, 5: 1, 6: 2},
                keep=True,
            )(block_slot, pops, *state[1:], flow, turned, bits, opens, *y_halos, *z_halos)
            break
        *state, flow, solute = moved
        *state, flow, ydn, yup = call(
            functools.partial(edge_kernel, False),
            states + (flow_out, message, message),
            [VMEM] * 12,
            [ghost],
            10**7,
            10**7,
            aliases={0: 0, 1: 1, 2: 2, 3: 3, 4: 4},
            keep=True,
        )(*state, flow, solute, bits, opens, *y_halos, *z_halos)
        zdn, zup = call(
            z_kernel, (message, message), [VMEM] * 5, [], 10**6, 10**6, keep=True
        )(*state, bits)

    recv = lax.all_to_all(send, "gz", split_axis=0, concat_axis=0, tiled=True)
    out = call(scatter_kernel, shape(BLOCKROWS, L), [SMEM, VMEM], [], 1, 2 * 10**6)(
        slot_block, recv
    )
    new_solute = out.reshape(7, 32, 8, L).transpose(0, 2, 1, 3).reshape(7, 8, 4096)
    return pops.reshape(19, B, B, L), new_solute


def solution(mesh):
    in_specs = (
        P(None, "gz", "gy", "gx"),
        P(None, ("gx", "gy", "gz"), None),
        P("gz", "gy", "gx"),
        P("gz", "gy", "gx"),
        P(("gx", "gy", "gz")),
    )
    out_specs = (P(None, "gz", "gy", "gx"), P(None, ("gx", "gy", "gz"), None))
    return jax.shard_map(shards, mesh=mesh, in_specs=in_specs, out_specs=out_specs, check_vma=False)
```

```python
import functools

import jax
import jax.numpy as jnp
from jax import lax
from jax.experimental import pallas as pl
from jax.experimental.pallas import tpu as pltpu
from jax.sharding import PartitionSpec as P

STEPS = 4
DIRS = [
    (0, 0, 0),
    (1, 0, 0),
    (-1, 0, 0),
    (0, 1, 0),
    (0, -1, 0),
    (0, 0, 1),
    (0, 0, -1),
    (1, 1, 0),
    (-1, -1, 0),
    (1, -1, 0),
    (-1, 1, 0),
    (1, 0, 1),
    (-1, 0, -1),
    (1, 0, -1),
    (-1, 0, 1),
    (0, 1, 1),
    (0, -1, -1),
    (0, 1, -1),
    (0, -1, 1),
]
OPP = [DIRS.index((-a, -b, -c)) for a, b, c in DIRS]
PAIRS = [(i, OPP[i]) for i in range(1, 19, 2)]
WEIGHTS = [1.0 / 3.0] + [1.0 / 18.0] * 6 + [1.0 / 36.0] * 12
OMEGA_FLOW = 1.2
FORCE_GAIN = 0.02
REST_CONC = 8.0
Y_UP = [i for i in range(19) if DIRS[i][1] == 1]
Y_DN = [i for i in range(19) if DIRS[i][1] == -1]
Z_UP = [i for i in range(19) if DIRS[i][2] == 1]
Z_DN = [i for i in range(19) if DIRS[i][2] == -1]
RHO, VEL, PART, NORM, TRANS, MASK = 5, 6, 9, 10, 11, 12
SIDES = 2
UNROLL = 2
B = 16
L = 128
W = 8
PLANE = 2 * B
ROWS = B * PLANE
PADDED = 64
PADROWS = (B + 2) * PADDED
BLOCKROWS = 7 * 32 * 8
F32 = jnp.float32
VMEM = pl.BlockSpec(memory_space=pltpu.VMEM)
SMEM = pl.BlockSpec(memory_space=pltpu.SMEM)
HBM = pl.BlockSpec(memory_space=pltpu.HBM)


def call(
    kernel, out_shape, in_specs, scratch, flops, nbytes, aliases={}, keep=False, out_specs=None
):
    run = pl.pallas_call(
        kernel,
        out_shape=out_shape,
        in_specs=in_specs,
        out_specs=out_specs or jax.tree.map(lambda _: VMEM, out_shape),
        scratch_shapes=scratch,
        input_output_aliases=aliases,
        compiler_params=pltpu.CompilerParams(vmem_limit_bytes=20 * 1024 * 1024),
        cost_estimate=pl.CostEstimate(flops=flops, bytes_accessed=nbytes, transcendentals=0),
    )

    def place(x, spec):
        if spec is HBM or (keep and spec is VMEM):
            return pltpu.with_memory_space_constraint(x, spec.memory_space)
        return x

    def placed(*args):
        return run(*map(place, args, in_specs))

    return placed


def shape(*dims):
    return jax.ShapeDtypeStruct(dims, F32)


def held(*dims, dtype=F32):
    return pltpu.VMEM(dims, dtype)


def stored(*dims, dtype=F32):
    return pltpu.HBM(dims, dtype)


def lanes(rows):
    return lax.broadcasted_iota(jnp.int32, (rows, L), 1)


def row_ids(rows):
    return lax.broadcasted_iota(jnp.int32, (rows, L), 0)


def ring(v, step):
    rolled = pltpu.roll(v, step % L, axis=1)
    other = jnp.concatenate([rolled[B:], rolled[:B]], axis=0)
    return jnp.where(lanes(PLANE) == (0 if step > 0 else L - 1), other, rolled)


def halves(main, side):
    return jnp.concatenate([main, side], axis=0)


def shift_rows(v, step, fill):
    rolled = pltpu.roll(v, step % PLANE, axis=0)
    return jnp.where(row_ids(PLANE) % B == (0 if step > 0 else B - 1), fill, rolled)


def is_open(bits, which):
    return (bits & (1 << which)) != 0


def along(which, vx, vy, vz):
    total = None
    for sign, part in zip(DIRS[which], (vx, vy, vz)):
        if sign != 0:
            if total is None:
                total = part if sign > 0 else -part
            else:
                total = total + part if sign > 0 else total - part
    return total


def moments(pops, porous):
    rho = pops[0]
    for which in range(1, 19):
        rho = rho + pops[which]
    scale = porous / rho
    parts = []
    for coord in range(3):
        plus = sum(pops[i] for i in range(19) if DIRS[i][coord] == 1)
        minus = sum(pops[i] for i in range(19) if DIRS[i][coord] == -1)
        parts.append((plus - minus) * scale)
    return rho, parts


def solute_collide(solute, velocity):
    conc = sum(solute)
    out = [-0.5 * solute[0] + 0.375 * conc]
    base = 0.1875 * conc
    for coord in range(3):
        turn = 0.75 * conc * velocity[coord]
        out.append((base - 0.5 * solute[1 + 2 * coord]) + turn)
        out.append((base - 0.5 * solute[2 + 2 * coord]) - turn)
    return out


def chosen(bits, moved, post, which):
    return jnp.where(
        is_open(bits, which),
        moved,
        jnp.where(is_open(bits, 0), post[OPP[which]], post[which]),
    )


def turn_blocks(x):
    row, lane = row_ids(8), lanes(8)
    x = take(x, (lane - B * row) & (L - 1), 1)
    x = take(x, (lane // B - row) & 7, 0)
    return take(x, (lane + B * row) & (L - 1), 1)


def take(x, index, axis):
    return jnp.take_along_axis(x, index, axis=axis, mode="promise_in_bounds")


def send_blocks(pick, blocks_ref, out_ref, hold_ref, sems):
    copies = []
    for dest in range(8):
        hold_ref[dest] = blocks_ref[pl.ds(pick(dest), BLOCKROWS // 8, stride=8), :]
        copies.append(pltpu.make_async_copy(hold_ref.at[dest], out_ref.at[dest], sems.at[dest]))
        copies[-1].start()
    return copies


def gather_kernel(slot_ref, state_ref, send_ref, blocks_ref, hold_ref, sems):
    def slot_for(dest):
        slot = jnp.int32(0)
        for s in range(8):
            home = slot_ref[s]
            slot = jnp.where((home >= 0) & (home // 8 == dest), s, slot)
        return slot

    load = pltpu.make_async_copy(state_ref, blocks_ref, sems.at[8])
    load.start()
    load.wait()
    for copy in send_blocks(slot_for, blocks_ref, send_ref, hold_ref, sems):
        copy.wait()


def spread_kernel(slot_ref, recv_ref, *refs):
    *refs, turn_ref, sems = refs
    sources, dense_ref, targets = refs[:6], refs[6], refs[7:]
    loads = [
        pltpu.make_async_copy(source, target, sems.at[k])
        for k, (source, target) in enumerate(zip(sources, targets))
    ]
    for load in loads:
        load.start()
    for tile in range(8):
        owner = jnp.maximum(slot_ref[0, 0, tile], 0) // 8
        turn_ref[pl.ds(tile, BLOCKROWS // 8, stride=8), :] = recv_ref[owner]

    def body(group, carry):
        for i in range(32):
            at = pl.multiple_of(group * 256 + i * 8, 8)
            dense_ref[pl.ds(at, 8), :] = turn_blocks(turn_ref[pl.ds(at, 8), :])
        return carry

    lax.fori_loop(0, BLOCKROWS // 256, body, 0)
    for load in loads:
        load.wait()


def pack_columns(load, low_ref, high_ref, at):
    lane = lanes(8) // W
    low = jnp.zeros((8, L), F32)
    high = jnp.zeros((8, L), F32)
    for i in range(16):
        x = load(i)
        low = jnp.where(lane == i, x if i == 0 else pltpu.roll(x, W * i, axis=1), low)
        turn = (W + W * i) % L
        high = jnp.where(lane == i, x if turn == 0 else pltpu.roll(x, turn, axis=1), high)
    at = pl.multiple_of(at, 8)
    low_ref[pl.ds(at, 8), :] = low
    high_ref[pl.ds(at, 8), :] = high


def columns_kernel(pops_ref, mask_ref, low_ref, high_ref):
    def rows(start, i):
        return pl.ds(pl.multiple_of(start + i * 8, 8), 8)

    def body(group, carry):
        at = (group % 2) * 128
        pack_columns(
            lambda i: pops_ref[group // 2, rows(at, i), :], low_ref, high_ref, group * 8
        )
        return carry

    lax.fori_loop(0, 38, body, 0, unroll=UNROLL)
    for group in range(2):
        pack_columns(
            lambda i: mask_ref[rows(group * 128, i), :].astype(F32),
            low_ref,
            high_ref,
            (38 + group) * 8,
        )


def unpack_columns(right, left, i):
    a = right if i == 0 else pltpu.roll(right, L - W * i, axis=1)
    b = left if i == 15 else pltpu.roll(left, L - W - W * i, axis=1)
    return jnp.where(lanes(8) < L // 2, a, b)


def ring_kernel(
    flag_ref, pops_ref, mask_ref, right_ref, left_ref,
    side_ref, ring_ref, aux_ref, mask_out, bits_ref,
):
    def body(group, carry):
        at = pl.ds(pl.multiple_of(group * 8, 8), 8)
        right, left = right_ref[at, :], left_ref[at, :]
        for i in range(16):
            row = pl.multiple_of((group % 2) * 128 + i * 8, 8)
            side_ref[group // 2, pl.ds(row, 8), :] = unpack_columns(right, left, i)
        return carry

    lax.fori_loop(0, 38, body, 0, unroll=UNROLL)
    lane = lanes(8)
    inside = jnp.where(lane < W, flag_ref[1], jnp.where(lane >= L - W, flag_ref[0], 0.0))
    for group in range(2):
        right, left = right_ref[pl.ds(304 + group * 8, 8), :], left_ref[pl.ds(304 + group * 8, 8), :]
        for i in range(16):
            z = group * 8 + i // 2
            row = z * PLANE + (i % 2) * 8
            ring_ref[pl.ds(row, 8), :] = mask_ref[pl.ds(group * 128 + i * 8, 8), :].astype(F32)
            ring_ref[pl.ds(row + B, 8), :] = unpack_columns(right, left, i) * inside
    mask_out[...] = jnp.zeros_like(mask_out)
    for z in range(B):
        put_rows(mask_out, z + 1, ring_ref[pl.ds(z * PLANE, PLANE), :])

    def flow(z, carry):
        set_bits(mask_out, bits_ref, z)
        pops = [flow_plane((pops_ref, side_ref), z, i) for i in range(19)]
        rho, velocity = moments(pops, plane(ring_ref, z))
        for k, v in enumerate([rho] + velocity):
            aux_ref[k, pl.ds(pl.multiple_of(z * PLANE, PLANE), PLANE), :] = v
        return carry

    lax.fori_loop(0, B, flow, 0, unroll=UNROLL)


def plane(ref, z, *lead):
    return ref[(*lead, pl.ds(pl.multiple_of(z * PLANE, PLANE), PLANE), slice(None))]


def put_face(ref, row, v, *lead):
    for tile in range(2):
        at = pl.ds(tile * B + row, B, stride=PLANE)
        ref[(*lead, at, slice(None))] = v[tile * B : (tile + 1) * B]


def flow_plane(refs, z, which):
    at = pl.ds(pl.multiple_of(z * B, B), B)
    return halves(refs[0][which, at, :], refs[1][which, at, :])


def flow_rows(refs, row, which):
    at = pl.ds(row, B, stride=B)
    return halves(refs[0][which, at, :], refs[1][which, at, :])


def padded_plane(ref, zz, shift, *lead):
    at = zz * PADDED + 8
    return halves(
        ref[(*lead, pl.ds(at - shift, B), slice(None))],
        ref[(*lead, pl.ds(at + 32 - shift, B), slice(None))],
    )


def put_rows(ref, zz, v):
    ref[pl.ds(zz * PADDED + 8, B), :] = v[:B]
    ref[pl.ds(zz * PADDED + 40, B), :] = v[B:]


def put_padded(ref, comp, zz, v):
    at = zz * PADDED + 8
    if not isinstance(zz, int):
        at = pl.multiple_of(at, 8)
    ref[comp, pl.ds(at, B), :] = v[:B]
    ref[comp, pl.ds(at + 32, B), :] = v[B:]


def face_rows(ref, row, *lead):
    return halves(
        ref[(*lead, pl.ds(row, B, stride=PLANE), slice(None))],
        ref[(*lead, pl.ds(B + row, B, stride=PLANE), slice(None))],
    )


def set_bits(mask_ref, bits_ref, z):
    here = padded_plane(mask_ref, z + 1, 0)
    bits = jnp.where(here > 0, 1, 0)
    for which in range(1, 19):
        cx, cy, cz = DIRS[which]
        source = padded_plane(mask_ref, z + 1 - cz, cy)
        if cx:
            source = ring(source, cx)
        bits = bits + jnp.where(source * here > 0, 1 << which, 0)
    bits_ref[pl.ds(pl.multiple_of(z * PLANE, PLANE), PLANE), :] = bits


def side_open_kernel(
    flag_ref, ylo_ref, yhi_ref, mask_in, bits_in, mask_ref, bits_ref, open_ref
):
    for side in range(2):
        halo = read_field((ylo_ref, yhi_ref)[side], MASK) * flag_ref[2 + side]
        edge, row = ((0, 7), (B - 1, 24))[side]
        own = []
        for tile in range(2):
            part = halo[tile * B : (tile + 1) * B]
            at = PADDED + tile * 32
            mask_ref[pl.ds(at + row, B, stride=PADDED), :] = part
            own.append(mask_ref[pl.ds(at + 8 + edge, B, stride=PADDED), :])
            put_open(open_ref, 0, side, tile, part * own[tile])
        own = halves(*own)
        bits = face_rows(bits_ref, edge)
        for which in (Y_UP, Y_DN)[side]:
            cx, _, cz = DIRS[which]
            source = halo
            if cz:
                source = pltpu.roll(source, cz % PLANE, axis=0)
            if cx:
                source = ring(source, cx)
            bits = bits + jnp.where(source * own > 0, 1 << which, 0)
        put_face(bits_ref, edge, bits)


def edge_open_kernel(
    flag_ref, zlo_ref, zhi_ref, mask_in, bits_in, open_in, mask_ref, bits_ref, open_ref
):
    row = row_ids(B)
    for side in range(2):
        z_ref, zz = (zlo_ref, zhi_ref)[side], (0, B + 1)[side]
        put_rows(mask_ref, zz, read_field(z_ref, MASK) * flag_ref[4 + side])
        for y_side in range(2):
            pair = read_diag(z_ref, y_side, MASK)
            for tile in range(2):
                at = zz * PADDED + tile * 32 + (7, 24)[y_side]
                scale = flag_ref[4 + side] * flag_ref[2 + y_side]
                mask_ref[pl.ds(at, 1), :] = pair[tile][:1] * scale

    def body(k, carry):
        set_bits(mask_ref, bits_ref, k * (B - 1))
        return carry

    lax.fori_loop(0, 2, body, 0)
    for tile in range(2):
        for side in range(2):
            edge = tile * 32 + (7, 24)[side]
            halo = mask_ref[pl.ds(PADDED + edge, B, stride=PADDED), :]
            first = mask_ref[pl.ds(edge, 1), :]
            last = mask_ref[pl.ds(PADROWS - PADDED + edge, 1), :]
            ends = jnp.where(row == 0, halo * first, jnp.where(row == B - 1, halo * last, 0.0))
            put_open(open_ref, 1, side, tile, ends)
            at = (0, B + 1)[side] * PADDED + tile * 32
            near = (1, B)[side]
            halo = mask_ref[pl.ds(at + 8, B), :]
            own = mask_ref[pl.ds(near * PADDED + tile * 32 + 8, B), :]
            first = mask_ref[pl.ds(at + 7, 1), :]
            last = mask_ref[pl.ds(at + 24, 1), :]
            ends = jnp.where(row == 0, halo * first, jnp.where(row == B - 1, halo * last, 0.0))
            put_open(open_ref, 2, side, tile, halo * own)
            put_open(open_ref, 3, side, tile, ends)


def open_at(kind, side, tile):
    return ((kind * 2 + side) * 2 + tile) * B


def put_open(ref, kind, side, tile, v):
    ref[pl.ds(open_at(kind, side, tile), B), :] = v


def get_open(ref, kind, side):
    return ref[pl.ds(open_at(kind, side, 0), PLANE), :] > 0


def write_message(out_ref, fields):
    lane = lanes(B) // 16
    for slab in range(SIDES):
        packed = jnp.zeros((B, L), F32)
        for k, field in enumerate(fields[slab * 8 : slab * 8 + 8]):
            turn = (W + 16 * k) % L
            packed = jnp.where(lane == k, pltpu.roll(field[B:], turn, axis=1), packed)
        out_ref[pl.ds(slab * B, B), :] = packed
    for f, field in enumerate(fields):
        out_ref[pl.ds((SIDES + f) * B, B), :] = field[:B]


def unpack_side(packed, f):
    return pltpu.roll(packed, L - W - 16 * (f % 8), axis=1)


def read_field(ref, f):
    side = ref[pl.ds(f // 8 * B, B), :]
    return halves(ref[pl.ds((SIDES + f) * B, B), :], unpack_side(side, f))


def read_row(ref, f, row):
    main = jnp.broadcast_to(ref[pl.ds((SIDES + f) * B + row, 1), :], (8, L))
    side = jnp.broadcast_to(ref[pl.ds(f // 8 * B + row, 1), :], (8, L))
    return main, unpack_side(side, f)


def read_diag(ref, side, f):
    slabs = ref.shape[0] // (B + 2)
    base = slabs * B + side * slabs
    main = jnp.broadcast_to(ref[pl.ds(base + SIDES + f, 1), :], (8, L))
    packed = jnp.broadcast_to(ref[pl.ds(base + f // 8, 1), :], (8, L))
    return main, unpack_side(packed, f)


def spread8(pair):
    return halves(
        jnp.concatenate([pair[0], pair[0]], axis=0), jnp.concatenate([pair[1], pair[1]], axis=0)
    )


def partial_sum(f, inner, is_open, outward, in_rows):
    row = row_ids(PLANE) % B
    total = f[0]
    total = total + jnp.where(is_open(1), ring(f[1], 1), f[2])
    total = total + jnp.where(is_open(2), ring(f[2], -1), f[1])
    up, down = in_rows
    moved = jnp.where(is_open(up), pltpu.roll(f[up], 1, axis=0), f[down])
    total = total + jnp.where(row == 0, 0.0, moved)
    moved = jnp.where(is_open(down), pltpu.roll(f[down], PLANE - 1, axis=0), f[up])
    total = total + jnp.where(row == B - 1, 0.0, moved)
    return total + jnp.where(is_open(outward), inner, f[OPP[outward]])


def open_bits(bits):
    return lambda which: is_open(bits, which)


def open_mask(own, inner, in_rows):
    shifted = {
        1: ring(own, 1),
        2: ring(own, -1),
        in_rows[0]: pltpu.roll(own, 1, axis=0),
        in_rows[1]: pltpu.roll(own, PLANE - 1, axis=0),
    }
    return lambda which: shifted.get(which, inner) > 0


def write_y_messages(pops_refs, post_ref, aux_ref, y_refs, bits_ref=None, ring_ref=None):
    row = row_ids(PLANE) % B
    for side in range(2):
        names = (Y_DN, Y_UP)[side]
        edge, inner = ((0, 1), (B - 1, B - 2))[side]
        normal = (4, 3)[side]
        if ring_ref is None:
            opened = open_bits(face_rows(bits_ref, edge))
        else:
            opened = open_mask(face_rows(ring_ref, edge), face_rows(ring_ref, inner), (5, 6))
        f = [face_rows(post_ref, edge, i) for i in range(7)]
        part = partial_sum(f, face_rows(post_ref, inner, normal), opened, normal, (5, 6))
        fields = [flow_rows(pops_refs, edge, c) for c in names]
        fields += [face_rows(aux_ref, edge, k) for k in range(4)]
        fields += [part, f[normal], jnp.where(row == 0, f[6], f[5])]
        if ring_ref is not None:
            fields.append(face_rows(ring_ref, edge))
        write_message(y_refs[side], fields)


def write_z_messages(pops_refs, post_ref, aux_ref, z_refs, bits_ref=None, ring_ref=None):
    row = row_ids(PLANE) % B
    for side in range(2):
        names = (Z_DN, Z_UP)[side]
        edge, inner = ((0, 1), (B - 1, B - 2))[side]
        normal = (6, 5)[side]
        if ring_ref is None:
            opened = open_bits(plane(bits_ref, edge))
        else:
            opened = open_mask(plane(ring_ref, edge), plane(ring_ref, inner), (3, 4))
        f = [plane(post_ref, edge, i) for i in range(7)]
        part = partial_sum(f, plane(post_ref, inner, normal), opened, normal, (3, 4))
        fields = [flow_plane(pops_refs, edge, c) for c in names]
        fields += [plane(aux_ref, edge, k) for k in range(4)]
        fields += [part, f[normal], jnp.where(row == 0, f[4], f[3])]
        if ring_ref is not None:
            fields.append(plane(ring_ref, edge))
        write_message(z_refs[side], fields)


def relax(f, which, rho, vx, vy, vz, base):
    a = along(which, vx, vy, vz)
    scale = (OMEGA_FLOW * WEIGHTS[which]) * rho
    return (1.0 - OMEGA_FLOW) * f + scale * (base + a * (3.0 + 4.5 * a))


def lifted(conc, vx, vy, vz):
    vz = vz + FORCE_GAIN * (conc - REST_CONC)
    return vz, 1.0 - 1.5 * (vx * vx + vy * vy + vz * vz)


def stream_solute(z, post_ref, bits, fills, below, above):
    post = [plane(post_ref, z, i) for i in range(7)]
    moved = [
        None,
        ring(post[1], 1),
        ring(post[2], -1),
        shift_rows(post[3], 1, fills[0]),
        shift_rows(post[4], -1, fills[1]),
        below,
        above,
    ]
    return [post[0]] + [chosen(bits, moved[i], post, i) for i in range(1, 7)]


def collide_face(msg, names, conc, put):
    rho, vx, vy, vz = (read_field(msg, k) for k in range(RHO, RHO + 4))
    vz, base = lifted(conc, vx, vy, vz)
    for k, which in enumerate(names):
        put(which, relax(read_field(msg, k), which, rho, vx, vy, vz, base))


def collide_y_halos(post_ref, open_ref, y_refs, z_refs, flow_ref):
    row = row_ids(PLANE) % B
    for side in range(2):
        msg = y_refs[side]
        own = face_rows(post_ref, (0, B - 1)[side], (4, 3)[side])
        conc = read_field(msg, PART)
        conc = conc + jnp.where(get_open(open_ref, 0, side), own, read_field(msg, NORM))
        if z_refs is not None:
            ends = jnp.where(
                row == 0,
                spread8(read_diag(z_refs[0], side, TRANS)),
                spread8(read_diag(z_refs[1], side, TRANS)),
            )
            ends = jnp.where(get_open(open_ref, 1, side), ends, read_field(msg, TRANS))
            conc = conc + ends
        at = PADDED + (7, 24)[side]

        def put(which, v):
            for tile in range(2):
                part = v[tile * B : (tile + 1) * B]
                if z_refs is None:
                    flow_ref[which, pl.ds(at + tile * 32, B, stride=PADDED), :] = part
                else:
                    for z in (0, B - 1):
                        flow_ref[which, pl.ds(at + tile * 32 + z * PADDED, 1), :] = part[z : z + 1]

        collide_face(msg, (Y_UP, Y_DN)[side], conc, put)


def collide_z_halos(post_ref, open_ref, y_refs, z_refs, flow_ref):
    row = row_ids(PLANE) % B
    for side in range(2):
        msg = z_refs[side]
        own = plane(post_ref, (0, B - 1)[side], (6, 5)[side])
        ends = jnp.where(
            row == 0, spread8(read_diag(msg, 0, NORM)), spread8(read_diag(msg, 1, NORM))
        )
        ends = jnp.where(get_open(open_ref, 3, side), ends, read_field(msg, TRANS))
        conc = read_field(msg, PART)
        conc = conc + jnp.where(get_open(open_ref, 2, side), own, read_field(msg, NORM))
        conc = conc + jnp.where((row == 0) | (row == B - 1), ends, 0.0)
        zz = (0, B + 1)[side]
        collide_face(
            msg, (Z_UP, Z_DN)[side], conc, lambda which, v: put_padded(flow_ref, which, zz, v)
        )
    for y_side in range(2):
        for z_side in range(2):
            which = DIRS.index((0, 1 - 2 * y_side, 1 - 2 * z_side))
            names = (Y_UP, Y_DN)[y_side]
            msg = z_refs[z_side]
            z_row = (0, B - 1)[z_side]
            y_row = (0, B - 1)[y_side]
            from_y = read_row(y_refs[y_side], TRANS, z_row)
            from_z = read_row(msg, TRANS, y_row)
            get = [read_diag(msg, y_side, f) for f in range(TRANS + 1)]
            for tile in range(2):
                open_y = open_ref[pl.ds(open_at(1, y_side, tile) + z_row, 1), :]
                open_z = open_ref[pl.ds(open_at(3, z_side, tile) + y_row, 1), :]
                conc = get[PART][tile]
                conc = conc + jnp.where(open_y > 0, from_y[tile], get[TRANS][tile])
                conc = conc + jnp.where(open_z > 0, from_z[tile], get[NORM][tile])
                rho, vx, vy, vz = (get[k][tile] for k in range(RHO, RHO + 4))
                vz, base = lifted(conc, vx, vy, vz)
                v = relax(get[names.index(which)][tile], which, rho, vx, vy, vz, base)
                at = (0, B + 1)[z_side] * PADDED + tile * 32 + (7, 24)[y_side]
                flow_ref[which, pl.ds(at, 1), :] = v[:1]


def collide_flow(load, rho, vx, vy, vz, bits, conc, put):
    porous = is_open(bits, 0)
    vz = vz + jnp.where(porous, FORCE_GAIN * (conc - REST_CONC), 0.0)
    base = 1.0 - 1.5 * (vx * vx + vy * vy + vz * vz)
    keep = 1.0 - OMEGA_FLOW
    scaled = OMEGA_FLOW * rho
    f = load(0)
    put(0, jnp.where(porous, keep * f + (WEIGHTS[0] * scaled) * base, f))
    for i, j in PAIRS:
        a = along(i, vx, vy, vz)
        scale = WEIGHTS[i] * scaled
        even = scale * (base + 4.5 * (a * a))
        odd = scale * (3.0 * a)
        f, g = load(i), load(j)
        put(i, jnp.where(porous, keep * f + (even + odd), g))
        put(j, jnp.where(porous, keep * g + (even - odd), f))


def stream_flow(z, bits, flow_ref):
    post = [padded_plane(flow_ref, z + 1, 0, i) for i in range(19)]
    out = [post[0]]
    for which in range(1, 19):
        cx, cy, cz = DIRS[which]
        moved = post[which]
        if cy or cz:
            moved = padded_plane(flow_ref, z + 1 - cz, cy, which)
        if cx:
            moved = ring(moved, cx)
        out.append(jnp.where(is_open(bits, which), moved, post[OPP[which]]))
    return out


def first_kernel(
    dense_ref, right_ref, left_ref, pops_ref, side_ref, aux_ref, ring_ref,
    post_ref, ydn_ref, yup_ref, turn_ref,
):
    turn_ref[pl.ds(0, BLOCKROWS // 8, stride=8), :] = right_ref[...]
    turn_ref[pl.ds(7, BLOCKROWS // 8, stride=8), :] = left_ref[...]
    lane = lanes(8)
    near = (lane < W) | (lane >= L - W)

    def body(z, carry):
        solute = []
        for i in range(7):
            at = pl.multiple_of(i * 256 + z * B, B)
            side = [
                jnp.where(near, turn_blocks(turn_ref[pl.ds(at + 8 * k, 8), :]), 0.0)
                for k in range(2)
            ]
            solute.append(jnp.concatenate([dense_ref[pl.ds(at, B), :]] + side, axis=0))
        post = solute_collide(solute, [plane(aux_ref, z, k) for k in range(1, 4)])
        for i in range(7):
            post_ref[i, pl.ds(pl.multiple_of(z * PLANE, PLANE), PLANE), :] = post[i]
        return carry

    lax.fori_loop(0, B, body, 0, unroll=UNROLL)
    pops_refs = pops_ref, side_ref
    write_y_messages(pops_refs, post_ref, aux_ref, (ydn_ref, yup_ref), ring_ref=ring_ref)


def pull(z, refs, bits_ref, flow_ref, solute_ref):
    pops_ref, side_ref, post_ref, aux_ref = refs
    at = pl.ds(pl.multiple_of(z * PLANE, PLANE), PLANE)
    main = pl.ds(pl.multiple_of(z * B, B), B)
    bits = bits_ref[at, :]
    pops = stream_flow(z, bits, flow_ref)
    for i in range(19):
        pops_ref[i, main, :] = pops[i][:B]
        if side_ref is not None:
            side_ref[i, main, :] = pops[i][B:]
    if side_ref is None:
        return
    rho, velocity = moments(pops, jnp.where(is_open(bits, 0), 1.0, 0.0))
    for k, v in enumerate([rho] + velocity):
        aux_ref[k, at, :] = v
    post = solute_collide([solute_ref[i, at, :] for i in range(7)], velocity)
    for i in range(7):
        post_ref[i, at, :] = post[i]


def push(z, pops_refs, aux_ref, bits, solute, flow_ref):
    rho, vx, vy, vz = (plane(aux_ref, z, k) for k in range(4))
    collide_flow(
        lambda i: flow_plane(pops_refs, z, i), rho, vx, vy, vz, bits, sum(solute),
        lambda i, v: put_padded(flow_ref, i, z + 1, v),
    )


def put_solute(solute_ref, z, solute):
    for i in range(7):
        solute_ref[i, pl.ds(pl.multiple_of(z * PLANE, PLANE), PLANE), :] = solute[i]


def turn_plane(turn_ref, z, solute):
    for i in range(7):
        for half in range(2):
            at = pl.multiple_of(i * 256 + z * B + half * 8, 8)
            turn_ref[pl.ds(at, 8), :] = turn_blocks(solute[i][half * 8 : half * 8 + 8])


def core_kernel(first, *refs):
    pops_ref, side_ref, post_ref, aux_ref, bits_ref = refs[:5]
    ring_ref, refs = (refs[5], refs[6:]) if first else (None, refs[5:])
    zdn_ref, zup_ref, flow_ref, solute_ref = refs
    write_z_messages(
        (pops_ref, side_ref), post_ref, aux_ref, (zdn_ref, zup_ref), bits_ref, ring_ref
    )
    fills = [jnp.zeros((PLANE, L), F32)] * 2

    def body(z, carry):
        bits = plane(bits_ref, z)
        solute = stream_solute(
            z, post_ref, bits, fills, plane(post_ref, z - 1, 5), plane(post_ref, z + 1, 6)
        )
        put_solute(solute_ref, z, solute)
        push(z, (pops_ref, side_ref), aux_ref, bits, solute, flow_ref)
        return carry

    lax.fori_loop(1, B - 1, body, 0, unroll=UNROLL)


def fix_rows(pops_refs, post_ref, aux_ref, bits_ref, y_refs, flow_ref, solute_ref):
    for side in range(2):
        edge = (0, B - 1)[side]
        which = (3, 4)[side]
        bits = face_rows(bits_ref, edge)
        post = {i: face_rows(post_ref, edge, i) for i in (3, 4)}
        new = chosen(bits, read_field(y_refs[side], NORM), post, which)
        conc = new + sum(face_rows(solute_ref, edge, i) for i in range(7) if i != which)
        put_face(solute_ref, edge, new, which)

        def put(i, v):
            for tile in range(2):
                at = PADDED + tile * 32 + 8 + edge
                flow_ref[i, pl.ds(at, B, stride=PADDED), :] = v[tile * B : (tile + 1) * B]

        rho, vx, vy, vz = (face_rows(aux_ref, edge, k) for k in range(4))
        collide_flow(
            lambda i: flow_rows(pops_refs, edge, i), rho, vx, vy, vz, bits, conc, put
        )


def inner_kernel(last, *refs):
    pops_in, side_in, post_in, aux_in, flow_in, solute_in, bits_ref, open_ref = refs[:8]
    y_refs = refs[8:10]
    if last:
        pops_ref, flow_ref, solute_ref, turn_ref = refs[10:]
        state, out = (pops_ref, side_in, post_in, aux_in), (pops_ref, None, None, None)
    else:
        *state, flow_ref, solute_ref = refs[10:]
        out = state
    pops_ref, side_ref, post_ref, aux_ref = state
    fix_rows((pops_ref, side_ref), post_ref, aux_ref, bits_ref, y_refs, flow_ref, solute_ref)
    collide_y_halos(post_ref, open_ref, y_refs, None, flow_ref)

    def turn(z, carry):
        turn_plane(turn_ref, z, [plane(solute_ref, z, i) for i in range(7)])
        return carry

    def body(z, carry):
        pull(z, out, bits_ref, flow_ref, solute_ref)
        return carry

    if last:
        lax.fori_loop(1, B - 1, turn, 0, unroll=UNROLL)
    lax.fori_loop(2, B - 2, body, 0, unroll=UNROLL)


def edge_kernel(last, *refs):
    if last:
        slot_ref, refs = refs[0], refs[1:]
    pops_in, side_in, post_in, aux_in, flow_in, solute_in, bits_ref, open_ref = refs[:8]
    y_refs, z_refs = refs[8:10], refs[10:12]
    if last:
        pops_ref, flow_ref, turn_ref, send_ref, hold_ref, sems = refs[12:]
        state, out = (pops_ref, side_in, post_in, aux_in), (pops_ref, None, None, None)
        solute_ref = None
    else:
        *state, flow_ref, solute_ref, ydn_ref, yup_ref = refs[12:]
        out = state
    pops_ref, side_ref, post_ref, aux_ref = state
    solutes = []
    for z in (0, B - 1):
        bits = plane(bits_ref, z)
        fills = [spread8(read_row(y_refs[side], NORM, z)) for side in range(2)]
        below = read_field(z_refs[0], NORM) if z == 0 else plane(post_ref, z - 1, 5)
        above = read_field(z_refs[1], NORM) if z == B - 1 else plane(post_ref, z + 1, 6)
        solutes.append(stream_solute(z, post_ref, bits, fills, below, above))
        if last:
            turn_plane(turn_ref, z, solutes[-1])
        else:
            put_solute(solute_ref, z, solutes[-1])
    if last:

        def tile_for(owner):
            tile = jnp.int32(0)
            for j in range(8):
                slot = slot_ref[0, 0, j]
                tile = jnp.where((slot >= 0) & (slot // 8 == owner), j, tile)
            return tile

        copies = send_blocks(tile_for, turn_ref, send_ref, hold_ref, sems)
    collide_y_halos(post_ref, open_ref, y_refs, z_refs, flow_ref)
    collide_z_halos(post_ref, open_ref, y_refs, z_refs, flow_ref)
    for z, solute in zip((0, B - 1), solutes):
        push(z, (pops_ref, side_ref), aux_ref, plane(bits_ref, z), solute, flow_ref)

    for z in (0, 1, B - 2, B - 1):
        pull(z, out, bits_ref, flow_ref, solute_ref)
    if last:
        for copy in copies:
            copy.wait()
    else:
        write_y_messages(
            (pops_ref, side_ref), post_ref, aux_ref, (ydn_ref, yup_ref), bits_ref=bits_ref
        )


def scatter_kernel(slot_ref, recv_ref, out_ref):
    for s in range(8):
        home = slot_ref[s]
        block = recv_ref[jnp.maximum(home, 0) // 8]
        out_ref[pl.ds(s, BLOCKROWS // 8, stride=8), :] = jnp.where(home >= 0, block, 0.0)


def neighbours(low, high, axis):
    count = lax.axis_size(axis)
    up = [(i, (i + 1) % count) for i in range(count)]
    down = [(i, (i - 1) % count) for i in range(count)]
    return lax.ppermute(high, axis, up), lax.ppermute(low, axis, down)


def inside():
    flags = []
    for axis in ("gx", "gy", "gz"):
        at = lax.axis_index(axis)
        flags += [at > 0, at < lax.axis_size(axis) - 1]
    return jnp.stack(flags).astype(F32)


def with_edges(face, halos, row):
    slabs = face.shape[0] // B
    rows = [face] + [halo.reshape(slabs, B, L)[:, row] for halo in halos]
    pad = -slabs * (B + 2) % 8
    return jnp.concatenate(rows + [jnp.zeros((pad, L), F32)], axis=0)


def exchange_z(halos, zdn, zup):
    return neighbours(with_edges(zdn, halos, 0), with_edges(zup, halos, B - 1), "gz")


def shards(populations, solute_state, pore_mask, block_slot, slot_block):
    flags = inside()
    hold = [pltpu.VMEM((8, BLOCKROWS // 8, L), F32), pltpu.SemaphoreType.DMA((9,))]
    turn = pltpu.VMEM((BLOCKROWS, L), F32)
    send_out = pltpu.HBM((8, BLOCKROWS // 8, L), F32)
    state = solute_state.reshape(7, 8, 32, L).transpose(0, 2, 1, 3).reshape(BLOCKROWS, L)
    send = call(
        gather_kernel, send_out, [SMEM, HBM], [turn] + hold, 1, 2 * 10**6, out_specs=HBM
    )(slot_block, state)
    recv = lax.all_to_all(send, "gz", split_axis=0, concat_axis=0, tiled=True)

    pops = populations.reshape(19, 256, L)
    mask = pore_mask.reshape(256, L)
    low, high = call(columns_kernel, (stored(320, L),) * 2, [VMEM] * 2, [], 1, 1)(pops, mask)
    left, right = neighbours(low, high, "gx")
    dims = ((19, 256, L), (ROWS, L), (4, ROWS, L), (PADROWS, L), (ROWS, L))
    kinds = (F32,) * 4 + (jnp.int32,)
    side, ring_mask, aux, mask, bits = call(
        ring_kernel,
        tuple(stored(*d, dtype=k) for d, k in zip(dims, kinds)),
        [SMEM] + [VMEM] * 4,
        [],
        1,
        1,
    )(flags, pops, mask, right, left)

    after = jnp.minimum(bits[0, 0], 0)

    def block_of(tile):
        owner = jnp.maximum(block_slot[0, 0, tile], 0) // 8 + after
        return lax.dynamic_index_in_dim(recv, owner, 0, keepdims=False)

    left, right = neighbours(block_of(0), block_of(7), "gx")
    state = (pops, side, ring_mask, aux, mask, bits)
    dense, pops, side, ring_mask, aux, mask, bits = call(
        spread_kernel,
        (held(BLOCKROWS, L), held(19, 256, L))
        + tuple(held(*d, dtype=k) for d, k in zip(dims, kinds)),
        [SMEM, VMEM] + [HBM] * 6,
        [turn, pltpu.SemaphoreType.DMA((6,))],
        10**7,
        2 * 10**6,
    )(block_slot, recv, *state)
    message = held((SIDES + MASK + 1) * B, L)
    post, ydn, yup = call(
        first_kernel,
        (held(7, ROWS, L),) + (message,) * 2,
        [VMEM] * 7,
        [turn],
        10**7,
        10**7,
        keep=True,
    )(dense, right, left, pops, side, aux, ring_mask)

    states = (held(19, 256, L), held(19, 256, L), held(7, ROWS, L), held(4, ROWS, L))
    works = (held(19, PADROWS, L), held(7, ROWS, L))
    opens_out = (held(PADROWS, L), held(ROWS, L, dtype=jnp.int32), held(PLANE * 8, L))
    message = held((SIDES + MASK) * B, L)
    state = (pops, side, post, aux)
    for step in range(STEPS):
        last = step == STEPS - 1
        y_halos = neighbours(ydn, yup, "gy")
        zdn, zup, *work = call(
            functools.partial(core_kernel, step == 0),
            (held(*ydn.shape),) * 2 + works,
            [VMEM] * (6 if step == 0 else 5),
            [],
            10**7,
            10**7,
            keep=True,
        )(*state, bits, *([ring_mask] if step == 0 else []))
        z_halos = exchange_z(y_halos, zdn, zup)
        if step == 0:
            mask, bits, opens = call(
                side_open_kernel,
                opens_out,
                [SMEM] + [VMEM] * 4,
                [],
                10**6,
                10**6,
                aliases={3: 0, 4: 1},
                keep=True,
            )(flags, *y_halos, mask, bits)
        outs = states[:1] + works + (held(BLOCKROWS, L),) if last else states + works
        moved = call(
            functools.partial(inner_kernel, last),
            outs,
            [VMEM] * 10,
            [],
            10**7,
            10**7,
            aliases={0: 0, 4: 1, 5: 2} if last else {i: i for i in range(6)},
            keep=True,
        )(*state, *work, bits, opens, *y_halos)
        if step == 0:
            mask, bits, opens = call(
                edge_open_kernel,
                opens_out,
                [SMEM] + [VMEM] * 5,
                [],
                10**6,
                10**6,
                aliases={3: 0, 4: 1, 5: 2},
                keep=True,
            )(flags, *z_halos, mask, bits, opens)
        if last:
            pops, flow, _, turned = moved
            pops, _, _, send = call(
                functools.partial(edge_kernel, True),
                (states[0], works[0], held(BLOCKROWS, L), send_out),
                [SMEM] + [VMEM] * 12,
                hold,
                10**7,
                10**7,
                aliases={1: 0, 5: 1, 6: 2},
                keep=True,
                out_specs=(VMEM, VMEM, VMEM, HBM),
            )(block_slot, pops, *state[1:], flow, turned, bits, opens, *y_halos, *z_halos)
            break
        *state, _, _, ydn, yup = call(
            functools.partial(edge_kernel, False),
            states + works + (message, message),
            [VMEM] * 12,
            [],
            10**7,
            10**7,
            aliases={i: i for i in range(6)},
            keep=True,
        )(*moved, bits, opens, *y_halos, *z_halos)

    recv = lax.all_to_all(send, "gz", split_axis=0, concat_axis=0, tiled=True)
    out = call(scatter_kernel, shape(BLOCKROWS, L), [SMEM, VMEM], [], 1, 2 * 10**6)(
        slot_block, recv
    )
    new_solute = out.reshape(7, 32, 8, L).transpose(0, 2, 1, 3).reshape(7, 8, 4096)
    return pops.reshape(19, B, B, L), new_solute


def solution(mesh):
    in_specs = (
        P(None, "gz", "gy", "gx"),
        P(None, ("gx", "gy", "gz"), None),
        P("gz", "gy", "gx"),
        P("gz", "gy", "gx"),
        P(("gx", "gy", "gz")),
    )
    out_specs = (P(None, "gz", "gy", "gx"), P(None, ("gx", "gy", "gz"), None))
    return jax.shard_map(shards, mesh=mesh, in_specs=in_specs, out_specs=out_specs, check_vma=False)
```

```python
import functools

import jax
import jax.numpy as jnp
from jax import lax
from jax.experimental import pallas as pl
from jax.experimental.pallas import tpu as pltpu
from jax.sharding import PartitionSpec as P

STEPS = 4
DIRS = [
    (0, 0, 0),
    (1, 0, 0),
    (-1, 0, 0),
    (0, 1, 0),
    (0, -1, 0),
    (0, 0, 1),
    (0, 0, -1),
    (1, 1, 0),
    (-1, -1, 0),
    (1, -1, 0),
    (-1, 1, 0),
    (1, 0, 1),
    (-1, 0, -1),
    (1, 0, -1),
    (-1, 0, 1),
    (0, 1, 1),
    (0, -1, -1),
    (0, 1, -1),
    (0, -1, 1),
]
OPP = [DIRS.index((-a, -b, -c)) for a, b, c in DIRS]
PAIRS = [(i, OPP[i]) for i in range(1, 19, 2)]
WEIGHTS = [1.0 / 3.0] + [1.0 / 18.0] * 6 + [1.0 / 36.0] * 12
OMEGA_FLOW = 1.2
FORCE_GAIN = 0.02
REST_CONC = 8.0
Y_UP = [i for i in range(19) if DIRS[i][1] == 1]
Y_DN = [i for i in range(19) if DIRS[i][1] == -1]
Z_UP = [i for i in range(19) if DIRS[i][2] == 1]
Z_DN = [i for i in range(19) if DIRS[i][2] == -1]
RHO, VEL, PART, NORM, TRANS, MASK = 5, 6, 9, 10, 11, 12
SIDES = 2
UNROLL = 2
B = 16
L = 128
W = 8
PLANE = 2 * B
ROWS = B * PLANE
PADDED = 64
PADROWS = (B + 2) * PADDED
ROW = 7 * 32
HALF = ROW // 2
BLOCKROWS = ROW * 8
F32 = jnp.float32
VMEM = pl.BlockSpec(memory_space=pltpu.VMEM)
SMEM = pl.BlockSpec(memory_space=pltpu.SMEM)
HBM = pl.BlockSpec(memory_space=pltpu.HBM)


def call(
    kernel, out_shape, in_specs, scratch, flops, nbytes, aliases={}, keep=False, out_specs=None
):
    run = pl.pallas_call(
        kernel,
        out_shape=out_shape,
        in_specs=in_specs,
        out_specs=out_specs or jax.tree.map(lambda _: VMEM, out_shape),
        scratch_shapes=scratch,
        input_output_aliases=aliases,
        compiler_params=pltpu.CompilerParams(vmem_limit_bytes=20 * 1024 * 1024),
        cost_estimate=pl.CostEstimate(flops=flops, bytes_accessed=nbytes, transcendentals=0),
    )

    def place(x, spec):
        if spec is HBM or (keep and spec is VMEM):
            return pltpu.with_memory_space_constraint(x, spec.memory_space)
        return x

    def placed(*args):
        return run(*map(place, args, in_specs))

    return placed


def shape(*dims):
    return jax.ShapeDtypeStruct(dims, F32)


def held(*dims, dtype=F32):
    return pltpu.VMEM(dims, dtype)


def lanes(rows):
    return lax.broadcasted_iota(jnp.int32, (rows, L), 1)


def row_ids(rows):
    return lax.broadcasted_iota(jnp.int32, (rows, L), 0)


def ring(v, step):
    rolled = pltpu.roll(v, step % L, axis=1)
    other = jnp.concatenate([rolled[B:], rolled[:B]], axis=0)
    return jnp.where(lanes(PLANE) == (0 if step > 0 else L - 1), other, rolled)


def halves(main, side):
    return jnp.concatenate([main, side], axis=0)


def shift_rows(v, step, fill):
    rolled = pltpu.roll(v, step % PLANE, axis=0)
    return jnp.where(row_ids(PLANE) % B == (0 if step > 0 else B - 1), fill, rolled)


def is_open(bits, which):
    return (bits & (1 << which)) != 0


def along(which, vx, vy, vz):
    total = None
    for sign, part in zip(DIRS[which], (vx, vy, vz)):
        if sign != 0:
            if total is None:
                total = part if sign > 0 else -part
            else:
                total = total + part if sign > 0 else total - part
    return total


def moments(pops, porous):
    rho = pops[0]
    for which in range(1, 19):
        rho = rho + pops[which]
    scale = porous / rho
    parts = []
    for coord in range(3):
        plus = sum(pops[i] for i in range(19) if DIRS[i][coord] == 1)
        minus = sum(pops[i] for i in range(19) if DIRS[i][coord] == -1)
        parts.append((plus - minus) * scale)
    return rho, parts


def solute_collide(solute, velocity):
    conc = sum(solute)
    out = [-0.5 * solute[0] + 0.375 * conc]
    base = 0.1875 * conc
    for coord in range(3):
        turn = 0.75 * conc * velocity[coord]
        out.append((base - 0.5 * solute[1 + 2 * coord]) + turn)
        out.append((base - 0.5 * solute[2 + 2 * coord]) - turn)
    return out


def chosen(bits, moved, post, which):
    return jnp.where(
        is_open(bits, which),
        moved,
        jnp.where(is_open(bits, 0), post[OPP[which]], post[which]),
    )


def turn_blocks(x):
    row, lane = row_ids(8), lanes(8)
    x = take(x, (lane - B * row) & (L - 1), 1)
    x = take(x, (lane // B - row) & 7, 0)
    return take(x, (lane + B * row) & (L - 1), 1)


def take(x, index, axis):
    return jnp.take_along_axis(x, index, axis=axis, mode="promise_in_bounds")


PARTS = (
    (0, 0, 0, ROW, 0),
    (7, 1, 0, ROW, 0),
    (1, 2, 0, ROW, 0),
    (6, 3, 0, ROW, 0),
    (2, 4, 0, ROW, 0),
    (5, 5, 0, ROW, 0),
    (3, 6, 0, ROW, 0),
    (4, 5, ROW, HALF, 0),
    (4, 6, ROW, HALF, HALF),
)


def find(slots, home):
    found = jnp.int32(-1)
    for k, slot in enumerate(slots):
        found = jnp.where((slot >= 0) & (slot // 8 == home), k, found)
    return found


def fill_messages(me, slots, blocks_ref, outs):
    own, up1, down1, up2, down2, up3, down3 = outs
    for off, ref in ((0, own), (1, up1), (7, down1), (2, up2), (6, down2), (3, up3), (5, down3)):
        at = jnp.maximum(find(slots, (me + off) & 7), 0)
        ref[pl.ds(0, ROW), :] = blocks_ref[pl.ds(at, ROW, stride=8), :]
    at = jnp.maximum(find(slots, (me + 4) & 7), 0)
    up1[pl.ds(ROW, HALF), :] = blocks_ref[pl.ds(at, HALF, stride=8), :]
    down1[pl.ds(ROW, HALF), :] = blocks_ref[pl.ds(HALF * 8 + at, HALF, stride=8), :]


def receive(me, slots, refs, out_ref):
    for k, slot in enumerate(slots):

        @pl.when(slot < 0)
        def _():
            out_ref[pl.ds(k, ROW, stride=8), :] = jnp.zeros((ROW, L), F32)

    for off, k, at, count, first in PARTS:
        slot = find(slots, (me + off) & 7)

        @pl.when(slot >= 0)
        def _():
            out_ref[pl.ds(first * 8 + slot, count, stride=8), :] = refs[k][pl.ds(at, count), :]


def gather_kernel(me_ref, slot_ref, state_ref, *refs):
    *outs, blocks_ref, sem = refs
    load = pltpu.make_async_copy(state_ref, blocks_ref, sem)
    load.start()
    load.wait()
    fill_messages(me_ref[0], [slot_ref[s] for s in range(8)], blocks_ref, outs)


def pick_kernel(me_ref, slot_ref, *refs):
    for tile, out_ref in ((0, refs[-2]), (7, refs[-1])):
        slot = slot_ref[0, 0, tile]

        @pl.when(slot < 0)
        def _():
            out_ref[...] = jnp.zeros((ROW, L), F32)

        for off, k, at, count, first in PARTS:

            @pl.when((slot >= 0) & (slot // 8 == ((me_ref[0] + off) & 7)))
            def _():
                out_ref[pl.ds(first, count), :] = refs[k][pl.ds(at, count), :]


def spread_kernel(me_ref, slot_ref, *refs):
    *blocks, dense_ref, turn_ref = refs
    receive(me_ref[0], [slot_ref[0, 0, tile] for tile in range(8)], blocks, turn_ref)

    def body(group, carry):
        for i in range(32):
            at = pl.multiple_of(group * 256 + i * 8, 8)
            dense_ref[pl.ds(at, 8), :] = turn_blocks(turn_ref[pl.ds(at, 8), :])
        return carry

    lax.fori_loop(0, BLOCKROWS // 256, body, 0)


def pack_columns(load, low_ref, high_ref, at):
    lane = lanes(8) // W
    low = jnp.zeros((8, L), F32)
    high = jnp.zeros((8, L), F32)
    for i in range(16):
        x = load(i)
        low = jnp.where(lane == i, x if i == 0 else pltpu.roll(x, W * i, axis=1), low)
        turn = (W + W * i) % L
        high = jnp.where(lane == i, x if turn == 0 else pltpu.roll(x, turn, axis=1), high)
    at = pl.multiple_of(at, 8)
    low_ref[pl.ds(at, 8), :] = low
    high_ref[pl.ds(at, 8), :] = high


def columns_kernel(pops_ref, mask_ref, low_ref, high_ref):
    def rows(start, i):
        return pl.ds(pl.multiple_of(start + i * 8, 8), 8)

    def body(group, carry):
        at = (group % 2) * 128
        pack_columns(
            lambda i: pops_ref[group // 2, rows(at, i), :], low_ref, high_ref, group * 8
        )
        return carry

    lax.fori_loop(0, 38, body, 0, unroll=UNROLL)
    for group in range(2):
        pack_columns(
            lambda i: mask_ref[rows(group * 128, i), :].astype(F32),
            low_ref,
            high_ref,
            (38 + group) * 8,
        )


def unpack_columns(right, left, i):
    a = right if i == 0 else pltpu.roll(right, L - W * i, axis=1)
    b = left if i == 15 else pltpu.roll(left, L - W - W * i, axis=1)
    return jnp.where(lanes(8) < L // 2, a, b)


def ring_kernel(
    flag_ref, pops_in, mask_ref, right_ref, left_ref,
    pops_ref, side_ref, ring_ref, aux_ref, mask_out, bits_ref, sem,
):
    load = pltpu.make_async_copy(pops_in, pops_ref, sem)
    load.start()

    def body(group, carry):
        at = pl.ds(pl.multiple_of(group * 8, 8), 8)
        right, left = right_ref[at, :], left_ref[at, :]
        for i in range(16):
            row = pl.multiple_of((group % 2) * 128 + i * 8, 8)
            side_ref[group // 2, pl.ds(row, 8), :] = unpack_columns(right, left, i)
        return carry

    lax.fori_loop(0, 38, body, 0, unroll=UNROLL)
    lane = lanes(8)
    inside = jnp.where(lane < W, flag_ref[1], jnp.where(lane >= L - W, flag_ref[0], 0.0))
    for group in range(2):
        right, left = right_ref[pl.ds(304 + group * 8, 8), :], left_ref[pl.ds(304 + group * 8, 8), :]
        for i in range(16):
            z = group * 8 + i // 2
            row = z * PLANE + (i % 2) * 8
            ring_ref[pl.ds(row, 8), :] = mask_ref[pl.ds(group * 128 + i * 8, 8), :].astype(F32)
            ring_ref[pl.ds(row + B, 8), :] = unpack_columns(right, left, i) * inside
    mask_out[...] = jnp.zeros_like(mask_out)
    for z in range(B):
        put_rows(mask_out, z + 1, ring_ref[pl.ds(z * PLANE, PLANE), :])

    load.wait()

    def flow(z, carry):
        set_bits(mask_out, bits_ref, z)
        pops = [flow_plane((pops_ref, side_ref), z, i) for i in range(19)]
        rho, velocity = moments(pops, plane(ring_ref, z))
        for k, v in enumerate([rho] + velocity):
            aux_ref[k, pl.ds(pl.multiple_of(z * PLANE, PLANE), PLANE), :] = v
        return carry

    lax.fori_loop(0, B, flow, 0, unroll=UNROLL)


def plane(ref, z, *lead):
    return ref[(*lead, pl.ds(pl.multiple_of(z * PLANE, PLANE), PLANE), slice(None))]


def put_face(ref, row, v, *lead):
    for tile in range(2):
        at = pl.ds(tile * B + row, B, stride=PLANE)
        ref[(*lead, at, slice(None))] = v[tile * B : (tile + 1) * B]


def flow_plane(refs, z, which):
    at = pl.ds(pl.multiple_of(z * B, B), B)
    return halves(refs[0][which, at, :], refs[1][which, at, :])


def flow_rows(refs, row, which):
    at = pl.ds(row, B, stride=B)
    return halves(refs[0][which, at, :], refs[1][which, at, :])


def padded_plane(ref, zz, shift, *lead):
    at = zz * PADDED + 8
    return halves(
        ref[(*lead, pl.ds(at - shift, B), slice(None))],
        ref[(*lead, pl.ds(at + 32 - shift, B), slice(None))],
    )


def put_rows(ref, zz, v):
    ref[pl.ds(zz * PADDED + 8, B), :] = v[:B]
    ref[pl.ds(zz * PADDED + 40, B), :] = v[B:]


def put_padded(ref, comp, zz, v):
    at = zz * PADDED + 8
    if not isinstance(zz, int):
        at = pl.multiple_of(at, 8)
    ref[comp, pl.ds(at, B), :] = v[:B]
    ref[comp, pl.ds(at + 32, B), :] = v[B:]


def face_rows(ref, row, *lead):
    return halves(
        ref[(*lead, pl.ds(row, B, stride=PLANE), slice(None))],
        ref[(*lead, pl.ds(B + row, B, stride=PLANE), slice(None))],
    )


def set_bits(mask_ref, bits_ref, z):
    here = padded_plane(mask_ref, z + 1, 0)
    bits = jnp.where(here > 0, 1, 0)
    for which in range(1, 19):
        cx, cy, cz = DIRS[which]
        source = padded_plane(mask_ref, z + 1 - cz, cy)
        if cx:
            source = ring(source, cx)
        bits = bits + jnp.where(source * here > 0, 1 << which, 0)
    bits_ref[pl.ds(pl.multiple_of(z * PLANE, PLANE), PLANE), :] = bits


def side_open_kernel(
    flag_ref, ylo_ref, yhi_ref, mask_in, bits_in, mask_ref, bits_ref, open_ref
):
    for side in range(2):
        halo = read_field((ylo_ref, yhi_ref)[side], MASK) * flag_ref[2 + side]
        edge, row = ((0, 7), (B - 1, 24))[side]
        own = []
        for tile in range(2):
            part = halo[tile * B : (tile + 1) * B]
            at = PADDED + tile * 32
            mask_ref[pl.ds(at + row, B, stride=PADDED), :] = part
            own.append(mask_ref[pl.ds(at + 8 + edge, B, stride=PADDED), :])
            put_open(open_ref, 0, side, tile, part * own[tile])
        own = halves(*own)
        bits = face_rows(bits_ref, edge)
        for which in (Y_UP, Y_DN)[side]:
            cx, _, cz = DIRS[which]
            source = halo
            if cz:
                source = pltpu.roll(source, cz % PLANE, axis=0)
            if cx:
                source = ring(source, cx)
            bits = bits + jnp.where(source * own > 0, 1 << which, 0)
        put_face(bits_ref, edge, bits)


def edge_open_kernel(
    flag_ref, zlo_ref, zhi_ref, mask_in, bits_in, open_in, mask_ref, bits_ref, open_ref
):
    row = row_ids(B)
    for side in range(2):
        z_ref, zz = (zlo_ref, zhi_ref)[side], (0, B + 1)[side]
        put_rows(mask_ref, zz, read_field(z_ref, MASK) * flag_ref[4 + side])
        for y_side in range(2):
            pair = read_diag(z_ref, y_side, MASK)
            for tile in range(2):
                at = zz * PADDED + tile * 32 + (7, 24)[y_side]
                scale = flag_ref[4 + side] * flag_ref[2 + y_side]
                mask_ref[pl.ds(at, 1), :] = pair[tile][:1] * scale

    def body(k, carry):
        set_bits(mask_ref, bits_ref, k * (B - 1))
        return carry

    lax.fori_loop(0, 2, body, 0)
    for tile in range(2):
        for side in range(2):
            edge = tile * 32 + (7, 24)[side]
            halo = mask_ref[pl.ds(PADDED + edge, B, stride=PADDED), :]
            first = mask_ref[pl.ds(edge, 1), :]
            last = mask_ref[pl.ds(PADROWS - PADDED + edge, 1), :]
            ends = jnp.where(row == 0, halo * first, jnp.where(row == B - 1, halo * last, 0.0))
            put_open(open_ref, 1, side, tile, ends)
            at = (0, B + 1)[side] * PADDED + tile * 32
            near = (1, B)[side]
            halo = mask_ref[pl.ds(at + 8, B), :]
            own = mask_ref[pl.ds(near * PADDED + tile * 32 + 8, B), :]
            first = mask_ref[pl.ds(at + 7, 1), :]
            last = mask_ref[pl.ds(at + 24, 1), :]
            ends = jnp.where(row == 0, halo * first, jnp.where(row == B - 1, halo * last, 0.0))
            put_open(open_ref, 2, side, tile, halo * own)
            put_open(open_ref, 3, side, tile, ends)


def open_at(kind, side, tile):
    return ((kind * 2 + side) * 2 + tile) * B


def put_open(ref, kind, side, tile, v):
    ref[pl.ds(open_at(kind, side, tile), B), :] = v


def get_open(ref, kind, side):
    return ref[pl.ds(open_at(kind, side, 0), PLANE), :] > 0


def write_message(out_ref, fields):
    lane = lanes(B) // 16
    for slab in range(SIDES):
        packed = jnp.zeros((B, L), F32)
        for k, field in enumerate(fields[slab * 8 : slab * 8 + 8]):
            turn = (W + 16 * k) % L
            packed = jnp.where(lane == k, pltpu.roll(field[B:], turn, axis=1), packed)
        out_ref[pl.ds(slab * B, B), :] = packed
    for f, field in enumerate(fields):
        out_ref[pl.ds((SIDES + f) * B, B), :] = field[:B]


def unpack_side(packed, f):
    return pltpu.roll(packed, L - W - 16 * (f % 8), axis=1)


def read_field(ref, f):
    side = ref[pl.ds(f // 8 * B, B), :]
    return halves(ref[pl.ds((SIDES + f) * B, B), :], unpack_side(side, f))


def read_row(ref, f, row):
    main = jnp.broadcast_to(ref[pl.ds((SIDES + f) * B + row, 1), :], (8, L))
    side = jnp.broadcast_to(ref[pl.ds(f // 8 * B + row, 1), :], (8, L))
    return main, unpack_side(side, f)


def read_diag(ref, side, f):
    slabs = ref.shape[0] // (B + 2)
    base = slabs * B + side * slabs
    main = jnp.broadcast_to(ref[pl.ds(base + SIDES + f, 1), :], (8, L))
    packed = jnp.broadcast_to(ref[pl.ds(base + f // 8, 1), :], (8, L))
    return main, unpack_side(packed, f)


def spread8(pair):
    return halves(
        jnp.concatenate([pair[0], pair[0]], axis=0), jnp.concatenate([pair[1], pair[1]], axis=0)
    )


def partial_sum(f, inner, is_open, outward, in_rows):
    row = row_ids(PLANE) % B
    total = f[0]
    total = total + jnp.where(is_open(1), ring(f[1], 1), f[2])
    total = total + jnp.where(is_open(2), ring(f[2], -1), f[1])
    up, down = in_rows
    moved = jnp.where(is_open(up), pltpu.roll(f[up], 1, axis=0), f[down])
    total = total + jnp.where(row == 0, 0.0, moved)
    moved = jnp.where(is_open(down), pltpu.roll(f[down], PLANE - 1, axis=0), f[up])
    total = total + jnp.where(row == B - 1, 0.0, moved)
    return total + jnp.where(is_open(outward), inner, f[OPP[outward]])


def open_bits(bits):
    return lambda which: is_open(bits, which)


def open_mask(own, inner, in_rows):
    shifted = {
        1: ring(own, 1),
        2: ring(own, -1),
        in_rows[0]: pltpu.roll(own, 1, axis=0),
        in_rows[1]: pltpu.roll(own, PLANE - 1, axis=0),
    }
    return lambda which: shifted.get(which, inner) > 0


def write_y_messages(pops_refs, post_ref, aux_ref, y_refs, bits_ref=None, ring_ref=None):
    row = row_ids(PLANE) % B
    for side in range(2):
        names = (Y_DN, Y_UP)[side]
        edge, inner = ((0, 1), (B - 1, B - 2))[side]
        normal = (4, 3)[side]
        if ring_ref is None:
            opened = open_bits(face_rows(bits_ref, edge))
        else:
            opened = open_mask(face_rows(ring_ref, edge), face_rows(ring_ref, inner), (5, 6))
        f = [face_rows(post_ref, edge, i) for i in range(7)]
        part = partial_sum(f, face_rows(post_ref, inner, normal), opened, normal, (5, 6))
        fields = [flow_rows(pops_refs, edge, c) for c in names]
        fields += [face_rows(aux_ref, edge, k) for k in range(4)]
        fields += [part, f[normal], jnp.where(row == 0, f[6], f[5])]
        if ring_ref is not None:
            fields.append(face_rows(ring_ref, edge))
        write_message(y_refs[side], fields)


def write_z_messages(pops_refs, post_ref, aux_ref, z_refs, bits_ref=None, ring_ref=None):
    row = row_ids(PLANE) % B
    for side in range(2):
        names = (Z_DN, Z_UP)[side]
        edge, inner = ((0, 1), (B - 1, B - 2))[side]
        normal = (6, 5)[side]
        if ring_ref is None:
            opened = open_bits(plane(bits_ref, edge))
        else:
            opened = open_mask(plane(ring_ref, edge), plane(ring_ref, inner), (3, 4))
        f = [plane(post_ref, edge, i) for i in range(7)]
        part = partial_sum(f, plane(post_ref, inner, normal), opened, normal, (3, 4))
        fields = [flow_plane(pops_refs, edge, c) for c in names]
        fields += [plane(aux_ref, edge, k) for k in range(4)]
        fields += [part, f[normal], jnp.where(row == 0, f[4], f[3])]
        if ring_ref is not None:
            fields.append(plane(ring_ref, edge))
        write_message(z_refs[side], fields)


def relax(f, which, rho, vx, vy, vz, base):
    a = along(which, vx, vy, vz)
    scale = (OMEGA_FLOW * WEIGHTS[which]) * rho
    return (1.0 - OMEGA_FLOW) * f + scale * (base + a * (3.0 + 4.5 * a))


def lifted(conc, vx, vy, vz):
    vz = vz + FORCE_GAIN * (conc - REST_CONC)
    return vz, 1.0 - 1.5 * (vx * vx + vy * vy + vz * vz)


def stream_solute(z, post_ref, bits, fills, below, above):
    post = [plane(post_ref, z, i) for i in range(7)]
    moved = [
        None,
        ring(post[1], 1),
        ring(post[2], -1),
        shift_rows(post[3], 1, fills[0]),
        shift_rows(post[4], -1, fills[1]),
        below,
        above,
    ]
    return [post[0]] + [chosen(bits, moved[i], post, i) for i in range(1, 7)]


def collide_face(msg, names, conc, put):
    rho, vx, vy, vz = (read_field(msg, k) for k in range(RHO, RHO + 4))
    vz, base = lifted(conc, vx, vy, vz)
    for k, which in enumerate(names):
        put(which, relax(read_field(msg, k), which, rho, vx, vy, vz, base))


def collide_y_halos(post_ref, open_ref, y_refs, z_refs, flow_ref):
    row = row_ids(PLANE) % B
    for side in range(2):
        msg = y_refs[side]
        own = face_rows(post_ref, (0, B - 1)[side], (4, 3)[side])
        conc = read_field(msg, PART)
        conc = conc + jnp.where(get_open(open_ref, 0, side), own, read_field(msg, NORM))
        if z_refs is not None:
            ends = jnp.where(
                row == 0,
                spread8(read_diag(z_refs[0], side, TRANS)),
                spread8(read_diag(z_refs[1], side, TRANS)),
            )
            ends = jnp.where(get_open(open_ref, 1, side), ends, read_field(msg, TRANS))
            conc = conc + ends
        at = PADDED + (7, 24)[side]

        def put(which, v):
            for tile in range(2):
                part = v[tile * B : (tile + 1) * B]
                if z_refs is None:
                    flow_ref[which, pl.ds(at + tile * 32, B, stride=PADDED), :] = part
                else:
                    for z in (0, B - 1):
                        flow_ref[which, pl.ds(at + tile * 32 + z * PADDED, 1), :] = part[z : z + 1]

        collide_face(msg, (Y_UP, Y_DN)[side], conc, put)


def collide_z_halos(post_ref, open_ref, y_refs, z_refs, flow_ref):
    row = row_ids(PLANE) % B
    for side in range(2):
        msg = z_refs[side]
        own = plane(post_ref, (0, B - 1)[side], (6, 5)[side])
        ends = jnp.where(
            row == 0, spread8(read_diag(msg, 0, NORM)), spread8(read_diag(msg, 1, NORM))
        )
        ends = jnp.where(get_open(open_ref, 3, side), ends, read_field(msg, TRANS))
        conc = read_field(msg, PART)
        conc = conc + jnp.where(get_open(open_ref, 2, side), own, read_field(msg, NORM))
        conc = conc + jnp.where((row == 0) | (row == B - 1), ends, 0.0)
        zz = (0, B + 1)[side]
        collide_face(
            msg, (Z_UP, Z_DN)[side], conc, lambda which, v: put_padded(flow_ref, which, zz, v)
        )
    for y_side in range(2):
        for z_side in range(2):
            which = DIRS.index((0, 1 - 2 * y_side, 1 - 2 * z_side))
            names = (Y_UP, Y_DN)[y_side]
            msg = z_refs[z_side]
            z_row = (0, B - 1)[z_side]
            y_row = (0, B - 1)[y_side]
            from_y = read_row(y_refs[y_side], TRANS, z_row)
            from_z = read_row(msg, TRANS, y_row)
            get = [read_diag(msg, y_side, f) for f in range(TRANS + 1)]
            for tile in range(2):
                open_y = open_ref[pl.ds(open_at(1, y_side, tile) + z_row, 1), :]
                open_z = open_ref[pl.ds(open_at(3, z_side, tile) + y_row, 1), :]
                conc = get[PART][tile]
                conc = conc + jnp.where(open_y > 0, from_y[tile], get[TRANS][tile])
                conc = conc + jnp.where(open_z > 0, from_z[tile], get[NORM][tile])
                rho, vx, vy, vz = (get[k][tile] for k in range(RHO, RHO + 4))
                vz, base = lifted(conc, vx, vy, vz)
                v = relax(get[names.index(which)][tile], which, rho, vx, vy, vz, base)
                at = (0, B + 1)[z_side] * PADDED + tile * 32 + (7, 24)[y_side]
                flow_ref[which, pl.ds(at, 1), :] = v[:1]


def collide_flow(load, rho, vx, vy, vz, bits, conc, put):
    porous = is_open(bits, 0)
    vz = vz + jnp.where(porous, FORCE_GAIN * (conc - REST_CONC), 0.0)
    base = 1.0 - 1.5 * (vx * vx + vy * vy + vz * vz)
    keep = 1.0 - OMEGA_FLOW
    scaled = OMEGA_FLOW * rho
    f = load(0)
    put(0, jnp.where(porous, keep * f + (WEIGHTS[0] * scaled) * base, f))
    for i, j in PAIRS:
        a = along(i, vx, vy, vz)
        scale = WEIGHTS[i] * scaled
        even = scale * (base + 4.5 * (a * a))
        odd = scale * (3.0 * a)
        f, g = load(i), load(j)
        put(i, jnp.where(porous, keep * f + (even + odd), g))
        put(j, jnp.where(porous, keep * g + (even - odd), f))


def stream_flow(z, bits, flow_ref):
    post = [padded_plane(flow_ref, z + 1, 0, i) for i in range(19)]
    out = [post[0]]
    for which in range(1, 19):
        cx, cy, cz = DIRS[which]
        moved = post[which]
        if cy or cz:
            moved = padded_plane(flow_ref, z + 1 - cz, cy, which)
        if cx:
            moved = ring(moved, cx)
        out.append(jnp.where(is_open(bits, which), moved, post[OPP[which]]))
    return out


def first_kernel(
    dense_ref, right_ref, left_ref, pops_ref, side_ref, aux_ref, ring_ref,
    post_ref, ydn_ref, yup_ref, turn_ref,
):
    turn_ref[pl.ds(0, BLOCKROWS // 8, stride=8), :] = right_ref[...]
    turn_ref[pl.ds(7, BLOCKROWS // 8, stride=8), :] = left_ref[...]
    lane = lanes(8)
    near = (lane < W) | (lane >= L - W)

    def body(z, carry):
        solute = []
        for i in range(7):
            at = pl.multiple_of(i * 256 + z * B, B)
            side = [
                jnp.where(near, turn_blocks(turn_ref[pl.ds(at + 8 * k, 8), :]), 0.0)
                for k in range(2)
            ]
            solute.append(jnp.concatenate([dense_ref[pl.ds(at, B), :]] + side, axis=0))
        post = solute_collide(solute, [plane(aux_ref, z, k) for k in range(1, 4)])
        for i in range(7):
            post_ref[i, pl.ds(pl.multiple_of(z * PLANE, PLANE), PLANE), :] = post[i]
        return carry

    lax.fori_loop(0, B, body, 0, unroll=UNROLL)
    pops_refs = pops_ref, side_ref
    write_y_messages(pops_refs, post_ref, aux_ref, (ydn_ref, yup_ref), ring_ref=ring_ref)


def pull(z, refs, bits_ref, flow_ref, solute_ref):
    pops_ref, side_ref, post_ref, aux_ref = refs
    at = pl.ds(pl.multiple_of(z * PLANE, PLANE), PLANE)
    main = pl.ds(pl.multiple_of(z * B, B), B)
    bits = bits_ref[at, :]
    pops = stream_flow(z, bits, flow_ref)
    for i in range(19):
        pops_ref[i, main, :] = pops[i][:B]
        if side_ref is not None:
            side_ref[i, main, :] = pops[i][B:]
    if side_ref is None:
        return
    rho, velocity = moments(pops, jnp.where(is_open(bits, 0), 1.0, 0.0))
    for k, v in enumerate([rho] + velocity):
        aux_ref[k, at, :] = v
    post = solute_collide([solute_ref[i, at, :] for i in range(7)], velocity)
    for i in range(7):
        post_ref[i, at, :] = post[i]


def push(z, pops_refs, aux_ref, bits, solute, flow_ref):
    rho, vx, vy, vz = (plane(aux_ref, z, k) for k in range(4))
    collide_flow(
        lambda i: flow_plane(pops_refs, z, i), rho, vx, vy, vz, bits, sum(solute),
        lambda i, v: put_padded(flow_ref, i, z + 1, v),
    )


def put_solute(solute_ref, z, solute):
    for i in range(7):
        solute_ref[i, pl.ds(pl.multiple_of(z * PLANE, PLANE), PLANE), :] = solute[i]


def turn_plane(turn_ref, z, solute):
    for i in range(7):
        for half in range(2):
            at = pl.multiple_of(i * 256 + z * B + half * 8, 8)
            turn_ref[pl.ds(at, 8), :] = turn_blocks(solute[i][half * 8 : half * 8 + 8])


def core_kernel(first, *refs):
    pops_ref, side_ref, post_ref, aux_ref, bits_ref = refs[:5]
    ring_ref, refs = (refs[5], refs[6:]) if first else (None, refs[5:])
    zdn_ref, zup_ref, flow_ref, solute_ref = refs
    write_z_messages(
        (pops_ref, side_ref), post_ref, aux_ref, (zdn_ref, zup_ref), bits_ref, ring_ref
    )
    fills = [jnp.zeros((PLANE, L), F32)] * 2

    def body(z, carry):
        bits = plane(bits_ref, z)
        solute = stream_solute(
            z, post_ref, bits, fills, plane(post_ref, z - 1, 5), plane(post_ref, z + 1, 6)
        )
        put_solute(solute_ref, z, solute)
        push(z, (pops_ref, side_ref), aux_ref, bits, solute, flow_ref)
        return carry

    lax.fori_loop(1, B - 1, body, 0, unroll=UNROLL)


def fix_rows(pops_refs, post_ref, aux_ref, bits_ref, y_refs, flow_ref, solute_ref):
    for side in range(2):
        edge = (0, B - 1)[side]
        which = (3, 4)[side]
        bits = face_rows(bits_ref, edge)
        post = {i: face_rows(post_ref, edge, i) for i in (3, 4)}
        new = chosen(bits, read_field(y_refs[side], NORM), post, which)
        conc = new + sum(face_rows(solute_ref, edge, i) for i in range(7) if i != which)
        put_face(solute_ref, edge, new, which)

        def put(i, v):
            for tile in range(2):
                at = PADDED + tile * 32 + 8 + edge
                flow_ref[i, pl.ds(at, B, stride=PADDED), :] = v[tile * B : (tile + 1) * B]

        rho, vx, vy, vz = (face_rows(aux_ref, edge, k) for k in range(4))
        collide_flow(
            lambda i: flow_rows(pops_refs, edge, i), rho, vx, vy, vz, bits, conc, put
        )


def inner_kernel(*refs):
    bits_ref, open_ref, ylo_ref, yhi_ref = refs[6:10]
    *state, flow_ref, solute_ref = refs[10:]
    pops_ref, side_ref, post_ref, aux_ref = state
    y_refs = ylo_ref, yhi_ref
    fix_rows((pops_ref, side_ref), post_ref, aux_ref, bits_ref, y_refs, flow_ref, solute_ref)
    collide_y_halos(post_ref, open_ref, y_refs, None, flow_ref)

    def body(z, carry):
        pull(z, state, bits_ref, flow_ref, solute_ref)
        return carry

    lax.fori_loop(2, B - 2, body, 0, unroll=UNROLL)


def inner_last_kernel(*refs):
    pops_ref, side_ref, post_ref, aux_ref = refs[:4]
    bits_ref, open_ref, ylo_ref, yhi_ref, flow_ref, solute_ref, turn_ref = refs[6:]
    y_refs = ylo_ref, yhi_ref
    fix_rows((pops_ref, side_ref), post_ref, aux_ref, bits_ref, y_refs, flow_ref, solute_ref)

    def turn(z, carry):
        turn_plane(turn_ref, z, [plane(solute_ref, z, i) for i in range(7)])
        return carry

    lax.fori_loop(1, B - 1, turn, 0, unroll=UNROLL)
    collide_y_halos(post_ref, open_ref, y_refs, None, flow_ref)


def edge_solute(z, post_ref, bits_ref, y_refs, z_refs):
    fills = [spread8(read_row(y_refs[side], NORM, z)) for side in range(2)]
    below = read_field(z_refs[0], NORM) if z == 0 else plane(post_ref, z - 1, 5)
    above = read_field(z_refs[1], NORM) if z == B - 1 else plane(post_ref, z + 1, 6)
    return stream_solute(z, post_ref, plane(bits_ref, z), fills, below, above)


def edge_kernel(*refs):
    bits_ref, open_ref, ylo_ref, yhi_ref, zlo_ref, zhi_ref = refs[6:12]
    *state, flow_ref, solute_ref, ydn_ref, yup_ref = refs[12:]
    pops_ref, side_ref, post_ref, aux_ref = state
    y_refs, z_refs = (ylo_ref, yhi_ref), (zlo_ref, zhi_ref)
    for z in (0, B - 1):
        solute = edge_solute(z, post_ref, bits_ref, y_refs, z_refs)
        put_solute(solute_ref, z, solute)
        push(z, (pops_ref, side_ref), aux_ref, plane(bits_ref, z), solute, flow_ref)
    collide_y_halos(post_ref, open_ref, y_refs, z_refs, flow_ref)
    collide_z_halos(post_ref, open_ref, y_refs, z_refs, flow_ref)
    for z in (0, 1, B - 2, B - 1):
        pull(z, state, bits_ref, flow_ref, solute_ref)
    write_y_messages(
        (pops_ref, side_ref), post_ref, aux_ref, (ydn_ref, yup_ref), bits_ref=bits_ref
    )


def send_kernel(me_ref, slot_ref, *refs):
    post_ref, bits_ref, ylo_ref, yhi_ref, zlo_ref, zhi_ref = refs[2:8]
    solute_ref, turn_ref, *outs = refs[8:]
    for z in (0, B - 1):
        solute = edge_solute(z, post_ref, bits_ref, (ylo_ref, yhi_ref), (zlo_ref, zhi_ref))
        put_solute(solute_ref, z, solute)
        turn_plane(turn_ref, z, solute)
    fill_messages(me_ref[0], [slot_ref[0, 0, j] for j in range(8)], turn_ref, outs)


def last_kernel(*refs):
    pops_ref, side_ref, post_ref, aux_ref, flow_in, solute_ref, bits_ref, open_ref = refs[:8]
    y_refs, z_refs = refs[8:10], refs[10:12]
    out_ref, flow_ref = refs[12:]
    for z in (0, B - 1):
        solute = [plane(solute_ref, z, i) for i in range(7)]
        push(z, (pops_ref, side_ref), aux_ref, plane(bits_ref, z), solute, flow_ref)
    collide_y_halos(post_ref, open_ref, y_refs, z_refs, flow_ref)
    collide_z_halos(post_ref, open_ref, y_refs, z_refs, flow_ref)

    def body(z, carry):
        pull(z, (out_ref, None, None, None), bits_ref, flow_ref, None)
        return carry

    lax.fori_loop(0, B, body, 0, unroll=UNROLL)


def scatter_kernel(me_ref, slot_ref, *refs):
    receive(me_ref[0], [slot_ref[s] for s in range(8)], refs[:-1], refs[-1])


def neighbours(low, high, axis):
    count = lax.axis_size(axis)
    up = [(i, (i + 1) % count) for i in range(count)]
    down = [(i, (i - 1) % count) for i in range(count)]
    return lax.ppermute(high, axis, up), lax.ppermute(low, axis, down)


def exchange_blocks(own, up1, down1, up2, down2, up3, down3):
    def shifted(x, step):
        return lax.ppermute(x, "gz", [(i, (i + step) % 8) for i in range(8)])

    up1, down1 = shifted(up1, 1), shifted(down1, -1)
    up2, down2 = shifted(up2, 2), shifted(down2, -2)
    up3 = shifted(jnp.concatenate([up3, up1[ROW:]], axis=0), 3)
    down3 = shifted(jnp.concatenate([down3, down1[ROW:]], axis=0), -3)
    return own, up1, down1, up2, down2, up3, down3


def inside():
    flags = []
    for axis in ("gx", "gy", "gz"):
        at = lax.axis_index(axis)
        flags += [at > 0, at < lax.axis_size(axis) - 1]
    return jnp.stack(flags).astype(F32)


def with_edges(face, halos, row):
    slabs = face.shape[0] // B
    rows = [face] + [halo.reshape(slabs, B, L)[:, row] for halo in halos]
    pad = -slabs * (B + 2) % 8
    return jnp.concatenate(rows + [jnp.zeros((pad, L), F32)], axis=0)


def exchange_z(halos, zdn, zup):
    return neighbours(with_edges(zdn, halos, 0), with_edges(zup, halos, B - 1), "gz")


def shards(populations, solute_state, pore_mask, block_slot, slot_block):
    flags = inside()
    me = lax.axis_index("gz").astype(jnp.int32).reshape(1)
    turn = pltpu.VMEM((BLOCKROWS, L), F32)
    sent = tuple(held(n, L) for n in (ROW, ROW + HALF, ROW + HALF, ROW, ROW, ROW, ROW))
    state = solute_state.reshape(7, 8, 32, L).transpose(0, 2, 1, 3).reshape(BLOCKROWS, L)
    send = call(
        gather_kernel, sent, [SMEM, SMEM, HBM], [turn, pltpu.SemaphoreType.DMA], 1, 2 * 10**6
    )(me, slot_block, state)
    recv = exchange_blocks(*send)

    pops = populations.reshape(19, 256, L)
    mask = pore_mask.reshape(256, L)
    low, high = call(columns_kernel, (held(320, L),) * 2, [VMEM] * 2, [], 10**6, 13 * 10**6)(
        pops, mask
    )
    left, right = neighbours(low, high, "gx")
    dims = ((19, 256, L), (19, 256, L), (ROWS, L), (4, ROWS, L), (PADROWS, L))
    pops, side, ring_mask, aux, mask, bits = call(
        ring_kernel,
        tuple(held(*d) for d in dims) + (held(ROWS, L, dtype=jnp.int32),),
        [SMEM, HBM] + [VMEM] * 3,
        [pltpu.SemaphoreType.DMA],
        10**6,
        20 * 10**6,
    )(flags, pops, mask, right, left)

    low, high = call(
        pick_kernel, (held(ROW, L),) * 2, [SMEM] * 2 + [VMEM] * 8, [], 1, 10**6, keep=True
    )(me, block_slot, *recv, bits)
    left, right = neighbours(low, high, "gx")
    dense = call(
        spread_kernel, held(BLOCKROWS, L), [SMEM] * 2 + [VMEM] * 7, [turn], 10**6, 10**7, keep=True
    )(me, block_slot, *recv)
    message = held((SIDES + MASK + 1) * B, L)
    post, ydn, yup = call(
        first_kernel,
        (held(7, ROWS, L),) + (message,) * 2,
        [VMEM] * 7,
        [turn],
        10**7,
        10**7,
        keep=True,
    )(dense, right, left, pops, side, aux, ring_mask)

    states = (held(19, 256, L), held(19, 256, L), held(7, ROWS, L), held(4, ROWS, L))
    works = (held(19, PADROWS, L), held(7, ROWS, L))
    opens_out = (held(PADROWS, L), held(ROWS, L, dtype=jnp.int32), held(PLANE * 8, L))
    message = held((SIDES + MASK) * B, L)
    state = (pops, side, post, aux)
    for step in range(STEPS):
        last = step == STEPS - 1
        y_halos = neighbours(ydn, yup, "gy")
        zdn, zup, *work = call(
            functools.partial(core_kernel, step == 0),
            (held(*ydn.shape),) * 2 + works,
            [VMEM] * (6 if step == 0 else 5),
            [],
            10**7,
            10**7,
            keep=True,
        )(*state, bits, *([ring_mask] if step == 0 else []))
        z_halos = exchange_z(y_halos, zdn, zup)
        if step == 0:
            mask, bits, opens = call(
                side_open_kernel,
                opens_out,
                [SMEM] + [VMEM] * 4,
                [],
                10**6,
                10**6,
                aliases={3: 0, 4: 1},
                keep=True,
            )(flags, *y_halos, mask, bits)
        if last:
            break
        moved = call(
            inner_kernel,
            states + works,
            [VMEM] * 10,
            [],
            10**7,
            10**7,
            aliases={i: i for i in range(6)},
            keep=True,
        )(*state, *work, bits, opens, *y_halos)
        if step == 0:
            mask, bits, opens = call(
                edge_open_kernel,
                opens_out,
                [SMEM] + [VMEM] * 5,
                [],
                10**6,
                10**6,
                aliases={3: 0, 4: 1, 5: 2},
                keep=True,
            )(flags, *z_halos, mask, bits, opens)
        *state, _, _, ydn, yup = call(
            edge_kernel,
            states + works + (message, message),
            [VMEM] * 12,
            [],
            10**7,
            10**7,
            aliases={i: i for i in range(6)},
            keep=True,
        )(*moved, bits, opens, *y_halos, *z_halos)

    flow, solute, turned = call(
        inner_last_kernel,
        works + (held(BLOCKROWS, L),),
        [VMEM] * 10,
        [],
        10**7,
        10**7,
        aliases={4: 0, 5: 1},
        keep=True,
    )(*state, *work, bits, opens, *y_halos)
    solute, _, *send = call(
        send_kernel,
        (works[1], held(BLOCKROWS, L)) + sent,
        [SMEM] * 2 + [VMEM] * 8,
        [],
        10**6,
        10**6,
        aliases={2: 0, 3: 1},
        keep=True,
    )(me, block_slot, solute, turned, state[2], bits, *y_halos, *z_halos)
    recv = exchange_blocks(*send)
    pops, _ = call(
        last_kernel,
        (shape(19, 256, L), works[0]),
        [VMEM] * 12,
        [],
        10**7,
        10**7,
        aliases={4: 1},
        keep=True,
    )(*state, flow, solute, bits, opens, *y_halos, *z_halos)
    out = call(scatter_kernel, shape(BLOCKROWS, L), [SMEM] * 2 + [VMEM] * 7, [], 1, 2 * 10**6)(
        me, slot_block, *recv
    )
    new_solute = out.reshape(7, 32, 8, L).transpose(0, 2, 1, 3).reshape(7, 8, 4096)
    return pops.reshape(19, B, B, L), new_solute


def solution(mesh):
    in_specs = (
        P(None, "gz", "gy", "gx"),
        P(None, ("gx", "gy", "gz"), None),
        P("gz", "gy", "gx"),
        P("gz", "gy", "gx"),
        P(("gx", "gy", "gz")),
    )
    out_specs = (P(None, "gz", "gy", "gx"), P(None, ("gx", "gy", "gz"), None))
    return jax.shard_map(shards, mesh=mesh, in_specs=in_specs, out_specs=out_specs, check_vma=False)
```

```python
import functools

import jax
import jax.numpy as jnp
from jax import lax
from jax.experimental import pallas as pl
from jax.experimental.pallas import tpu as pltpu
from jax.sharding import PartitionSpec as P

STEPS = 4
DIRS = [
    (0, 0, 0),
    (1, 0, 0),
    (-1, 0, 0),
    (0, 1, 0),
    (0, -1, 0),
    (0, 0, 1),
    (0, 0, -1),
    (1, 1, 0),
    (-1, -1, 0),
    (1, -1, 0),
    (-1, 1, 0),
    (1, 0, 1),
    (-1, 0, -1),
    (1, 0, -1),
    (-1, 0, 1),
    (0, 1, 1),
    (0, -1, -1),
    (0, 1, -1),
    (0, -1, 1),
]
OPP = [DIRS.index((-a, -b, -c)) for a, b, c in DIRS]
PAIRS = [(i, OPP[i]) for i in range(1, 19, 2)]
WEIGHTS = [1.0 / 3.0] + [1.0 / 18.0] * 6 + [1.0 / 36.0] * 12
OMEGA_FLOW = 1.2
FORCE_GAIN = 0.02
REST_CONC = 8.0
Y_UP = [i for i in range(19) if DIRS[i][1] == 1]
Y_DN = [i for i in range(19) if DIRS[i][1] == -1]
Z_UP = [i for i in range(19) if DIRS[i][2] == 1]
Z_DN = [i for i in range(19) if DIRS[i][2] == -1]
RHO, NORM, TRANS, MASK = 5, 9, 10, 11
SIDES = 2
UNROLL = 2
B = 16
L = 128
W = 8
PLANE = 2 * B
ROWS = B * PLANE
PADDED = 64
PADROWS = (B + 2) * PADDED
ROW = 7 * 32
HALF = ROW // 2
BLOCKROWS = ROW * 8
F32 = jnp.float32
VMEM = pl.BlockSpec(memory_space=pltpu.VMEM)
SMEM = pl.BlockSpec(memory_space=pltpu.SMEM)
HBM = pl.BlockSpec(memory_space=pltpu.HBM)


def call(
    kernel, out_shape, in_specs, scratch, flops, nbytes, aliases={}, keep=False, out_specs=None
):
    run = pl.pallas_call(
        kernel,
        out_shape=out_shape,
        in_specs=in_specs,
        out_specs=out_specs or jax.tree.map(lambda _: VMEM, out_shape),
        scratch_shapes=scratch,
        input_output_aliases=aliases,
        compiler_params=pltpu.CompilerParams(vmem_limit_bytes=20 * 1024 * 1024),
        cost_estimate=pl.CostEstimate(flops=flops, bytes_accessed=nbytes, transcendentals=0),
    )

    def place(x, spec):
        if spec is HBM or (keep and spec is VMEM):
            return pltpu.with_memory_space_constraint(x, spec.memory_space)
        return x

    def placed(*args):
        return run(*map(place, args, in_specs))

    return placed


def shape(*dims):
    return jax.ShapeDtypeStruct(dims, F32)


def held(*dims, dtype=F32):
    return pltpu.VMEM(dims, dtype)


def lanes(rows):
    return lax.broadcasted_iota(jnp.int32, (rows, L), 1)


def row_ids(rows):
    return lax.broadcasted_iota(jnp.int32, (rows, L), 0)


def ring(v, step):
    rolled = pltpu.roll(v, step % L, axis=1)
    other = jnp.concatenate([rolled[B:], rolled[:B]], axis=0)
    return jnp.where(lanes(PLANE) == (0 if step > 0 else L - 1), other, rolled)


def halves(main, side):
    return jnp.concatenate([main, side], axis=0)


def shift_rows(v, step, fill):
    rolled = pltpu.roll(v, step % PLANE, axis=0)
    return jnp.where(row_ids(PLANE) % B == (0 if step > 0 else B - 1), fill, rolled)


def is_open(bits, which):
    return (bits & (1 << which)) != 0


def along(which, vx, vy, vz):
    total = None
    for sign, part in zip(DIRS[which], (vx, vy, vz)):
        if sign != 0:
            if total is None:
                total = part if sign > 0 else -part
            else:
                total = total + part if sign > 0 else total - part
    return total


def moments(pops, porous):
    rho = pops[0]
    for which in range(1, 19):
        rho = rho + pops[which]
    scale = porous / rho
    parts = []
    for coord in range(3):
        plus = sum(pops[i] for i in range(19) if DIRS[i][coord] == 1)
        minus = sum(pops[i] for i in range(19) if DIRS[i][coord] == -1)
        parts.append((plus - minus) * scale)
    return rho, parts


def solute_collide(solute, velocity):
    conc = sum(solute)
    out = [-0.5 * solute[0] + 0.375 * conc]
    base = 0.1875 * conc
    for coord in range(3):
        turn = 0.75 * conc * velocity[coord]
        out.append((base - 0.5 * solute[1 + 2 * coord]) + turn)
        out.append((base - 0.5 * solute[2 + 2 * coord]) - turn)
    return out


def chosen(bits, moved, post, which):
    return jnp.where(
        is_open(bits, which),
        moved,
        jnp.where(is_open(bits, 0), post[OPP[which]], post[which]),
    )


def turn_blocks(x):
    row, lane = row_ids(8), lanes(8)
    x = take(x, (lane - B * row) & (L - 1), 1)
    x = take(x, (lane // B - row) & 7, 0)
    return take(x, (lane + B * row) & (L - 1), 1)


def take(x, index, axis):
    return jnp.take_along_axis(x, index, axis=axis, mode="promise_in_bounds")


PARTS = (
    (0, 0, 0, ROW, 0),
    (7, 1, 0, ROW, 0),
    (1, 2, 0, ROW, 0),
    (6, 3, 0, ROW, 0),
    (2, 4, 0, ROW, 0),
    (5, 5, 0, ROW, 0),
    (3, 6, 0, ROW, 0),
    (4, 5, ROW, HALF, 0),
    (4, 6, ROW, HALF, HALF),
)


def find(slots, home):
    found = jnp.int32(-1)
    for k, slot in enumerate(slots):
        found = jnp.where((slot >= 0) & (slot // 8 == home), k, found)
    return found


def fill_messages(me, slots, blocks_ref, outs):
    own, up1, down1, up2, down2, up3, down3 = outs
    for off, ref in ((0, own), (1, up1), (7, down1), (2, up2), (6, down2), (3, up3), (5, down3)):
        at = jnp.maximum(find(slots, (me + off) & 7), 0)
        ref[pl.ds(0, ROW), :] = blocks_ref[pl.ds(at, ROW, stride=8), :]
    at = jnp.maximum(find(slots, (me + 4) & 7), 0)
    up1[pl.ds(ROW, HALF), :] = blocks_ref[pl.ds(at, HALF, stride=8), :]
    down1[pl.ds(ROW, HALF), :] = blocks_ref[pl.ds(HALF * 8 + at, HALF, stride=8), :]


def receive(me, slots, refs, out_ref):
    for k, slot in enumerate(slots):

        @pl.when(slot < 0)
        def _():
            out_ref[pl.ds(k, ROW, stride=8), :] = jnp.zeros((ROW, L), F32)

    for off, k, at, count, first in PARTS:
        slot = find(slots, (me + off) & 7)

        @pl.when(slot >= 0)
        def _():
            out_ref[pl.ds(first * 8 + slot, count, stride=8), :] = refs[k][pl.ds(at, count), :]


def gather_kernel(me_ref, slot_ref, state_ref, *refs):
    *outs, blocks_ref, sem = refs
    load = pltpu.make_async_copy(state_ref, blocks_ref, sem)
    load.start()
    load.wait()
    fill_messages(me_ref[0], [slot_ref[s] for s in range(8)], blocks_ref, outs)


def pick_kernel(me_ref, slot_ref, *refs):
    low_ref, high_ref, hold_ref = refs[-3:]
    outer = (lanes(HALF) & 8) == 0
    for tile in (0, 7):
        slot = slot_ref[0, 0, tile]

        @pl.when(slot < 0)
        def _():
            hold_ref[...] = jnp.zeros((ROW, L), F32)

        for off, k, at, count, first in PARTS:

            @pl.when((slot >= 0) & (slot // 8 == ((me_ref[0] + off) & 7)))
            def _():
                hold_ref[pl.ds(first, count), :] = refs[k][pl.ds(at, count), :]

        one, two = hold_ref[pl.ds(0, HALF), :], hold_ref[pl.ds(HALF, HALF), :]
        if tile == 0:
            low_ref[...] = jnp.where(outer, one, pltpu.roll(two, W, axis=1))
        else:
            high_ref[...] = jnp.where(outer, pltpu.roll(two, L - W, axis=1), one)


def spread_kernel(me_ref, slot_ref, *refs):
    *blocks, dense_ref, turn_ref = refs
    receive(me_ref[0], [slot_ref[0, 0, tile] for tile in range(8)], blocks, turn_ref)

    def body(group, carry):
        for i in range(32):
            at = pl.multiple_of(group * 256 + i * 8, 8)
            dense_ref[pl.ds(at, 8), :] = turn_blocks(turn_ref[pl.ds(at, 8), :])
        return carry

    lax.fori_loop(0, BLOCKROWS // 256, body, 0)


def pack_columns(load, low_ref, high_ref, at):
    lane = lanes(8) // W
    low = jnp.zeros((8, L), F32)
    high = jnp.zeros((8, L), F32)
    for i in range(16):
        x = load(i)
        low = jnp.where(lane == i, x if i == 0 else pltpu.roll(x, W * i, axis=1), low)
        turn = (W + W * i) % L
        high = jnp.where(lane == i, x if turn == 0 else pltpu.roll(x, turn, axis=1), high)
    at = pl.multiple_of(at, 8)
    low_ref[pl.ds(at, 8), :] = low
    high_ref[pl.ds(at, 8), :] = high


def columns_kernel(pops_in, mask_in, low_ref, high_ref, pops_ref, mask_ref, sems):
    load = pltpu.make_async_copy(mask_in, mask_ref, sems.at[19])
    load.start()

    def part(comp):
        return pltpu.make_async_copy(pops_in.at[comp], pops_ref.at[comp], sems.at[comp])

    for comp in range(19):
        part(comp).start()

    def rows(start, i):
        return pl.ds(pl.multiple_of(start + i * 8, 8), 8)

    for comp in range(19):
        part(comp).wait()
        for half in range(2):
            pack_columns(
                lambda i: pops_ref[comp, rows(half * 128, i), :],
                low_ref,
                high_ref,
                (2 * comp + half) * 8,
            )
    load.wait()
    for half in range(2):
        pack_columns(
            lambda i: mask_ref[rows(half * 128, i), :].astype(F32),
            low_ref,
            high_ref,
            (38 + half) * 8,
        )


def unpack_columns(right, left, i):
    a = right if i == 0 else pltpu.roll(right, L - W * i, axis=1)
    b = left if i == 15 else pltpu.roll(left, L - W - W * i, axis=1)
    return jnp.where(lanes(8) < L // 2, a, b)


def ring_kernel(
    flag_ref, pops_in, mask_ref, right_ref, left_ref,
    pops_ref, side_ref, ring_ref, aux_ref, mask_out, bits_ref, sem,
):
    load = pltpu.make_async_copy(pops_in, pops_ref, sem)
    load.start()

    def body(group, carry):
        at = pl.ds(pl.multiple_of(group * 8, 8), 8)
        right, left = right_ref[at, :], left_ref[at, :]
        for i in range(16):
            row = pl.multiple_of((group % 2) * 128 + i * 8, 8)
            side_ref[group // 2, pl.ds(row, 8), :] = unpack_columns(right, left, i)
        return carry

    lax.fori_loop(0, 38, body, 0, unroll=UNROLL)
    lane = lanes(8)
    inside = jnp.where(lane < W, flag_ref[1], jnp.where(lane >= L - W, flag_ref[0], 0.0))
    for group in range(2):
        right, left = right_ref[pl.ds(304 + group * 8, 8), :], left_ref[pl.ds(304 + group * 8, 8), :]
        for i in range(16):
            z = group * 8 + i // 2
            row = z * PLANE + (i % 2) * 8
            ring_ref[pl.ds(row, 8), :] = mask_ref[pl.ds(group * 128 + i * 8, 8), :].astype(F32)
            ring_ref[pl.ds(row + B, 8), :] = unpack_columns(right, left, i) * inside
    mask_out[...] = jnp.zeros_like(mask_out)
    for z in range(B):
        put_rows(mask_out, z + 1, ring_ref[pl.ds(z * PLANE, PLANE), :])

    load.wait()

    def flow(z, carry):
        set_bits(mask_out, bits_ref, z)
        pops = [flow_plane((pops_ref, side_ref), z, i) for i in range(19)]
        rho, velocity = moments(pops, plane(ring_ref, z))
        for k, v in enumerate([rho] + velocity):
            aux_ref[k, pl.ds(pl.multiple_of(z * PLANE, PLANE), PLANE), :] = v
        return carry

    lax.fori_loop(0, B, flow, 0, unroll=UNROLL)


def plane(ref, z, *lead):
    return ref[(*lead, pl.ds(pl.multiple_of(z * PLANE, PLANE), PLANE), slice(None))]


def put_face(ref, row, v, *lead):
    for tile in range(2):
        at = pl.ds(tile * B + row, B, stride=PLANE)
        ref[(*lead, at, slice(None))] = v[tile * B : (tile + 1) * B]


def flow_plane(refs, z, which):
    at = pl.ds(pl.multiple_of(z * B, B), B)
    return halves(refs[0][which, at, :], refs[1][which, at, :])


def flow_rows(refs, row, which):
    at = pl.ds(row, B, stride=B)
    return halves(refs[0][which, at, :], refs[1][which, at, :])


def padded_plane(ref, zz, shift, *lead):
    at = zz * PADDED + 8
    return halves(
        ref[(*lead, pl.ds(at - shift, B), slice(None))],
        ref[(*lead, pl.ds(at + 32 - shift, B), slice(None))],
    )


def put_rows(ref, zz, v):
    ref[pl.ds(zz * PADDED + 8, B), :] = v[:B]
    ref[pl.ds(zz * PADDED + 40, B), :] = v[B:]


def put_padded(ref, comp, zz, v):
    at = zz * PADDED + 8
    if not isinstance(zz, int):
        at = pl.multiple_of(at, 8)
    ref[comp, pl.ds(at, B), :] = v[:B]
    ref[comp, pl.ds(at + 32, B), :] = v[B:]


def face_rows(ref, row, *lead):
    return halves(
        ref[(*lead, pl.ds(row, B, stride=PLANE), slice(None))],
        ref[(*lead, pl.ds(B + row, B, stride=PLANE), slice(None))],
    )


def set_bits(mask_ref, bits_ref, z):
    here = padded_plane(mask_ref, z + 1, 0)
    bits = jnp.where(here > 0, 1, 0)
    for which in range(1, 19):
        cx, cy, cz = DIRS[which]
        source = padded_plane(mask_ref, z + 1 - cz, cy)
        if cx:
            source = ring(source, cx)
        bits = bits + jnp.where(source * here > 0, 1 << which, 0)
    bits_ref[pl.ds(pl.multiple_of(z * PLANE, PLANE), PLANE), :] = bits


def side_open_kernel(
    flag_ref, ylo_ref, yhi_ref, mask_in, bits_in, mask_ref, bits_ref, open_ref
):
    for side in range(2):
        halo = read_field((ylo_ref, yhi_ref)[side], MASK) * flag_ref[2 + side]
        edge, row = ((0, 7), (B - 1, 24))[side]
        own = []
        for tile in range(2):
            part = halo[tile * B : (tile + 1) * B]
            at = PADDED + tile * 32
            mask_ref[pl.ds(at + row, B, stride=PADDED), :] = part
            own.append(mask_ref[pl.ds(at + 8 + edge, B, stride=PADDED), :])
            put_open(open_ref, 0, side, tile, part * own[tile])
        own = halves(*own)
        bits = face_rows(bits_ref, edge)
        for which in (Y_UP, Y_DN)[side]:
            cx, _, cz = DIRS[which]
            source = halo
            if cz:
                source = pltpu.roll(source, cz % PLANE, axis=0)
            if cx:
                source = ring(source, cx)
            bits = bits + jnp.where(source * own > 0, 1 << which, 0)
        put_face(bits_ref, edge, bits)


def edge_open_kernel(
    flag_ref, zlo_ref, zhi_ref, mask_in, bits_in, open_in, mask_ref, bits_ref, open_ref
):
    row = row_ids(B)
    for side in range(2):
        z_ref, zz = (zlo_ref, zhi_ref)[side], (0, B + 1)[side]
        put_rows(mask_ref, zz, read_field(z_ref, MASK) * flag_ref[4 + side])
        for y_side in range(2):
            pair = read_diag(z_ref, y_side, MASK)
            for tile in range(2):
                at = zz * PADDED + tile * 32 + (7, 24)[y_side]
                scale = flag_ref[4 + side] * flag_ref[2 + y_side]
                mask_ref[pl.ds(at, 1), :] = pair[tile][:1] * scale

    def body(k, carry):
        set_bits(mask_ref, bits_ref, k * (B - 1))
        return carry

    lax.fori_loop(0, 2, body, 0)
    for tile in range(2):
        for side in range(2):
            edge = tile * 32 + (7, 24)[side]
            halo = mask_ref[pl.ds(PADDED + edge, B, stride=PADDED), :]
            first = mask_ref[pl.ds(edge, 1), :]
            last = mask_ref[pl.ds(PADROWS - PADDED + edge, 1), :]
            ends = jnp.where(row == 0, halo * first, jnp.where(row == B - 1, halo * last, 0.0))
            put_open(open_ref, 1, side, tile, ends)
            at = (0, B + 1)[side] * PADDED + tile * 32
            near = (1, B)[side]
            halo = mask_ref[pl.ds(at + 8, B), :]
            own = mask_ref[pl.ds(near * PADDED + tile * 32 + 8, B), :]
            first = mask_ref[pl.ds(at + 7, 1), :]
            last = mask_ref[pl.ds(at + 24, 1), :]
            ends = jnp.where(row == 0, halo * first, jnp.where(row == B - 1, halo * last, 0.0))
            put_open(open_ref, 2, side, tile, halo * own)
            put_open(open_ref, 3, side, tile, ends)


def open_at(kind, side, tile):
    return ((kind * 2 + side) * 2 + tile) * B


def put_open(ref, kind, side, tile, v):
    ref[pl.ds(open_at(kind, side, tile), B), :] = v


def get_open(ref, kind, side):
    return ref[pl.ds(open_at(kind, side, 0), PLANE), :] > 0


def write_message(out_ref, fields):
    lane = lanes(B) // 16
    for slab in range(SIDES):
        packed = jnp.zeros((B, L), F32)
        for k, field in enumerate(fields[slab * 8 : slab * 8 + 8]):
            turn = (W + 16 * k) % L
            packed = jnp.where(lane == k, pltpu.roll(field[B:], turn, axis=1), packed)
        out_ref[pl.ds(slab * B, B), :] = packed
    for f, field in enumerate(fields):
        out_ref[pl.ds((SIDES + f) * B, B), :] = field[:B]


def unpack_side(packed, f):
    return pltpu.roll(packed, L - W - 16 * (f % 8), axis=1)


def read_field(ref, f):
    side = ref[pl.ds(f // 8 * B, B), :]
    return halves(ref[pl.ds((SIDES + f) * B, B), :], unpack_side(side, f))


def read_row(ref, f, row):
    main = jnp.broadcast_to(ref[pl.ds((SIDES + f) * B + row, 1), :], (8, L))
    side = jnp.broadcast_to(ref[pl.ds(f // 8 * B + row, 1), :], (8, L))
    return main, unpack_side(side, f)


def read_diag(ref, side, f):
    slabs = ref.shape[0] // (B + 2)
    base = slabs * B + side * slabs
    main = jnp.broadcast_to(ref[pl.ds(base + SIDES + f, 1), :], (8, L))
    packed = jnp.broadcast_to(ref[pl.ds(base + f // 8, 1), :], (8, L))
    return main, unpack_side(packed, f)


def spread8(pair):
    return halves(
        jnp.concatenate([pair[0], pair[0]], axis=0), jnp.concatenate([pair[1], pair[1]], axis=0)
    )


def partial_sum(f, inner, is_open, outward, in_rows):
    row = row_ids(PLANE) % B
    total = f[0]
    total = total + jnp.where(is_open(1), ring(f[1], 1), f[2])
    total = total + jnp.where(is_open(2), ring(f[2], -1), f[1])
    up, down = in_rows
    moved = jnp.where(is_open(up), pltpu.roll(f[up], 1, axis=0), f[down])
    total = total + jnp.where(row == 0, 0.0, moved)
    moved = jnp.where(is_open(down), pltpu.roll(f[down], PLANE - 1, axis=0), f[up])
    total = total + jnp.where(row == B - 1, 0.0, moved)
    return total + jnp.where(is_open(outward), inner, f[OPP[outward]])


def open_bits(bits):
    return lambda which: is_open(bits, which)


def open_mask(own, inner, in_rows):
    shifted = {
        1: ring(own, 1),
        2: ring(own, -1),
        in_rows[0]: pltpu.roll(own, 1, axis=0),
        in_rows[1]: pltpu.roll(own, PLANE - 1, axis=0),
    }
    return lambda which: shifted.get(which, inner) > 0


def write_y_messages(pops_refs, post_ref, aux_ref, y_refs, bits_ref=None, ring_ref=None):
    row = row_ids(PLANE) % B
    for side in range(2):
        names = (Y_DN, Y_UP)[side]
        edge, inner = ((0, 1), (B - 1, B - 2))[side]
        normal = (4, 3)[side]
        if ring_ref is None:
            opened = open_bits(face_rows(bits_ref, edge))
        else:
            opened = open_mask(face_rows(ring_ref, edge), face_rows(ring_ref, inner), (5, 6))
        f = [face_rows(post_ref, edge, i) for i in range(7)]
        part = partial_sum(f, face_rows(post_ref, inner, normal), opened, normal, (5, 6))
        fields = [flow_rows(pops_refs, edge, c) for c in names]
        fields += [face_rows(aux_ref, edge, k) for k in range(4)]
        fields[-1] = fields[-1] + FORCE_GAIN * (part - REST_CONC)
        fields += [f[normal], jnp.where(row == 0, f[6], f[5])]
        if ring_ref is not None:
            fields.append(face_rows(ring_ref, edge))
        write_message(y_refs[side], fields)


def write_z_messages(pops_refs, post_ref, aux_ref, z_refs, bits_ref=None, ring_ref=None):
    row = row_ids(PLANE) % B
    for side in range(2):
        names = (Z_DN, Z_UP)[side]
        edge, inner = ((0, 1), (B - 1, B - 2))[side]
        normal = (6, 5)[side]
        if ring_ref is None:
            opened = open_bits(plane(bits_ref, edge))
        else:
            opened = open_mask(plane(ring_ref, edge), plane(ring_ref, inner), (3, 4))
        f = [plane(post_ref, edge, i) for i in range(7)]
        part = partial_sum(f, plane(post_ref, inner, normal), opened, normal, (3, 4))
        fields = [flow_plane(pops_refs, edge, c) for c in names]
        fields += [plane(aux_ref, edge, k) for k in range(4)]
        fields[-1] = fields[-1] + FORCE_GAIN * (part - REST_CONC)
        fields += [f[normal], jnp.where(row == 0, f[4], f[3])]
        if ring_ref is not None:
            fields.append(plane(ring_ref, edge))
        write_message(z_refs[side], fields)


def relax(f, which, rho, vx, vy, vz, base):
    a = along(which, vx, vy, vz)
    scale = (OMEGA_FLOW * WEIGHTS[which]) * rho
    return (1.0 - OMEGA_FLOW) * f + scale * (base + a * (3.0 + 4.5 * a))


def lifted(conc, vx, vy, vz):
    vz = vz + FORCE_GAIN * conc
    return vz, 1.0 - 1.5 * (vx * vx + vy * vy + vz * vz)


def stream_solute(z, post_ref, bits, fills, below, above):
    post = [plane(post_ref, z, i) for i in range(7)]
    moved = [
        None,
        ring(post[1], 1),
        ring(post[2], -1),
        shift_rows(post[3], 1, fills[0]),
        shift_rows(post[4], -1, fills[1]),
        below,
        above,
    ]
    return [post[0]] + [chosen(bits, moved[i], post, i) for i in range(1, 7)]


def collide_face(msg, names, conc, put):
    rho, vx, vy, vz = (read_field(msg, k) for k in range(RHO, RHO + 4))
    vz, base = lifted(conc, vx, vy, vz)
    for k, which in enumerate(names):
        put(which, relax(read_field(msg, k), which, rho, vx, vy, vz, base))


def collide_y_halos(post_ref, open_ref, y_refs, z_refs, flow_ref):
    row = row_ids(PLANE) % B
    for side in range(2):
        msg = y_refs[side]
        own = face_rows(post_ref, (0, B - 1)[side], (4, 3)[side])
        conc = jnp.where(get_open(open_ref, 0, side), own, read_field(msg, NORM))
        if z_refs is not None:
            ends = jnp.where(
                row == 0,
                spread8(read_diag(z_refs[0], side, TRANS)),
                spread8(read_diag(z_refs[1], side, TRANS)),
            )
            ends = jnp.where(get_open(open_ref, 1, side), ends, read_field(msg, TRANS))
            conc = conc + ends
        at = PADDED + (7, 24)[side]

        def put(which, v):
            for tile in range(2):
                part = v[tile * B : (tile + 1) * B]
                if z_refs is None:
                    flow_ref[which, pl.ds(at + tile * 32, B, stride=PADDED), :] = part
                else:
                    for z in (0, B - 1):
                        flow_ref[which, pl.ds(at + tile * 32 + z * PADDED, 1), :] = part[z : z + 1]

        collide_face(msg, (Y_UP, Y_DN)[side], conc, put)


def collide_z_halos(post_ref, open_ref, y_refs, z_refs, flow_ref):
    row = row_ids(PLANE) % B
    for side in range(2):
        msg = z_refs[side]
        own = plane(post_ref, (0, B - 1)[side], (6, 5)[side])
        ends = jnp.where(
            row == 0, spread8(read_diag(msg, 0, NORM)), spread8(read_diag(msg, 1, NORM))
        )
        ends = jnp.where(get_open(open_ref, 3, side), ends, read_field(msg, TRANS))
        conc = jnp.where(get_open(open_ref, 2, side), own, read_field(msg, NORM))
        conc = conc + jnp.where((row == 0) | (row == B - 1), ends, 0.0)
        zz = (0, B + 1)[side]
        collide_face(
            msg, (Z_UP, Z_DN)[side], conc, lambda which, v: put_padded(flow_ref, which, zz, v)
        )
    for y_side in range(2):
        for z_side in range(2):
            which = DIRS.index((0, 1 - 2 * y_side, 1 - 2 * z_side))
            names = (Y_UP, Y_DN)[y_side]
            msg = z_refs[z_side]
            z_row = (0, B - 1)[z_side]
            y_row = (0, B - 1)[y_side]
            from_y = read_row(y_refs[y_side], TRANS, z_row)
            from_z = read_row(msg, TRANS, y_row)
            get = [read_diag(msg, y_side, f) for f in range(TRANS + 1)]
            for tile in range(2):
                open_y = open_ref[pl.ds(open_at(1, y_side, tile) + z_row, 1), :]
                open_z = open_ref[pl.ds(open_at(3, z_side, tile) + y_row, 1), :]
                conc = jnp.where(open_y > 0, from_y[tile], get[TRANS][tile])
                conc = conc + jnp.where(open_z > 0, from_z[tile], get[NORM][tile])
                rho, vx, vy, vz = (get[k][tile] for k in range(RHO, RHO + 4))
                vz, base = lifted(conc, vx, vy, vz)
                v = relax(get[names.index(which)][tile], which, rho, vx, vy, vz, base)
                at = (0, B + 1)[z_side] * PADDED + tile * 32 + (7, 24)[y_side]
                flow_ref[which, pl.ds(at, 1), :] = v[:1]


def collide_flow(load, rho, vx, vy, vz, bits, conc, put):
    porous = is_open(bits, 0)
    vz = vz + jnp.where(porous, FORCE_GAIN * (conc - REST_CONC), 0.0)
    base = 1.0 - 1.5 * (vx * vx + vy * vy + vz * vz)
    keep = 1.0 - OMEGA_FLOW
    scaled = OMEGA_FLOW * rho
    f = load(0)
    put(0, jnp.where(porous, keep * f + (WEIGHTS[0] * scaled) * base, f))
    for i, j in PAIRS:
        a = along(i, vx, vy, vz)
        scale = WEIGHTS[i] * scaled
        even = scale * (base + 4.5 * (a * a))
        odd = scale * (3.0 * a)
        f, g = load(i), load(j)
        put(i, jnp.where(porous, keep * f + (even + odd), g))
        put(j, jnp.where(porous, keep * g + (even - odd), f))


def stream_flow(z, bits, flow_ref):
    post = [padded_plane(flow_ref, z + 1, 0, i) for i in range(19)]
    out = [post[0]]
    for which in range(1, 19):
        cx, cy, cz = DIRS[which]
        moved = post[which]
        if cy or cz:
            moved = padded_plane(flow_ref, z + 1 - cz, cy, which)
        if cx:
            moved = ring(moved, cx)
        out.append(jnp.where(is_open(bits, which), moved, post[OPP[which]]))
    return out


def first_kernel(
    dense_ref, right_ref, left_ref, pops_ref, side_ref, aux_ref, ring_ref,
    post_ref, ydn_ref, yup_ref, turn_ref,
):
    right, left = right_ref[...], left_ref[...]
    turn_ref[pl.ds(0, HALF, stride=8), :] = right
    turn_ref[pl.ds(HALF * 8, HALF, stride=8), :] = pltpu.roll(right, L - W, axis=1)
    turn_ref[pl.ds(7, HALF, stride=8), :] = left
    turn_ref[pl.ds(HALF * 8 + 7, HALF, stride=8), :] = pltpu.roll(left, W, axis=1)
    lane = lanes(8)
    near = (lane < W) | (lane >= L - W)

    def body(z, carry):
        solute = []
        for i in range(7):
            at = pl.multiple_of(i * 256 + z * B, B)
            side = [
                jnp.where(near, turn_blocks(turn_ref[pl.ds(at + 8 * k, 8), :]), 0.0)
                for k in range(2)
            ]
            solute.append(jnp.concatenate([dense_ref[pl.ds(at, B), :]] + side, axis=0))
        post = solute_collide(solute, [plane(aux_ref, z, k) for k in range(1, 4)])
        for i in range(7):
            post_ref[i, pl.ds(pl.multiple_of(z * PLANE, PLANE), PLANE), :] = post[i]
        return carry

    lax.fori_loop(0, B, body, 0, unroll=UNROLL)
    pops_refs = pops_ref, side_ref
    write_y_messages(pops_refs, post_ref, aux_ref, (ydn_ref, yup_ref), ring_ref=ring_ref)


def pull(z, refs, bits_ref, flow_ref, solute_ref):
    pops_ref, side_ref, post_ref, aux_ref = refs
    at = pl.ds(pl.multiple_of(z * PLANE, PLANE), PLANE)
    main = pl.ds(pl.multiple_of(z * B, B), B)
    bits = bits_ref[at, :]
    pops = stream_flow(z, bits, flow_ref)
    for i in range(19):
        pops_ref[i, main, :] = pops[i][:B]
        if side_ref is not None:
            side_ref[i, main, :] = pops[i][B:]
    if side_ref is None:
        return
    rho, velocity = moments(pops, jnp.where(is_open(bits, 0), 1.0, 0.0))
    for k, v in enumerate([rho] + velocity):
        aux_ref[k, at, :] = v
    post = solute_collide([solute_ref[i, at, :] for i in range(7)], velocity)
    for i in range(7):
        post_ref[i, at, :] = post[i]


def push(z, pops_refs, aux_ref, bits, solute, flow_ref):
    rho, vx, vy, vz = (plane(aux_ref, z, k) for k in range(4))
    collide_flow(
        lambda i: flow_plane(pops_refs, z, i), rho, vx, vy, vz, bits, sum(solute),
        lambda i, v: put_padded(flow_ref, i, z + 1, v),
    )


def put_solute(solute_ref, z, solute):
    for i in range(7):
        solute_ref[i, pl.ds(pl.multiple_of(z * PLANE, PLANE), PLANE), :] = solute[i]


def turn_plane(turn_ref, z, solute):
    for i in range(7):
        for half in range(2):
            at = pl.multiple_of(i * 256 + z * B + half * 8, 8)
            turn_ref[pl.ds(at, 8), :] = turn_blocks(solute[i][half * 8 : half * 8 + 8])


def core_kernel(first, *refs):
    pops_ref, side_ref, post_ref, aux_ref, bits_ref = refs[:5]
    ring_ref, refs = (refs[5], refs[6:]) if first else (None, refs[5:])
    zdn_ref, zup_ref, flow_ref, solute_ref = refs
    write_z_messages(
        (pops_ref, side_ref), post_ref, aux_ref, (zdn_ref, zup_ref), bits_ref, ring_ref
    )
    fills = [jnp.zeros((PLANE, L), F32)] * 2

    def body(z, carry):
        bits = plane(bits_ref, z)
        solute = stream_solute(
            z, post_ref, bits, fills, plane(post_ref, z - 1, 5), plane(post_ref, z + 1, 6)
        )
        put_solute(solute_ref, z, solute)
        push(z, (pops_ref, side_ref), aux_ref, bits, solute, flow_ref)
        return carry

    lax.fori_loop(1, B - 1, body, 0, unroll=UNROLL)


def fix_rows(pops_refs, post_ref, aux_ref, bits_ref, y_refs, flow_ref, solute_ref):
    for side in range(2):
        edge = (0, B - 1)[side]
        which = (3, 4)[side]
        bits = face_rows(bits_ref, edge)
        post = {i: face_rows(post_ref, edge, i) for i in (3, 4)}
        new = chosen(bits, read_field(y_refs[side], NORM), post, which)
        conc = new + sum(face_rows(solute_ref, edge, i) for i in range(7) if i != which)
        put_face(solute_ref, edge, new, which)

        def put(i, v):
            for tile in range(2):
                at = PADDED + tile * 32 + 8 + edge
                flow_ref[i, pl.ds(at, B, stride=PADDED), :] = v[tile * B : (tile + 1) * B]

        rho, vx, vy, vz = (face_rows(aux_ref, edge, k) for k in range(4))
        collide_flow(
            lambda i: flow_rows(pops_refs, edge, i), rho, vx, vy, vz, bits, conc, put
        )


def inner_kernel(*refs):
    bits_ref, open_ref, ylo_ref, yhi_ref = refs[6:10]
    *state, flow_ref, solute_ref = refs[10:]
    pops_ref, side_ref, post_ref, aux_ref = state
    y_refs = ylo_ref, yhi_ref
    fix_rows((pops_ref, side_ref), post_ref, aux_ref, bits_ref, y_refs, flow_ref, solute_ref)
    collide_y_halos(post_ref, open_ref, y_refs, None, flow_ref)

    def body(z, carry):
        pull(z, state, bits_ref, flow_ref, solute_ref)
        return carry

    lax.fori_loop(2, B - 2, body, 0, unroll=UNROLL)


def inner_last_kernel(*refs):
    pops_ref, side_ref, post_ref, aux_ref = refs[:4]
    bits_ref, open_ref, ylo_ref, yhi_ref, flow_ref, solute_ref, turn_ref = refs[6:]
    y_refs = ylo_ref, yhi_ref
    fix_rows((pops_ref, side_ref), post_ref, aux_ref, bits_ref, y_refs, flow_ref, solute_ref)

    def turn(z, carry):
        turn_plane(turn_ref, z, [plane(solute_ref, z, i) for i in range(7)])
        return carry

    lax.fori_loop(1, B - 1, turn, 0, unroll=UNROLL)
    collide_y_halos(post_ref, open_ref, y_refs, None, flow_ref)


def edge_solute(z, post_ref, bits_ref, y_refs, z_refs):
    fills = [spread8(read_row(y_refs[side], NORM, z)) for side in range(2)]
    below = read_field(z_refs[0], NORM) if z == 0 else plane(post_ref, z - 1, 5)
    above = read_field(z_refs[1], NORM) if z == B - 1 else plane(post_ref, z + 1, 6)
    return stream_solute(z, post_ref, plane(bits_ref, z), fills, below, above)


def edge_kernel(*refs):
    bits_ref, open_ref, ylo_ref, yhi_ref, zlo_ref, zhi_ref = refs[6:12]
    *state, flow_ref, solute_ref, ydn_ref, yup_ref = refs[12:]
    pops_ref, side_ref, post_ref, aux_ref = state
    y_refs, z_refs = (ylo_ref, yhi_ref), (zlo_ref, zhi_ref)
    for z in (0, B - 1):
        solute = edge_solute(z, post_ref, bits_ref, y_refs, z_refs)
        put_solute(solute_ref, z, solute)
        push(z, (pops_ref, side_ref), aux_ref, plane(bits_ref, z), solute, flow_ref)
    collide_y_halos(post_ref, open_ref, y_refs, z_refs, flow_ref)
    collide_z_halos(post_ref, open_ref, y_refs, z_refs, flow_ref)
    for z in (0, 1, B - 2, B - 1):
        pull(z, state, bits_ref, flow_ref, solute_ref)
    write_y_messages(
        (pops_ref, side_ref), post_ref, aux_ref, (ydn_ref, yup_ref), bits_ref=bits_ref
    )


def send_kernel(me_ref, slot_ref, *refs):
    post_ref, bits_ref, ylo_ref, yhi_ref, zlo_ref, zhi_ref = refs[2:8]
    solute_ref, turn_ref, *outs = refs[8:]
    for z in (0, B - 1):
        solute = edge_solute(z, post_ref, bits_ref, (ylo_ref, yhi_ref), (zlo_ref, zhi_ref))
        put_solute(solute_ref, z, solute)
        turn_plane(turn_ref, z, solute)
    fill_messages(me_ref[0], [slot_ref[0, 0, j] for j in range(8)], turn_ref, outs)


def last_kernel(*refs):
    pops_ref, side_ref, post_ref, aux_ref, flow_in, solute_ref, bits_ref, open_ref = refs[:8]
    y_refs, z_refs = refs[8:10], refs[10:12]
    out_ref, flow_ref = refs[12:]
    for z in (0, B - 1):
        solute = [plane(solute_ref, z, i) for i in range(7)]
        push(z, (pops_ref, side_ref), aux_ref, plane(bits_ref, z), solute, flow_ref)
    collide_y_halos(post_ref, open_ref, y_refs, z_refs, flow_ref)
    collide_z_halos(post_ref, open_ref, y_refs, z_refs, flow_ref)

    def body(z, carry):
        pull(z, (out_ref, None, None, None), bits_ref, flow_ref, None)
        return carry

    lax.fori_loop(0, B, body, 0, unroll=UNROLL)


def scatter_kernel(me_ref, slot_ref, *refs):
    receive(me_ref[0], [slot_ref[s] for s in range(8)], refs[:-1], refs[-1])


def neighbours(low, high, axis):
    count = lax.axis_size(axis)
    up = [(i, (i + 1) % count) for i in range(count)]
    down = [(i, (i - 1) % count) for i in range(count)]
    return lax.ppermute(high, axis, up), lax.ppermute(low, axis, down)


def exchange_blocks(own, up1, down1, up2, down2, up3, down3):
    def shifted(x, step):
        return lax.ppermute(x, "gz", [(i, (i + step) % 8) for i in range(8)])

    up1, down1 = shifted(up1, 1), shifted(down1, -1)
    up2, down2 = shifted(up2, 2), shifted(down2, -2)
    up3 = shifted(jnp.concatenate([up3, up1[ROW:]], axis=0), 3)
    down3 = shifted(jnp.concatenate([down3, down1[ROW:]], axis=0), -3)
    return own, up1, down1, up2, down2, up3, down3


def inside():
    flags = []
    for axis in ("gx", "gy", "gz"):
        at = lax.axis_index(axis)
        flags += [at > 0, at < lax.axis_size(axis) - 1]
    return jnp.stack(flags).astype(F32)


def with_edges(face, halos, row):
    slabs = face.shape[0] // B
    rows = [face] + [halo.reshape(slabs, B, L)[:, row] for halo in halos]
    pad = -slabs * (B + 2) % 8
    return jnp.concatenate(rows + [jnp.zeros((pad, L), F32)], axis=0)


def exchange_z(halos, zdn, zup):
    return neighbours(with_edges(zdn, halos, 0), with_edges(zup, halos, B - 1), "gz")


def shards(populations, solute_state, pore_mask, block_slot, slot_block):
    flags = inside()
    me = lax.axis_index("gz").astype(jnp.int32).reshape(1)
    turn = pltpu.VMEM((BLOCKROWS, L), F32)
    sent = tuple(held(n, L) for n in (ROW, ROW + HALF, ROW + HALF, ROW, ROW, ROW, ROW))
    state = solute_state.reshape(7, 8, 32, L).transpose(0, 2, 1, 3).reshape(BLOCKROWS, L)
    send = call(
        gather_kernel, sent, [SMEM, SMEM, HBM], [turn, pltpu.SemaphoreType.DMA], 1, 2 * 10**6
    )(me, slot_block, state)
    recv = exchange_blocks(*send)

    pops = populations.reshape(19, 256, L)
    mask = pore_mask.reshape(256, L)
    low, high = call(
        columns_kernel,
        (held(320, L),) * 2,
        [HBM] * 2,
        [
            pltpu.VMEM((19, 256, L), F32),
            pltpu.VMEM((256, L), jnp.int32),
            pltpu.SemaphoreType.DMA((20,)),
        ],
        10**6,
        13 * 10**6,
    )(pops, mask)
    left, right = neighbours(low, high, "gx")
    dims = ((19, 256, L), (19, 256, L), (ROWS, L), (4, ROWS, L), (PADROWS, L))
    pops, side, ring_mask, aux, mask, bits = call(
        ring_kernel,
        tuple(held(*d) for d in dims) + (held(ROWS, L, dtype=jnp.int32),),
        [SMEM, HBM] + [VMEM] * 3,
        [pltpu.SemaphoreType.DMA],
        10**6,
        20 * 10**6,
    )(flags, pops, mask, right, left)

    low, high = call(
        pick_kernel,
        (held(HALF, L),) * 2,
        [SMEM] * 2 + [VMEM] * 8,
        [pltpu.VMEM((ROW, L), F32)],
        1,
        10**6,
        keep=True,
    )(me, block_slot, *recv, bits)
    left, right = neighbours(low, high, "gx")
    dense = call(
        spread_kernel, held(BLOCKROWS, L), [SMEM] * 2 + [VMEM] * 7, [turn], 10**6, 10**7, keep=True
    )(me, block_slot, *recv)
    message = held((SIDES + MASK + 1) * B, L)
    post, ydn, yup = call(
        first_kernel,
        (held(7, ROWS, L),) + (message,) * 2,
        [VMEM] * 7,
        [turn],
        10**7,
        10**7,
        keep=True,
    )(dense, right, left, pops, side, aux, ring_mask)

    states = (held(19, 256, L), held(19, 256, L), held(7, ROWS, L), held(4, ROWS, L))
    works = (held(19, PADROWS, L), held(7, ROWS, L))
    opens_out = (held(PADROWS, L), held(ROWS, L, dtype=jnp.int32), held(PLANE * 8, L))
    message = held((SIDES + MASK) * B, L)
    state = (pops, side, post, aux)
    for step in range(STEPS):
        last = step == STEPS - 1
        y_halos = neighbours(ydn, yup, "gy")
        zdn, zup, *work = call(
            functools.partial(core_kernel, step == 0),
            (held(*ydn.shape),) * 2 + works,
            [VMEM] * (6 if step == 0 else 5),
            [],
            10**7,
            10**7,
            keep=True,
        )(*state, bits, *([ring_mask] if step == 0 else []))
        z_halos = exchange_z(y_halos, zdn, zup)
        if step == 0:
            mask, bits, opens = call(
                side_open_kernel,
                opens_out,
                [SMEM] + [VMEM] * 4,
                [],
                10**6,
                10**6,
                aliases={3: 0, 4: 1},
                keep=True,
            )(flags, *y_halos, mask, bits)
        if last:
            break
        moved = call(
            inner_kernel,
            states + works,
            [VMEM] * 10,
            [],
            10**7,
            10**7,
            aliases={i: i for i in range(6)},
            keep=True,
        )(*state, *work, bits, opens, *y_halos)
        if step == 0:
            mask, bits, opens = call(
                edge_open_kernel,
                opens_out,
                [SMEM] + [VMEM] * 5,
                [],
                10**6,
                10**6,
                aliases={3: 0, 4: 1, 5: 2},
                keep=True,
            )(flags, *z_halos, mask, bits, opens)
        *state, _, _, ydn, yup = call(
            edge_kernel,
            states + works + (message, message),
            [VMEM] * 12,
            [],
            10**7,
            10**7,
            aliases={i: i for i in range(6)},
            keep=True,
        )(*moved, bits, opens, *y_halos, *z_halos)

    flow, solute, turned = call(
        inner_last_kernel,
        works + (held(BLOCKROWS, L),),
        [VMEM] * 10,
        [],
        10**7,
        10**7,
        aliases={4: 0, 5: 1},
        keep=True,
    )(*state, *work, bits, opens, *y_halos)
    solute, _, *send = call(
        send_kernel,
        (works[1], held(BLOCKROWS, L)) + sent,
        [SMEM] * 2 + [VMEM] * 8,
        [],
        10**6,
        10**6,
        aliases={2: 0, 3: 1},
        keep=True,
    )(me, block_slot, solute, turned, state[2], bits, *y_halos, *z_halos)
    recv = exchange_blocks(*send)
    pops, _ = call(
        last_kernel,
        (shape(19, 256, L), works[0]),
        [VMEM] * 12,
        [],
        10**7,
        10**7,
        aliases={4: 1},
        keep=True,
    )(*state, flow, solute, bits, opens, *y_halos, *z_halos)
    out = call(scatter_kernel, shape(BLOCKROWS, L), [SMEM] * 2 + [VMEM] * 7, [], 1, 2 * 10**6)(
        me, slot_block, *recv
    )
    new_solute = out.reshape(7, 32, 8, L).transpose(0, 2, 1, 3).reshape(7, 8, 4096)
    return pops.reshape(19, B, B, L), new_solute


def solution(mesh):
    in_specs = (
        P(None, "gz", "gy", "gx"),
        P(None, ("gx", "gy", "gz"), None),
        P("gz", "gy", "gx"),
        P("gz", "gy", "gx"),
        P(("gx", "gy", "gz")),
    )
    out_specs = (P(None, "gz", "gy", "gx"), P(None, ("gx", "gy", "gz"), None))
    return jax.shard_map(shards, mesh=mesh, in_specs=in_specs, out_specs=out_specs, check_vma=False)
```

```python
import functools

import jax
import jax.numpy as jnp
from jax import lax
from jax.experimental import pallas as pl
from jax.experimental.pallas import tpu as pltpu
from jax.sharding import PartitionSpec as P

STEPS = 4
DIRS = [
    (0, 0, 0),
    (1, 0, 0),
    (-1, 0, 0),
    (0, 1, 0),
    (0, -1, 0),
    (0, 0, 1),
    (0, 0, -1),
    (1, 1, 0),
    (-1, -1, 0),
    (1, -1, 0),
    (-1, 1, 0),
    (1, 0, 1),
    (-1, 0, -1),
    (1, 0, -1),
    (-1, 0, 1),
    (0, 1, 1),
    (0, -1, -1),
    (0, 1, -1),
    (0, -1, 1),
]
OPP = [DIRS.index((-a, -b, -c)) for a, b, c in DIRS]
PAIRS = [(i, OPP[i]) for i in range(1, 19, 2)]
WEIGHTS = [1.0 / 3.0] + [1.0 / 18.0] * 6 + [1.0 / 36.0] * 12
OMEGA_FLOW = 1.2
FORCE_GAIN = 0.02
REST_CONC = 8.0
Y_UP = [i for i in range(19) if DIRS[i][1] == 1]
Y_DN = [i for i in range(19) if DIRS[i][1] == -1]
Z_UP = [i for i in range(19) if DIRS[i][2] == 1]
Z_DN = [i for i in range(19) if DIRS[i][2] == -1]
RHO, NORM, TRANS, MASK = 5, 9, 10, 11
SIDES = 2
UNROLL = 2
B = 16
L = 128
W = 8
PLANE = 2 * B
ROWS = B * PLANE
PADDED = 64
PADROWS = (B + 2) * PADDED
ROW = 7 * 32
HALF = ROW // 2
BLOCKROWS = ROW * 8
F32 = jnp.float32
VMEM = pl.BlockSpec(memory_space=pltpu.VMEM)
SMEM = pl.BlockSpec(memory_space=pltpu.SMEM)
HBM = pl.BlockSpec(memory_space=pltpu.HBM)


def call(
    kernel, out_shape, in_specs, scratch, flops, nbytes, aliases={}, keep=False, out_specs=None
):
    run = pl.pallas_call(
        kernel,
        out_shape=out_shape,
        in_specs=in_specs,
        out_specs=out_specs or jax.tree.map(lambda _: VMEM, out_shape),
        scratch_shapes=scratch,
        input_output_aliases=aliases,
        compiler_params=pltpu.CompilerParams(vmem_limit_bytes=20 * 1024 * 1024),
        cost_estimate=pl.CostEstimate(flops=flops, bytes_accessed=nbytes, transcendentals=0),
    )

    def place(x, spec):
        if spec is HBM or (keep and spec is VMEM):
            return pltpu.with_memory_space_constraint(x, spec.memory_space)
        return x

    def placed(*args):
        return run(*map(place, args, in_specs))

    return placed


def shape(*dims):
    return jax.ShapeDtypeStruct(dims, F32)


def held(*dims, dtype=F32):
    return pltpu.VMEM(dims, dtype)


def lanes(rows):
    return lax.broadcasted_iota(jnp.int32, (rows, L), 1)


def row_ids(rows):
    return lax.broadcasted_iota(jnp.int32, (rows, L), 0)


def ring(v, step):
    rolled = pltpu.roll(v, step % L, axis=1)
    other = jnp.concatenate([rolled[B:], rolled[:B]], axis=0)
    return jnp.where(lanes(PLANE) == (0 if step > 0 else L - 1), other, rolled)


def halves(main, side):
    return jnp.concatenate([main, side], axis=0)


def shift_rows(v, step, fill):
    rolled = pltpu.roll(v, step % PLANE, axis=0)
    return jnp.where(row_ids(PLANE) % B == (0 if step > 0 else B - 1), fill, rolled)


def is_open(bits, which):
    return (bits & (1 << which)) != 0


def along(which, vx, vy, vz):
    total = None
    for sign, part in zip(DIRS[which], (vx, vy, vz)):
        if sign != 0:
            if total is None:
                total = part if sign > 0 else -part
            else:
                total = total + part if sign > 0 else total - part
    return total


def moments(pops, porous):
    rho = pops[0]
    for which in range(1, 19):
        rho = rho + pops[which]
    scale = porous / rho
    parts = []
    for coord in range(3):
        plus = sum(pops[i] for i in range(19) if DIRS[i][coord] == 1)
        minus = sum(pops[i] for i in range(19) if DIRS[i][coord] == -1)
        parts.append((plus - minus) * scale)
    return rho, parts


def solute_collide(solute, velocity):
    conc = sum(solute)
    out = [-0.5 * solute[0] + 0.375 * conc]
    base = 0.1875 * conc
    for coord in range(3):
        turn = 0.75 * conc * velocity[coord]
        out.append((base - 0.5 * solute[1 + 2 * coord]) + turn)
        out.append((base - 0.5 * solute[2 + 2 * coord]) - turn)
    return out


def chosen(bits, moved, post, which):
    return jnp.where(
        is_open(bits, which),
        moved,
        jnp.where(is_open(bits, 0), post[OPP[which]], post[which]),
    )


def turn_blocks(x):
    row, lane = row_ids(8), lanes(8)
    x = take(x, (lane - B * row) & (L - 1), 1)
    x = take(x, (lane // B - row) & 7, 0)
    return take(x, (lane + B * row) & (L - 1), 1)


def take(x, index, axis):
    return jnp.take_along_axis(x, index, axis=axis, mode="promise_in_bounds")


PARTS = (
    (0, 0, 0, ROW, 0),
    (7, 1, 0, ROW, 0),
    (1, 2, 0, ROW, 0),
    (6, 3, 0, ROW, 0),
    (2, 4, 0, ROW, 0),
    (5, 5, 0, ROW, 0),
    (3, 6, 0, ROW, 0),
    (4, 5, ROW, HALF, 0),
    (4, 6, ROW, HALF, HALF),
)


def find(slots, home):
    found = jnp.int32(-1)
    for k, slot in enumerate(slots):
        found = jnp.where((slot >= 0) & (slot // 8 == home), k, found)
    return found


def fill_messages(me, slots, blocks_ref, outs, ready=lambda comp: None):
    own, up1, down1, up2, down2, up3, down3 = outs
    places = ((0, own), (1, up1), (7, down1), (2, up2), (6, down2), (3, up3), (5, down3))
    slot_of = [jnp.maximum(find(slots, (me + off) & 7), 0) for off in range(8)]
    for comp in range(7):
        ready(comp)
        for off, ref in places:
            at = comp * 256 + slot_of[off]
            ref[pl.ds(comp * 32, 32), :] = blocks_ref[pl.ds(at, 32, stride=8), :]
    up1[pl.ds(ROW, HALF), :] = blocks_ref[pl.ds(slot_of[4], HALF, stride=8), :]
    down1[pl.ds(ROW, HALF), :] = blocks_ref[pl.ds(HALF * 8 + slot_of[4], HALF, stride=8), :]


def receive(me, slots, refs, out_ref):
    for k, slot in enumerate(slots):

        @pl.when(slot < 0)
        def _():
            out_ref[pl.ds(k, ROW, stride=8), :] = jnp.zeros((ROW, L), F32)

    for off, k, at, count, first in PARTS:
        slot = find(slots, (me + off) & 7)

        @pl.when(slot >= 0)
        def _():
            out_ref[pl.ds(first * 8 + slot, count, stride=8), :] = refs[k][pl.ds(at, count), :]


def gather_kernel(me_ref, slot_ref, state_ref, *refs):
    *outs, blocks_ref, sems = refs

    def load(comp):
        rows = pl.ds(comp * 256, 256)
        return pltpu.make_async_copy(state_ref.at[rows], blocks_ref.at[rows], sems.at[comp])

    for comp in range(7):
        load(comp).start()
    slots = [slot_ref[s] for s in range(8)]
    fill_messages(me_ref[0], slots, blocks_ref, outs, lambda comp: load(comp).wait())


def pick_kernel(me_ref, slot_ref, *refs):
    low_ref, high_ref, hold_ref = refs[-3:]
    outer = (lanes(HALF) & 8) == 0
    for tile in (0, 7):
        slot = slot_ref[0, 0, tile]

        @pl.when(slot < 0)
        def _():
            hold_ref[...] = jnp.zeros((ROW, L), F32)

        for off, k, at, count, first in PARTS:

            @pl.when((slot >= 0) & (slot // 8 == ((me_ref[0] + off) & 7)))
            def _():
                hold_ref[pl.ds(first, count), :] = refs[k][pl.ds(at, count), :]

        one, two = hold_ref[pl.ds(0, HALF), :], hold_ref[pl.ds(HALF, HALF), :]
        if tile == 0:
            low_ref[...] = jnp.where(outer, one, pltpu.roll(two, W, axis=1))
        else:
            high_ref[...] = jnp.where(outer, pltpu.roll(two, L - W, axis=1), one)


def spread_kernel(me_ref, slot_ref, *refs):
    *blocks, dense_ref, turn_ref = refs
    receive(me_ref[0], [slot_ref[0, 0, tile] for tile in range(8)], blocks, turn_ref)

    def body(group, carry):
        for i in range(32):
            at = pl.multiple_of(group * 256 + i * 8, 8)
            dense_ref[pl.ds(at, 8), :] = turn_blocks(turn_ref[pl.ds(at, 8), :])
        return carry

    lax.fori_loop(0, BLOCKROWS // 256, body, 0)


def pack_columns(load, low_ref, high_ref, at):
    lane = lanes(8) // W
    low = jnp.zeros((8, L), F32)
    high = jnp.zeros((8, L), F32)
    for i in range(16):
        x = load(i)
        low = jnp.where(lane == i, x if i == 0 else pltpu.roll(x, W * i, axis=1), low)
        turn = (W + W * i) % L
        high = jnp.where(lane == i, x if turn == 0 else pltpu.roll(x, turn, axis=1), high)
    at = pl.multiple_of(at, 8)
    low_ref[pl.ds(at, 8), :] = low
    high_ref[pl.ds(at, 8), :] = high


def columns_kernel(pops_in, mask_in, low_ref, high_ref, pops_ref, mask_ref, sems):
    load = pltpu.make_async_copy(mask_in, mask_ref, sems.at[19])
    load.start()

    def part(comp):
        return pltpu.make_async_copy(pops_in.at[comp], pops_ref.at[comp], sems.at[comp])

    for comp in range(19):
        part(comp).start()

    def rows(start, i):
        return pl.ds(pl.multiple_of(start + i * 8, 8), 8)

    for comp in range(19):
        part(comp).wait()
        for half in range(2):
            pack_columns(
                lambda i: pops_ref[comp, rows(half * 128, i), :],
                low_ref,
                high_ref,
                (2 * comp + half) * 8,
            )
    load.wait()
    for half in range(2):
        pack_columns(
            lambda i: mask_ref[rows(half * 128, i), :].astype(F32),
            low_ref,
            high_ref,
            (38 + half) * 8,
        )


def unpack_columns(right, left, i):
    a = right if i == 0 else pltpu.roll(right, L - W * i, axis=1)
    b = left if i == 15 else pltpu.roll(left, L - W - W * i, axis=1)
    return jnp.where(lanes(8) < L // 2, a, b)


def ring_kernel(
    flag_ref, pops_in, mask_ref, right_ref, left_ref,
    pops_ref, side_ref, ring_ref, aux_ref, mask_out, bits_ref, sem,
):
    load = pltpu.make_async_copy(pops_in, pops_ref, sem)
    load.start()

    def body(group, carry):
        at = pl.ds(pl.multiple_of(group * 8, 8), 8)
        right, left = right_ref[at, :], left_ref[at, :]
        for i in range(16):
            row = pl.multiple_of((group % 2) * 128 + i * 8, 8)
            side_ref[group // 2, pl.ds(row, 8), :] = unpack_columns(right, left, i)
        return carry

    lax.fori_loop(0, 38, body, 0, unroll=UNROLL)
    lane = lanes(8)
    inside = jnp.where(lane < W, flag_ref[1], jnp.where(lane >= L - W, flag_ref[0], 0.0))
    for group in range(2):
        right, left = right_ref[pl.ds(304 + group * 8, 8), :], left_ref[pl.ds(304 + group * 8, 8), :]
        for i in range(16):
            z = group * 8 + i // 2
            row = z * PLANE + (i % 2) * 8
            ring_ref[pl.ds(row, 8), :] = mask_ref[pl.ds(group * 128 + i * 8, 8), :].astype(F32)
            ring_ref[pl.ds(row + B, 8), :] = unpack_columns(right, left, i) * inside
    mask_out[...] = jnp.zeros_like(mask_out)
    for z in range(B):
        put_rows(mask_out, z + 1, ring_ref[pl.ds(z * PLANE, PLANE), :])

    load.wait()

    def flow(z, carry):
        set_bits(mask_out, bits_ref, z)
        pops = [flow_plane((pops_ref, side_ref), z, i) for i in range(19)]
        rho, velocity = moments(pops, plane(ring_ref, z))
        for k, v in enumerate([rho] + velocity):
            aux_ref[k, pl.ds(pl.multiple_of(z * PLANE, PLANE), PLANE), :] = v
        return carry

    lax.fori_loop(0, B, flow, 0, unroll=UNROLL)


def plane(ref, z, *lead):
    return ref[(*lead, pl.ds(pl.multiple_of(z * PLANE, PLANE), PLANE), slice(None))]


def put_face(ref, row, v, *lead):
    for tile in range(2):
        at = pl.ds(tile * B + row, B, stride=PLANE)
        ref[(*lead, at, slice(None))] = v[tile * B : (tile + 1) * B]


def flow_plane(refs, z, which):
    at = pl.ds(pl.multiple_of(z * B, B), B)
    return halves(refs[0][which, at, :], refs[1][which, at, :])


def flow_rows(refs, row, which):
    at = pl.ds(row, B, stride=B)
    return halves(refs[0][which, at, :], refs[1][which, at, :])


def padded_plane(ref, zz, shift, *lead):
    at = zz * PADDED + 8
    return halves(
        ref[(*lead, pl.ds(at - shift, B), slice(None))],
        ref[(*lead, pl.ds(at + 32 - shift, B), slice(None))],
    )


def put_rows(ref, zz, v):
    ref[pl.ds(zz * PADDED + 8, B), :] = v[:B]
    ref[pl.ds(zz * PADDED + 40, B), :] = v[B:]


def put_padded(ref, comp, zz, v):
    at = zz * PADDED + 8
    if not isinstance(zz, int):
        at = pl.multiple_of(at, 8)
    ref[comp, pl.ds(at, B), :] = v[:B]
    ref[comp, pl.ds(at + 32, B), :] = v[B:]


def face_rows(ref, row, *lead):
    return halves(
        ref[(*lead, pl.ds(row, B, stride=PLANE), slice(None))],
        ref[(*lead, pl.ds(B + row, B, stride=PLANE), slice(None))],
    )


def set_bits(mask_ref, bits_ref, z):
    here = padded_plane(mask_ref, z + 1, 0)
    bits = jnp.where(here > 0, 1, 0)
    for which in range(1, 19):
        cx, cy, cz = DIRS[which]
        source = padded_plane(mask_ref, z + 1 - cz, cy)
        if cx:
            source = ring(source, cx)
        bits = bits + jnp.where(source * here > 0, 1 << which, 0)
    bits_ref[pl.ds(pl.multiple_of(z * PLANE, PLANE), PLANE), :] = bits


def side_open_kernel(
    flag_ref, ylo_ref, yhi_ref, mask_in, bits_in, mask_ref, bits_ref, open_ref
):
    for side in range(2):
        halo = read_field((ylo_ref, yhi_ref)[side], MASK) * flag_ref[2 + side]
        edge, row = ((0, 7), (B - 1, 24))[side]
        own = []
        for tile in range(2):
            part = halo[tile * B : (tile + 1) * B]
            at = PADDED + tile * 32
            mask_ref[pl.ds(at + row, B, stride=PADDED), :] = part
            own.append(mask_ref[pl.ds(at + 8 + edge, B, stride=PADDED), :])
            put_open(open_ref, 0, side, tile, part * own[tile])
        own = halves(*own)
        bits = face_rows(bits_ref, edge)
        for which in (Y_UP, Y_DN)[side]:
            cx, _, cz = DIRS[which]
            source = halo
            if cz:
                source = pltpu.roll(source, cz % PLANE, axis=0)
            if cx:
                source = ring(source, cx)
            bits = bits + jnp.where(source * own > 0, 1 << which, 0)
        put_face(bits_ref, edge, bits)


def edge_open_kernel(
    flag_ref, zlo_ref, zhi_ref, mask_in, bits_in, open_in, mask_ref, bits_ref, open_ref
):
    row = row_ids(B)
    for side in range(2):
        z_ref, zz = (zlo_ref, zhi_ref)[side], (0, B + 1)[side]
        put_rows(mask_ref, zz, read_field(z_ref, MASK) * flag_ref[4 + side])
        for y_side in range(2):
            pair = read_diag(z_ref, y_side, MASK)
            for tile in range(2):
                at = zz * PADDED + tile * 32 + (7, 24)[y_side]
                scale = flag_ref[4 + side] * flag_ref[2 + y_side]
                mask_ref[pl.ds(at, 1), :] = pair[tile][:1] * scale

    def body(k, carry):
        set_bits(mask_ref, bits_ref, k * (B - 1))
        return carry

    lax.fori_loop(0, 2, body, 0)
    for tile in range(2):
        for side in range(2):
            edge = tile * 32 + (7, 24)[side]
            halo = mask_ref[pl.ds(PADDED + edge, B, stride=PADDED), :]
            first = mask_ref[pl.ds(edge, 1), :]
            last = mask_ref[pl.ds(PADROWS - PADDED + edge, 1), :]
            ends = jnp.where(row == 0, halo * first, jnp.where(row == B - 1, halo * last, 0.0))
            put_open(open_ref, 1, side, tile, ends)
            at = (0, B + 1)[side] * PADDED + tile * 32
            near = (1, B)[side]
            halo = mask_ref[pl.ds(at + 8, B), :]
            own = mask_ref[pl.ds(near * PADDED + tile * 32 + 8, B), :]
            first = mask_ref[pl.ds(at + 7, 1), :]
            last = mask_ref[pl.ds(at + 24, 1), :]
            ends = jnp.where(row == 0, halo * first, jnp.where(row == B - 1, halo * last, 0.0))
            put_open(open_ref, 2, side, tile, halo * own)
            put_open(open_ref, 3, side, tile, ends)


def open_at(kind, side, tile):
    return ((kind * 2 + side) * 2 + tile) * B


def put_open(ref, kind, side, tile, v):
    ref[pl.ds(open_at(kind, side, tile), B), :] = v


def get_open(ref, kind, side):
    return ref[pl.ds(open_at(kind, side, 0), PLANE), :] > 0


def write_message(out_ref, fields):
    lane = lanes(B) // 16
    for slab in range(SIDES):
        packed = jnp.zeros((B, L), F32)
        for k, field in enumerate(fields[slab * 8 : slab * 8 + 8]):
            turn = (W + 16 * k) % L
            packed = jnp.where(lane == k, pltpu.roll(field[B:], turn, axis=1), packed)
        out_ref[pl.ds(slab * B, B), :] = packed
    for f, field in enumerate(fields):
        out_ref[pl.ds((SIDES + f) * B, B), :] = field[:B]


def unpack_side(packed, f):
    return pltpu.roll(packed, L - W - 16 * (f % 8), axis=1)


def read_field(ref, f):
    side = ref[pl.ds(f // 8 * B, B), :]
    return halves(ref[pl.ds((SIDES + f) * B, B), :], unpack_side(side, f))


def read_row(ref, f, row):
    main = jnp.broadcast_to(ref[pl.ds((SIDES + f) * B + row, 1), :], (8, L))
    side = jnp.broadcast_to(ref[pl.ds(f // 8 * B + row, 1), :], (8, L))
    return main, unpack_side(side, f)


def read_diag(ref, side, f):
    slabs = ref.shape[0] // (B + 2)
    base = slabs * B + side * slabs
    main = jnp.broadcast_to(ref[pl.ds(base + SIDES + f, 1), :], (8, L))
    packed = jnp.broadcast_to(ref[pl.ds(base + f // 8, 1), :], (8, L))
    return main, unpack_side(packed, f)


def spread8(pair):
    return halves(
        jnp.concatenate([pair[0], pair[0]], axis=0), jnp.concatenate([pair[1], pair[1]], axis=0)
    )


def partial_sum(f, inner, is_open, outward, in_rows):
    row = row_ids(PLANE) % B
    total = f[0]
    total = total + jnp.where(is_open(1), ring(f[1], 1), f[2])
    total = total + jnp.where(is_open(2), ring(f[2], -1), f[1])
    up, down = in_rows
    moved = jnp.where(is_open(up), pltpu.roll(f[up], 1, axis=0), f[down])
    total = total + jnp.where(row == 0, 0.0, moved)
    moved = jnp.where(is_open(down), pltpu.roll(f[down], PLANE - 1, axis=0), f[up])
    total = total + jnp.where(row == B - 1, 0.0, moved)
    return total + jnp.where(is_open(outward), inner, f[OPP[outward]])


def open_bits(bits):
    return lambda which: is_open(bits, which)


def open_mask(own, inner, in_rows):
    shifted = {
        1: ring(own, 1),
        2: ring(own, -1),
        in_rows[0]: pltpu.roll(own, 1, axis=0),
        in_rows[1]: pltpu.roll(own, PLANE - 1, axis=0),
    }
    return lambda which: shifted.get(which, inner) > 0


def write_y_messages(pops_refs, post_ref, aux_ref, y_refs, bits_ref=None, ring_ref=None):
    row = row_ids(PLANE) % B
    for side in range(2):
        names = (Y_DN, Y_UP)[side]
        edge, inner = ((0, 1), (B - 1, B - 2))[side]
        normal = (4, 3)[side]
        if ring_ref is None:
            opened = open_bits(face_rows(bits_ref, edge))
        else:
            opened = open_mask(face_rows(ring_ref, edge), face_rows(ring_ref, inner), (5, 6))
        f = [face_rows(post_ref, edge, i) for i in range(7)]
        part = partial_sum(f, face_rows(post_ref, inner, normal), opened, normal, (5, 6))
        fields = [flow_rows(pops_refs, edge, c) for c in names]
        fields += [face_rows(aux_ref, edge, k) for k in range(4)]
        fields[-1] = fields[-1] + FORCE_GAIN * (part - REST_CONC)
        fields += [f[normal], jnp.where(row == 0, f[6], f[5])]
        if ring_ref is not None:
            fields.append(face_rows(ring_ref, edge))
        write_message(y_refs[side], fields)


def write_z_messages(pops_refs, post_ref, aux_ref, z_refs, bits_ref=None, ring_ref=None):
    row = row_ids(PLANE) % B
    for side in range(2):
        names = (Z_DN, Z_UP)[side]
        edge, inner = ((0, 1), (B - 1, B - 2))[side]
        normal = (6, 5)[side]
        if ring_ref is None:
            opened = open_bits(plane(bits_ref, edge))
        else:
            opened = open_mask(plane(ring_ref, edge), plane(ring_ref, inner), (3, 4))
        f = [plane(post_ref, edge, i) for i in range(7)]
        part = partial_sum(f, plane(post_ref, inner, normal), opened, normal, (3, 4))
        fields = [flow_plane(pops_refs, edge, c) for c in names]
        fields += [plane(aux_ref, edge, k) for k in range(4)]
        fields[-1] = fields[-1] + FORCE_GAIN * (part - REST_CONC)
        fields += [f[normal], jnp.where(row == 0, f[4], f[3])]
        if ring_ref is not None:
            fields.append(plane(ring_ref, edge))
        write_message(z_refs[side], fields)


def relax(f, which, rho, vx, vy, vz, base):
    a = along(which, vx, vy, vz)
    scale = (OMEGA_FLOW * WEIGHTS[which]) * rho
    return (1.0 - OMEGA_FLOW) * f + scale * (base + a * (3.0 + 4.5 * a))


def lifted(conc, vx, vy, vz):
    vz = vz + FORCE_GAIN * conc
    return vz, 1.0 - 1.5 * (vx * vx + vy * vy + vz * vz)


def stream_solute(z, post_ref, bits, fills, below, above):
    post = [plane(post_ref, z, i) for i in range(7)]
    moved = [
        None,
        ring(post[1], 1),
        ring(post[2], -1),
        shift_rows(post[3], 1, fills[0]),
        shift_rows(post[4], -1, fills[1]),
        below,
        above,
    ]
    return [post[0]] + [chosen(bits, moved[i], post, i) for i in range(1, 7)]


def collide_face(msg, names, conc, put):
    rho, vx, vy, vz = (read_field(msg, k) for k in range(RHO, RHO + 4))
    vz, base = lifted(conc, vx, vy, vz)
    for k, which in enumerate(names):
        put(which, relax(read_field(msg, k), which, rho, vx, vy, vz, base))


def collide_y_halos(post_ref, open_ref, y_refs, z_refs, flow_ref):
    row = row_ids(PLANE) % B
    for side in range(2):
        msg = y_refs[side]
        own = face_rows(post_ref, (0, B - 1)[side], (4, 3)[side])
        conc = jnp.where(get_open(open_ref, 0, side), own, read_field(msg, NORM))
        if z_refs is not None:
            ends = jnp.where(
                row == 0,
                spread8(read_diag(z_refs[0], side, TRANS)),
                spread8(read_diag(z_refs[1], side, TRANS)),
            )
            ends = jnp.where(get_open(open_ref, 1, side), ends, read_field(msg, TRANS))
            conc = conc + ends
        at = PADDED + (7, 24)[side]

        def put(which, v):
            for tile in range(2):
                part = v[tile * B : (tile + 1) * B]
                if z_refs is None:
                    flow_ref[which, pl.ds(at + tile * 32, B, stride=PADDED), :] = part
                else:
                    for z in (0, B - 1):
                        flow_ref[which, pl.ds(at + tile * 32 + z * PADDED, 1), :] = part[z : z + 1]

        collide_face(msg, (Y_UP, Y_DN)[side], conc, put)


def collide_z_halos(post_ref, open_ref, y_refs, z_refs, flow_ref):
    row = row_ids(PLANE) % B
    for side in range(2):
        msg = z_refs[side]
        own = plane(post_ref, (0, B - 1)[side], (6, 5)[side])
        ends = jnp.where(
            row == 0, spread8(read_diag(msg, 0, NORM)), spread8(read_diag(msg, 1, NORM))
        )
        ends = jnp.where(get_open(open_ref, 3, side), ends, read_field(msg, TRANS))
        conc = jnp.where(get_open(open_ref, 2, side), own, read_field(msg, NORM))
        conc = conc + jnp.where((row == 0) | (row == B - 1), ends, 0.0)
        zz = (0, B + 1)[side]
        collide_face(
            msg, (Z_UP, Z_DN)[side], conc, lambda which, v: put_padded(flow_ref, which, zz, v)
        )
    for y_side in range(2):
        for z_side in range(2):
            which = DIRS.index((0, 1 - 2 * y_side, 1 - 2 * z_side))
            names = (Y_UP, Y_DN)[y_side]
            msg = z_refs[z_side]
            z_row = (0, B - 1)[z_side]
            y_row = (0, B - 1)[y_side]
            from_y = read_row(y_refs[y_side], TRANS, z_row)
            from_z = read_row(msg, TRANS, y_row)
            get = [read_diag(msg, y_side, f) for f in range(TRANS + 1)]
            for tile in range(2):
                open_y = open_ref[pl.ds(open_at(1, y_side, tile) + z_row, 1), :]
                open_z = open_ref[pl.ds(open_at(3, z_side, tile) + y_row, 1), :]
                conc = jnp.where(open_y > 0, from_y[tile], get[TRANS][tile])
                conc = conc + jnp.where(open_z > 0, from_z[tile], get[NORM][tile])
                rho, vx, vy, vz = (get[k][tile] for k in range(RHO, RHO + 4))
                vz, base = lifted(conc, vx, vy, vz)
                v = relax(get[names.index(which)][tile], which, rho, vx, vy, vz, base)
                at = (0, B + 1)[z_side] * PADDED + tile * 32 + (7, 24)[y_side]
                flow_ref[which, pl.ds(at, 1), :] = v[:1]


def collide_flow(load, rho, vx, vy, vz, bits, conc, put):
    porous = is_open(bits, 0)
    vz = vz + jnp.where(porous, FORCE_GAIN * (conc - REST_CONC), 0.0)
    base = 1.0 - 1.5 * (vx * vx + vy * vy + vz * vz)
    keep = 1.0 - OMEGA_FLOW
    scaled = OMEGA_FLOW * rho
    f = load(0)
    put(0, jnp.where(porous, keep * f + (WEIGHTS[0] * scaled) * base, f))
    for i, j in PAIRS:
        a = along(i, vx, vy, vz)
        scale = WEIGHTS[i] * scaled
        even = scale * (base + 4.5 * (a * a))
        odd = scale * (3.0 * a)
        f, g = load(i), load(j)
        put(i, jnp.where(porous, keep * f + (even + odd), g))
        put(j, jnp.where(porous, keep * g + (even - odd), f))


def stream_flow(z, bits, flow_ref):
    post = [padded_plane(flow_ref, z + 1, 0, i) for i in range(19)]
    out = [post[0]]
    for which in range(1, 19):
        cx, cy, cz = DIRS[which]
        moved = post[which]
        if cy or cz:
            moved = padded_plane(flow_ref, z + 1 - cz, cy, which)
        if cx:
            moved = ring(moved, cx)
        out.append(jnp.where(is_open(bits, which), moved, post[OPP[which]]))
    return out


def first_kernel(
    dense_ref, right_ref, left_ref, pops_ref, side_ref, aux_ref, ring_ref,
    post_ref, ydn_ref, yup_ref, turn_ref,
):
    right, left = right_ref[...], left_ref[...]
    turn_ref[pl.ds(0, HALF, stride=8), :] = right
    turn_ref[pl.ds(HALF * 8, HALF, stride=8), :] = pltpu.roll(right, L - W, axis=1)
    turn_ref[pl.ds(7, HALF, stride=8), :] = left
    turn_ref[pl.ds(HALF * 8 + 7, HALF, stride=8), :] = pltpu.roll(left, W, axis=1)
    lane = lanes(8)
    near = (lane < W) | (lane >= L - W)

    def body(z, carry):
        solute = []
        for i in range(7):
            at = pl.multiple_of(i * 256 + z * B, B)
            side = [
                jnp.where(near, turn_blocks(turn_ref[pl.ds(at + 8 * k, 8), :]), 0.0)
                for k in range(2)
            ]
            solute.append(jnp.concatenate([dense_ref[pl.ds(at, B), :]] + side, axis=0))
        post = solute_collide(solute, [plane(aux_ref, z, k) for k in range(1, 4)])
        for i in range(7):
            post_ref[i, pl.ds(pl.multiple_of(z * PLANE, PLANE), PLANE), :] = post[i]
        return carry

    lax.fori_loop(0, B, body, 0, unroll=2 * UNROLL)
    pops_refs = pops_ref, side_ref
    write_y_messages(pops_refs, post_ref, aux_ref, (ydn_ref, yup_ref), ring_ref=ring_ref)


def pull(z, refs, bits_ref, flow_ref, solute_ref):
    pops_ref, side_ref, post_ref, aux_ref = refs
    at = pl.ds(pl.multiple_of(z * PLANE, PLANE), PLANE)
    main = pl.ds(pl.multiple_of(z * B, B), B)
    bits = bits_ref[at, :]
    pops = stream_flow(z, bits, flow_ref)
    for i in range(19):
        pops_ref[i, main, :] = pops[i][:B]
        if side_ref is not None:
            side_ref[i, main, :] = pops[i][B:]
    if side_ref is None:
        return
    rho, velocity = moments(pops, jnp.where(is_open(bits, 0), 1.0, 0.0))
    for k, v in enumerate([rho] + velocity):
        aux_ref[k, at, :] = v
    post = solute_collide([solute_ref[i, at, :] for i in range(7)], velocity)
    for i in range(7):
        post_ref[i, at, :] = post[i]


def push(z, pops_refs, aux_ref, bits, solute, flow_ref):
    rho, vx, vy, vz = (plane(aux_ref, z, k) for k in range(4))
    collide_flow(
        lambda i: flow_plane(pops_refs, z, i), rho, vx, vy, vz, bits, sum(solute),
        lambda i, v: put_padded(flow_ref, i, z + 1, v),
    )


def put_solute(solute_ref, z, solute):
    for i in range(7):
        solute_ref[i, pl.ds(pl.multiple_of(z * PLANE, PLANE), PLANE), :] = solute[i]


def turn_plane(turn_ref, z, solute):
    for i in range(7):
        for half in range(2):
            at = pl.multiple_of(i * 256 + z * B + half * 8, 8)
            turn_ref[pl.ds(at, 8), :] = turn_blocks(solute[i][half * 8 : half * 8 + 8])


def core_kernel(first, *refs):
    pops_ref, side_ref, post_ref, aux_ref, bits_ref = refs[:5]
    ring_ref, refs = (refs[5], refs[6:]) if first else (None, refs[5:])
    zdn_ref, zup_ref, flow_ref, solute_ref = refs
    write_z_messages(
        (pops_ref, side_ref), post_ref, aux_ref, (zdn_ref, zup_ref), bits_ref, ring_ref
    )
    fills = [jnp.zeros((PLANE, L), F32)] * 2

    def body(z, carry):
        bits = plane(bits_ref, z)
        solute = stream_solute(
            z, post_ref, bits, fills, plane(post_ref, z - 1, 5), plane(post_ref, z + 1, 6)
        )
        put_solute(solute_ref, z, solute)
        push(z, (pops_ref, side_ref), aux_ref, bits, solute, flow_ref)
        return carry

    lax.fori_loop(1, B - 1, body, 0, unroll=UNROLL)


def fix_rows(pops_refs, post_ref, aux_ref, bits_ref, y_refs, flow_ref, solute_ref):
    for side in range(2):
        edge = (0, B - 1)[side]
        which = (3, 4)[side]
        bits = face_rows(bits_ref, edge)
        post = {i: face_rows(post_ref, edge, i) for i in (3, 4)}
        new = chosen(bits, read_field(y_refs[side], NORM), post, which)
        conc = new + sum(face_rows(solute_ref, edge, i) for i in range(7) if i != which)
        put_face(solute_ref, edge, new, which)

        def put(i, v):
            for tile in range(2):
                at = PADDED + tile * 32 + 8 + edge
                flow_ref[i, pl.ds(at, B, stride=PADDED), :] = v[tile * B : (tile + 1) * B]

        rho, vx, vy, vz = (face_rows(aux_ref, edge, k) for k in range(4))
        collide_flow(
            lambda i: flow_rows(pops_refs, edge, i), rho, vx, vy, vz, bits, conc, put
        )


def inner_kernel(*refs):
    bits_ref, open_ref, ylo_ref, yhi_ref = refs[6:10]
    *state, flow_ref, solute_ref = refs[10:]
    pops_ref, side_ref, post_ref, aux_ref = state
    y_refs = ylo_ref, yhi_ref
    fix_rows((pops_ref, side_ref), post_ref, aux_ref, bits_ref, y_refs, flow_ref, solute_ref)
    collide_y_halos(post_ref, open_ref, y_refs, None, flow_ref)

    def body(z, carry):
        pull(z, state, bits_ref, flow_ref, solute_ref)
        return carry

    lax.fori_loop(2, B - 2, body, 0, unroll=UNROLL)


def inner_last_kernel(*refs):
    pops_ref, side_ref, post_ref, aux_ref = refs[:4]
    bits_ref, open_ref, ylo_ref, yhi_ref, flow_ref, solute_ref, turn_ref = refs[6:]
    y_refs = ylo_ref, yhi_ref
    fix_rows((pops_ref, side_ref), post_ref, aux_ref, bits_ref, y_refs, flow_ref, solute_ref)

    def turn(z, carry):
        turn_plane(turn_ref, z, [plane(solute_ref, z, i) for i in range(7)])
        return carry

    lax.fori_loop(1, B - 1, turn, 0, unroll=UNROLL)
    collide_y_halos(post_ref, open_ref, y_refs, None, flow_ref)


def edge_solute(z, post_ref, bits_ref, y_refs, z_refs):
    fills = [spread8(read_row(y_refs[side], NORM, z)) for side in range(2)]
    below = read_field(z_refs[0], NORM) if z == 0 else plane(post_ref, z - 1, 5)
    above = read_field(z_refs[1], NORM) if z == B - 1 else plane(post_ref, z + 1, 6)
    return stream_solute(z, post_ref, plane(bits_ref, z), fills, below, above)


def edge_kernel(*refs):
    bits_ref, open_ref, ylo_ref, yhi_ref, zlo_ref, zhi_ref = refs[6:12]
    *state, flow_ref, solute_ref, ydn_ref, yup_ref = refs[12:]
    pops_ref, side_ref, post_ref, aux_ref = state
    y_refs, z_refs = (ylo_ref, yhi_ref), (zlo_ref, zhi_ref)
    for z in (0, B - 1):
        solute = edge_solute(z, post_ref, bits_ref, y_refs, z_refs)
        put_solute(solute_ref, z, solute)
        push(z, (pops_ref, side_ref), aux_ref, plane(bits_ref, z), solute, flow_ref)
    collide_y_halos(post_ref, open_ref, y_refs, z_refs, flow_ref)
    collide_z_halos(post_ref, open_ref, y_refs, z_refs, flow_ref)
    for z in (0, 1, B - 2, B - 1):
        pull(z, state, bits_ref, flow_ref, solute_ref)
    write_y_messages(
        (pops_ref, side_ref), post_ref, aux_ref, (ydn_ref, yup_ref), bits_ref=bits_ref
    )


def send_kernel(me_ref, slot_ref, *refs):
    post_ref, bits_ref, ylo_ref, yhi_ref, zlo_ref, zhi_ref = refs[2:8]
    solute_ref, turn_ref, *outs = refs[8:]
    for z in (0, B - 1):
        solute = edge_solute(z, post_ref, bits_ref, (ylo_ref, yhi_ref), (zlo_ref, zhi_ref))
        put_solute(solute_ref, z, solute)
        turn_plane(turn_ref, z, solute)
    fill_messages(me_ref[0], [slot_ref[0, 0, j] for j in range(8)], turn_ref, outs)


def last_kernel(*refs):
    pops_ref, side_ref, post_ref, aux_ref, flow_in, solute_ref, bits_ref, open_ref = refs[:8]
    y_refs, z_refs = refs[8:10], refs[10:12]
    out_ref, flow_ref = refs[12:]
    for z in (0, B - 1):
        solute = [plane(solute_ref, z, i) for i in range(7)]
        push(z, (pops_ref, side_ref), aux_ref, plane(bits_ref, z), solute, flow_ref)
    collide_y_halos(post_ref, open_ref, y_refs, z_refs, flow_ref)
    collide_z_halos(post_ref, open_ref, y_refs, z_refs, flow_ref)

    def body(z, carry):
        pull(z, (out_ref, None, None, None), bits_ref, flow_ref, None)
        return carry

    lax.fori_loop(0, B, body, 0, unroll=UNROLL)


def scatter_kernel(me_ref, slot_ref, *refs):
    receive(me_ref[0], [slot_ref[s] for s in range(8)], refs[:-1], refs[-1])


def neighbours(low, high, axis):
    count = lax.axis_size(axis)
    up = [(i, (i + 1) % count) for i in range(count)]
    down = [(i, (i - 1) % count) for i in range(count)]
    return lax.ppermute(high, axis, up), lax.ppermute(low, axis, down)


def exchange_blocks(own, up1, down1, up2, down2, up3, down3):
    def shifted(x, step):
        return lax.ppermute(x, "gz", [(i, (i + step) % 8) for i in range(8)])

    up1, down1 = shifted(up1, 1), shifted(down1, -1)
    up2, down2 = shifted(up2, 2), shifted(down2, -2)
    up3 = shifted(jnp.concatenate([up3, up1[ROW:]], axis=0), 3)
    down3 = shifted(jnp.concatenate([down3, down1[ROW:]], axis=0), -3)
    return own, up1, down1, up2, down2, up3, down3


def inside():
    flags = []
    for axis in ("gx", "gy", "gz"):
        at = lax.axis_index(axis)
        flags += [at > 0, at < lax.axis_size(axis) - 1]
    return jnp.stack(flags).astype(F32)


def with_edges(face, halos, row):
    slabs = face.shape[0] // B
    rows = [face] + [halo.reshape(slabs, B, L)[:, row] for halo in halos]
    pad = -slabs * (B + 2) % 8
    return jnp.concatenate(rows + [jnp.zeros((pad, L), F32)], axis=0)


def exchange_z(halos, zdn, zup):
    return neighbours(with_edges(zdn, halos, 0), with_edges(zup, halos, B - 1), "gz")


def shards(populations, solute_state, pore_mask, block_slot, slot_block):
    flags = inside()
    me = lax.axis_index("gz").astype(jnp.int32).reshape(1)
    turn = pltpu.VMEM((BLOCKROWS, L), F32)
    sent = tuple(held(n, L) for n in (ROW, ROW + HALF, ROW + HALF, ROW, ROW, ROW, ROW))
    state = solute_state.reshape(7, 8, 32, L).transpose(0, 2, 1, 3).reshape(BLOCKROWS, L)
    send = call(
        gather_kernel, sent, [SMEM, SMEM, HBM], [turn, pltpu.SemaphoreType.DMA((7,))], 1, 2 * 10**6
    )(me, slot_block, state)
    recv = exchange_blocks(*send)

    pops = populations.reshape(19, 256, L)
    mask = pore_mask.reshape(256, L)
    low, high = call(
        columns_kernel,
        (held(320, L),) * 2,
        [HBM] * 2,
        [
            pltpu.VMEM((19, 256, L), F32),
            pltpu.VMEM((256, L), jnp.int32),
            pltpu.SemaphoreType.DMA((20,)),
        ],
        10**6,
        13 * 10**6,
    )(pops, mask)
    left, right = neighbours(low, high, "gx")
    dims = ((19, 256, L), (19, 256, L), (ROWS, L), (4, ROWS, L), (PADROWS, L))
    pops, side, ring_mask, aux, mask, bits = call(
        ring_kernel,
        tuple(held(*d) for d in dims) + (held(ROWS, L, dtype=jnp.int32),),
        [SMEM, HBM] + [VMEM] * 3,
        [pltpu.SemaphoreType.DMA],
        10**6,
        20 * 10**6,
    )(flags, pops, mask, right, left)

    low, high = call(
        pick_kernel,
        (held(HALF, L),) * 2,
        [SMEM] * 2 + [VMEM] * 8,
        [pltpu.VMEM((ROW, L), F32)],
        1,
        10**6,
        keep=True,
    )(me, block_slot, *recv, bits)
    left, right = neighbours(low, high, "gx")
    dense = call(
        spread_kernel, held(BLOCKROWS, L), [SMEM] * 2 + [VMEM] * 7, [turn], 10**6, 10**7, keep=True
    )(me, block_slot, *recv)
    message = held((SIDES + MASK + 1) * B, L)
    post, ydn, yup = call(
        first_kernel,
        (held(7, ROWS, L),) + (message,) * 2,
        [VMEM] * 7,
        [turn],
        10**7,
        10**7,
        keep=True,
    )(dense, right, left, pops, side, aux, ring_mask)

    states = (held(19, 256, L), held(19, 256, L), held(7, ROWS, L), held(4, ROWS, L))
    works = (held(19, PADROWS, L), held(7, ROWS, L))
    opens_out = (held(PADROWS, L), held(ROWS, L, dtype=jnp.int32), held(PLANE * 8, L))
    message = held((SIDES + MASK) * B, L)
    state = (pops, side, post, aux)
    for step in range(STEPS):
        last = step == STEPS - 1
        y_halos = neighbours(ydn, yup, "gy")
        zdn, zup, *work = call(
            functools.partial(core_kernel, step == 0),
            (held(*ydn.shape),) * 2 + works,
            [VMEM] * (6 if step == 0 else 5),
            [],
            10**7,
            10**7,
            keep=True,
        )(*state, bits, *([ring_mask] if step == 0 else []))
        z_halos = exchange_z(y_halos, zdn, zup)
        if step == 0:
            mask, bits, opens = call(
                side_open_kernel,
                opens_out,
                [SMEM] + [VMEM] * 4,
                [],
                10**6,
                10**6,
                aliases={3: 0, 4: 1},
                keep=True,
            )(flags, *y_halos, mask, bits)
        if last:
            break
        moved = call(
            inner_kernel,
            states + works,
            [VMEM] * 10,
            [],
            10**7,
            10**7,
            aliases={i: i for i in range(6)},
            keep=True,
        )(*state, *work, bits, opens, *y_halos)
        if step == 0:
            mask, bits, opens = call(
                edge_open_kernel,
                opens_out,
                [SMEM] + [VMEM] * 5,
                [],
                10**6,
                10**6,
                aliases={3: 0, 4: 1, 5: 2},
                keep=True,
            )(flags, *z_halos, mask, bits, opens)
        *state, _, _, ydn, yup = call(
            edge_kernel,
            states + works + (message, message),
            [VMEM] * 12,
            [],
            10**7,
            10**7,
            aliases={i: i for i in range(6)},
            keep=True,
        )(*moved, bits, opens, *y_halos, *z_halos)

    flow, solute, turned = call(
        inner_last_kernel,
        works + (held(BLOCKROWS, L),),
        [VMEM] * 10,
        [],
        10**7,
        10**7,
        aliases={4: 0, 5: 1},
        keep=True,
    )(*state, *work, bits, opens, *y_halos)
    solute, _, *send = call(
        send_kernel,
        (works[1], held(BLOCKROWS, L)) + sent,
        [SMEM] * 2 + [VMEM] * 8,
        [],
        10**6,
        10**6,
        aliases={2: 0, 3: 1},
        keep=True,
    )(me, block_slot, solute, turned, state[2], bits, *y_halos, *z_halos)
    recv = exchange_blocks(*send)
    pops, _ = call(
        last_kernel,
        (shape(19, 256, L), works[0]),
        [VMEM] * 12,
        [],
        10**7,
        10**7,
        aliases={4: 1},
        keep=True,
    )(*state, flow, solute, bits, opens, *y_halos, *z_halos)
    out = call(scatter_kernel, shape(BLOCKROWS, L), [SMEM] * 2 + [VMEM] * 7, [], 1, 2 * 10**6)(
        me, slot_block, *recv
    )
    new_solute = out.reshape(7, 32, 8, L).transpose(0, 2, 1, 3).reshape(7, 8, 4096)
    return pops.reshape(19, B, B, L), new_solute


def solution(mesh):
    in_specs = (
        P(None, "gz", "gy", "gx"),
        P(None, ("gx", "gy", "gz"), None),
        P("gz", "gy", "gx"),
        P("gz", "gy", "gx"),
        P(("gx", "gy", "gz")),
    )
    out_specs = (P(None, "gz", "gy", "gx"), P(None, ("gx", "gy", "gz"), None))
    return jax.shard_map(shards, mesh=mesh, in_specs=in_specs, out_specs=out_specs, check_vma=False)
```
